32 devices in a mesh: store: 8 (over z, x), trainer: 4 (over y, core).
Axes of the slice: x: 2, y: 2, z: 4, core: 2. Of those that a mesh axis runs over, the one named last changes fastest.
Arguments:
- features: float32 [1024, 768], P('store'), may hold values from -6 to 6
- self_rows: float32 [4096, 768], P(('store', 'trainer')), may hold values from -6 to 6
- edge_row: int32 [4, 8, 8, 12, 2], P('trainer', 'store'), may hold values from 0 to 128, as said below
- recv_target: int32 [4, 8, 8, 12], P('trainer', 'store'), may hold values from 0 to 128, as said below
- cotangent: bfloat16 [4096, 768], P(('store', 'trainer')), may hold values from -6 to 6
- w_self: bfloat16 [768, 768], replicated, may hold values from -0.21875 to 0.21875
- w_neigh: bfloat16 [768, 768], replicated, may hold values from -0.21875 to 0.21875
Outputs:
- hidden: bfloat16 [4096, 768], P(('store', 'trainer'))
- grad_self: float32 [768, 768], P('store')
- grad_neigh: float32 [768, 768], P('store')
The draws below stay inside these ranges and needn't reach their ends.
Inputs may be any that keep to these rules, and one draw needn't show every extreme that they name: `edge_row`: A slot that no target uses holds no rows, and every used slot holds at least one row. `recv_target`: slots of an owner to one destination may name the same target more than once; a target may have no slot.
All inputs are finite; a program needn't handle non-finite values.
Results may differ from the reference program's by a relative error of at most 0.0059.
Values may be sent and summed in bfloat16 or wider, within the bound.
No kernel may reach another device: no remote copies, remote signals or barrier semaphores. Data moves between devices by JAX's collectives and lax.ppermute only.
A program may use at most 64 MiB of HBM per device.

```python
import jax
import jax.numpy as jnp
from jax import lax

F = 768
H = 768
OWN = 128
TGT_DEV = 128
CAP = 12
MULT = 2
ROWS = 1024
TARGETS = 4096
N_STORE = 8
N_TRAINER = 4


def slot_plan(key):
    slot_shape = (N_TRAINER, N_STORE, N_STORE, CAP)
    owner_rank = jax.random.permutation(jax.random.fold_in(key, 11), N_STORE)
    threshold = 15 + 70 * owner_rank // max(N_STORE - 1, 1)
    dice_roll = jax.random.randint(jax.random.fold_in(key, 12), slot_shape, 0, 100)
    is_live = dice_roll < threshold[None, :, None, None]
    target_ids = jax.random.randint(jax.random.fold_in(key, 13), slot_shape, 0, TGT_DEV)
    edge_count = jax.random.randint(jax.random.fold_in(key, 14), slot_shape, 1, MULT + 1)
    row_ids = jax.random.randint(jax.random.fold_in(key, 15), slot_shape + (MULT,), 0, OWN)
    return (is_live, target_ids, edge_count, row_ids)


def draw_edge_row(key, part):
    is_live, target_ids, edge_count, row_ids = slot_plan(key)
    entry = jnp.arange(MULT, dtype=jnp.int32)
    used = is_live[..., None] & (entry < edge_count[..., None])
    return jnp.where(used, row_ids, OWN).astype(jnp.int32)


def draw_recv_target(key, part):
    is_live, target_ids, edge_count, row_ids = slot_plan(key)
    marked = jnp.where(is_live, target_ids, TGT_DEV).astype(jnp.int32)
    return jnp.transpose(marked, (0, 2, 1, 3))


def spiked(drawn, rng, source, target, parts, factor):
    owner, partner = [(jnp.arange(drawn.shape[dim]) // (drawn.shape[dim] // parts)).reshape([-1 if axis == dim else 1 for axis in range(drawn.ndim)]) for dim in (source, target)]
    chosen = jax.random.permutation(rng, parts)[partner]
    strong = (owner == chosen) | (owner == (partner + parts // 2) % parts)
    return jnp.where(strong, factor * drawn, drawn)


def level_of(stream_key, shape, shards, smallest, high):
    factor_of, own = 1.0, jax.random.fold_in(stream_key, 6)
    for dim, shards_of in shards:
        draws = jnp.exp(jax.random.uniform(jax.random.fold_in(own, dim), (shards_of,), jnp.float32, smallest / len(shards), high / len(shards)))
        factor_of = factor_of * jnp.repeat(draws, shape[dim] // shards_of).reshape([-1 if axis == dim else 1 for axis in range(len(shape))])
    return factor_of


def scatter_about(own_key, extent, scale, reach, cuts=(), kind=jnp.bfloat16):
    array = jax.random.normal(own_key, extent, jnp.float32) * scale
    if len(cuts) > 0:
        array = level_of(own_key, extent, cuts, -0.22, 0.18) * array
    return jnp.clip(array, min=-reach, max=reach).astype(kind)


def heavy_noise(own_key, dims, spread, limit, cuts, heavy, kind=jnp.bfloat16):
    drawn = spread * jax.random.normal(own_key, dims, jnp.float32)
    if cuts:
        drawn = drawn * level_of(own_key, dims, cuts, -0.22, 0.18)
    return jnp.clip(spiked(drawn, jax.random.fold_in(own_key, 3), *heavy), -limit, limit).astype(kind)


def setup_inputs(seed: int = 0) -> dict:
    seeds = jax.random.split(jax.random.key(seed), 8)
    features = scatter_about(seeds[0], (ROWS, F), 1.0, 6.0, ((0, 8),), jnp.float32)
    self_rows = heavy_noise(seeds[1], (TARGETS, F), 1.0, 6.0, ((0, 32),), (0, 1, 32, 2.75), jnp.float32)
    edge_row = draw_edge_row(jax.random.fold_in(seeds[7], 71), 0)
    recv_target = draw_recv_target(jax.random.fold_in(seeds[7], 71), 0)
    cotangent = scatter_about(seeds[4], (TARGETS, H), 1.0, 6.0, ((0, 32),))
    w_self = scatter_about(seeds[5], (F, H), F ** -0.5, 0.21875)
    w_neigh = scatter_about(seeds[6], (F, H), F ** -0.5, 0.21875)
    return dict(features=features, self_rows=self_rows, edge_row=edge_row, recv_target=recv_target, cotangent=cotangent, w_self=w_self, w_neigh=w_neigh)


def owner_sums(store_table, owner_edges):
    picked = store_table[owner_edges]
    partial_value = jnp.sum(picked, axis=2).astype(jnp.bfloat16)
    counts = jnp.sum((owner_edges < OWN).astype(jnp.float32), axis=2)
    return partial_value, counts


def dest_mean(slot_parts, slot_counts, slot_targets):
    flat_targets = slot_targets.reshape(-1)
    matches = flat_targets[None, :] == jnp.arange(TGT_DEV, dtype=jnp.int32)[:, None]
    onehot = matches.astype(jnp.bfloat16)
    summed = jnp.dot(onehot, slot_parts.reshape(-1, F), preferred_element_type=jnp.float32)
    number = jnp.sum(jnp.where(matches, slot_counts.reshape(-1)[None, :], jnp.float32(0.0)), axis=1)
    return (summed / jnp.maximum(number, 1.0)[:, None]).astype(jnp.bfloat16)


def reference(features, self_rows, edge_row, recv_target, cotangent, w_self, w_neigh):
    store_tables = jnp.concatenate(
        [features.reshape(N_STORE, OWN, F), jnp.zeros((N_STORE, 1, F), jnp.float32)], axis=1)

    def per_trainer(pair):
        trainer_edges, trainer_targets = pair
        partials, counts = lax.map(lambda inner: owner_sums(inner[0], inner[1]), (store_tables, trainer_edges))
        return lax.map(lambda inner: dest_mean(inner[0], inner[1], inner[2]),
                       (jnp.transpose(partials, (1, 0, 2, 3)), jnp.transpose(counts, (1, 0, 2)), trainer_targets))

    means = lax.map(per_trainer, (edge_row, recv_target))
    neighbor_mean = jnp.transpose(means, (1, 0, 2, 3)).reshape(TARGETS, F)
    own_rows = self_rows.astype(jnp.bfloat16)
    preact = jnp.dot(own_rows, w_self, preferred_element_type=jnp.float32) + jnp.dot(
        neighbor_mean, w_neigh, preferred_element_type=jnp.float32)
    sigmoid_val = jax.nn.sigmoid(preact)
    hidden = (preact * sigmoid_val).astype(jnp.bfloat16)
    grad_out = (cotangent.astype(jnp.float32) * (sigmoid_val * (1.0 + preact * (1.0 - sigmoid_val)))).astype(jnp.bfloat16)
    grad_self = jnp.dot(own_rows.T, grad_out, preferred_element_type=jnp.float32)
    grad_neigh = jnp.dot(neighbor_mean.T, grad_out, preferred_element_type=jnp.float32)
    return hidden, grad_self, grad_neigh
```

```python
import functools

import jax
import jax.numpy as jnp
from jax import lax
from jax.experimental import pallas as pl
from jax.experimental.pallas import tpu as pltpu
from jax.sharding import PartitionSpec as P

BF16, F32 = jnp.bfloat16, jnp.float32
SLOT_PAD = 16
VMEM = pl.BlockSpec(memory_space=pltpu.VMEM)
ANY = pl.BlockSpec(memory_space=pl.ANY)
HBM = pl.BlockSpec(memory_space=pltpu.HBM)
PARAMS = pltpu.CompilerParams(vmem_limit_bytes=16 * 1024 * 1024)


def dot(a, b):
    return jnp.dot(a, b, preferred_element_type=F32)


def call(body, outs, args, unread=(), hbm=(), scratch=(), flops=0):
    moved = sum(a.size * a.dtype.itemsize for a in tuple(args) + tuple(outs))
    return pl.pallas_call(
        body,
        out_shape=list(outs),
        in_specs=[VMEM] * len(args) + [ANY] * len(unread) + [HBM] * len(hbm),
        out_specs=[VMEM] * len(outs),
        scratch_shapes=list(scratch),
        compiler_params=PARAMS,
        cost_estimate=pl.CostEstimate(flops=flops, bytes_accessed=moved, transcendentals=0),
    )(*args, *unread, *hbm)


def shape(dims, kind):
    return jax.ShapeDtypeStruct(dims, kind)


def slot_sums(cap, ids, feat_copy, feat_ref, out_ref):
    owned, slots = feat_ref.shape[0], ids.shape[1]
    row = lax.broadcasted_iota(jnp.int32, (owned, slots), 0)
    weight = jnp.zeros((owned, slots), F32)
    count = jnp.zeros((1, slots), F32)
    for m in range(ids.shape[0]):
        weight += (row == ids[m:m + 1, :]).astype(F32)
        count += (ids[m:m + 1, :] < owned).astype(F32)
    pick = weight.T.astype(BF16)
    r = lax.broadcasted_iota(jnp.int32, (slots, slots), 0)
    c = lax.broadcasted_iota(jnp.int32, (slots, slots), 1)
    here = ((r & (SLOT_PAD - 1)) == cap) & ((c - (c & (SLOT_PAD - 1))) == (r - (r & (SLOT_PAD - 1))))
    spread = jnp.where(here, jnp.broadcast_to(count, (slots, slots)), 0.0).astype(BF16)
    c2 = lax.broadcasted_iota(jnp.int32, (slots, 128), 0)
    l2 = lax.broadcasted_iota(jnp.int32, (slots, 128), 1)
    fold = ((c2 & (SLOT_PAD - 1)) == l2).astype(BF16)
    counts = dot(spread, fold)
    feat_copy.wait()
    feat = feat_ref[...]
    high = feat.astype(BF16)
    low = (feat - high.astype(F32)).astype(BF16)
    sums = dot(pick, high) + dot(pick, low)
    out_ref[:, :128] = (sums[:, :128] + counts).astype(BF16)
    out_ref[:, 128:] = sums[:, 128:].astype(BF16)


def slot_sums_kernel(cap, feat_hbm, edge_hbm, out_ref, feat_ref, edge_ref, sems):
    copies = [pltpu.make_async_copy(edge_hbm, edge_ref, sems.at[0]),
              pltpu.make_async_copy(feat_hbm, feat_ref, sems.at[1])]
    for copy in copies:
        copy.start()
    owned = feat_ref.shape[0]
    ns, mult, _ = edge_ref.shape
    fill = jnp.full((mult, SLOT_PAD - cap), owned, jnp.int32)
    copies[0].wait()
    ids = jnp.concatenate([p for d in range(ns) for p in (edge_ref[d], fill)], axis=1)
    slot_sums(cap, ids, copies[1], feat_ref, out_ref)


def neighbor_mean(cap, rows, recv, targets):
    slots = rows.shape[0]
    target = lax.broadcasted_iota(jnp.int32, (targets, slots), 0)
    onehot = (target == recv).astype(BF16)
    r = lax.broadcasted_iota(jnp.int32, (slots, slots), 0)
    c = lax.broadcasted_iota(jnp.int32, (slots, slots), 1)
    from_count = (c == (r - (r & (SLOT_PAD - 1)) + cap)).astype(BF16)
    copied = dot(from_count, rows[:, :128])
    r2 = lax.broadcasted_iota(jnp.int32, (slots, 128), 0)
    l2 = lax.broadcasted_iota(jnp.int32, (slots, 128), 1)
    counts = jnp.where((r2 & (SLOT_PAD - 1)) == l2, copied, 0.0).astype(BF16)
    number = jnp.sum(dot(onehot, counts), axis=1, keepdims=True)
    return (dot(onehot, rows) / jnp.maximum(number, 1.0)).astype(BF16)


def forward(preact, cot):
    sig = jax.nn.sigmoid(preact)
    hidden = (preact * sig).astype(BF16)
    grad = (cot.astype(F32) * (sig * (1.0 + preact * (1.0 - sig)))).astype(BF16)
    return hidden, grad


class Plan:
    def __init__(self, mesh, width, out_width):
        self.ns, self.nt = mesh.shape["store"], mesh.shape["trainer"]
        self.gx = 2 if self.ns % 2 == 0 else 1
        self.nz = self.ns // self.gx
        self.gc = 2
        self.gy = max(self.nt // self.gc, 1)
        self.shard = width // self.ns
        self.rows = self.nz * self.shard
        self.cols = out_width // self.gy
        self.peers = [(dx, dy) for dx in range(self.gx) for dy in range(self.gy)]

    def fits(self):
        pow2 = all((n & (n - 1)) == 0 for n in (self.ns, self.nt))
        return (pow2 and self.ns <= 8 and self.gy * self.gc == self.nt and self.cols % 128 == 0
                and self.shard % 16 == 0 and len(self.peers) <= 4 and self.nz <= 4)

    def place(self):
        s, t = lax.axis_index("store"), lax.axis_index("trainer")
        return s // self.gx, s % self.gx, t // self.gc, t % self.gc

    def send(self, array, to):
        pairs = []
        for s in range(self.ns):
            for t in range(self.nt):
                z, x, y, c = to(s // self.gx, s % self.gx, t // self.gc, t % self.gc)
                pairs.append((s * self.nt + t, (z * self.gx + x) * self.nt + y * self.gc + c))
        return lax.ppermute(array, ("store", "trainer"), pairs)


def write_rows(plan, trans_ref, outs):
    x = plan.place()[1]
    for (dx, dy), out in zip(plan.peers, outs):
        for z in range(plan.nz):
            start = pl.multiple_of((z * plan.gx + (x ^ dx)) * plan.shard, 16)
            out[z * plan.shard:(z + 1) * plan.shard, :] = trans_ref[pl.ds(start, plan.shard), :]


def own_kernel(plan, self_ref, _, own_ref, *rest):
    outs, trans_ref = rest[:-1], rest[-1]
    own_ref[...] = self_ref[...].astype(BF16)
    trans_ref[...] = self_ref[...].T.astype(BF16)
    write_rows(plan, trans_ref, outs)


def mean_kernel(plan, cap, rows_ref, recv_ref, mean_ref, *rest):
    outs, trans_ref = rest[:-1], rest[-1]
    mean = neighbor_mean(cap, rows_ref[...], recv_ref[...], mean_ref.shape[0])
    mean_ref[...] = mean
    trans_ref[...] = mean.astype(F32).T.astype(BF16)
    write_rows(plan, trans_ref, outs)


def layer_kernel(plan, ordered, mean_ref, self_ref, cot_ref, w_ref, *rest):
    hidden_ref, *outs = rest[ordered:-1]
    grad_ref = rest[-1]
    targets = self_ref.shape[0]
    preact = self_ref[...] + dot(mean_ref[...], w_ref[...])
    hidden, grad = forward(preact, cot_ref[...])
    hidden_ref[...] = hidden
    for b in range(grad_ref.shape[0]):
        grad_ref[b] = grad[:, b * 128:(b + 1) * 128]
    y = plan.place()[2]
    each = plan.cols // 128
    for (dx, dy), out in zip(plan.peers, outs):
        for b in range(each):
            out[b * targets:(b + 1) * targets, :] = grad_ref[(y ^ dy) * each + b]


def terms_kernel(plan, *refs):
    n = len(plan.peers)
    own, mean, grad = refs[:n], refs[n:2 * n], refs[2 * n:3 * n]
    keep_ref, send_ref, total_ref = refs[3 * n:]
    rows, each, targets = plan.rows, plan.cols // 128, own[0].shape[1]
    left = jnp.concatenate(
        [jnp.concatenate([o[...], m[...]], axis=0) for o, m in zip(own, mean)], axis=1)
    right = jnp.concatenate(
        [jnp.concatenate([g[b * targets:(b + 1) * targets, :] for b in range(each)], axis=1)
         for g in grad], axis=0)
    total_ref[...] = dot(left, right)
    c = plan.place()[3]
    keep_ref[...] = total_ref[pl.ds(pl.multiple_of(c * rows, 16), rows), :]
    send_ref[...] = total_ref[pl.ds(pl.multiple_of((1 - c) * rows, 16), rows), :].astype(BF16)


def core_sum_kernel(plan, keep_ref, got_ref, *rest):
    outs, total_ref = rest[:-1], rest[-1]
    total_ref[...] = keep_ref[...] + got_ref[...].astype(F32)
    z = plan.place()[0]
    for k, out in enumerate(outs):
        start = pl.multiple_of((z ^ k) * plan.shard, 16)
        out[...] = total_ref[pl.ds(start, plan.shard), :].astype(out.dtype)


def store_sum_kernel(*refs):
    total = refs[0][...]
    for r in refs[1:-1]:
        total += r[...].astype(F32)
    refs[-1][...] = total.astype(BF16)


def assemble_kernel(plan, *refs):
    parts, (self_ref, neigh_ref, both_ref) = refs[:-3], refs[-3:]
    _, _, y, c = plan.place()
    for i, part in enumerate(parts):
        cols = pl.ds(pl.multiple_of((y ^ (i // plan.gc)) * plan.cols, 128), plan.cols)
        both_ref[c ^ (i % plan.gc), :, cols] = part[...].astype(F32)
    self_ref[...] = both_ref[0]
    neigh_ref[...] = both_ref[1]


def per_device(plan, features, self_rows, edge_row, recv_target, cotangent, w_self, w_neigh):
    owned, width = features.shape
    out_width = w_self.shape[1]
    targets = self_rows.shape[0]
    ns, cap, mult = edge_row.shape[2:]
    slots = ns * SLOT_PAD
    edges = edge_row[0, 0].transpose(0, 2, 1)
    pad = ((0, 0), (0, SLOT_PAD - cap))
    recv = jnp.pad(recv_target[0, 0], pad, constant_values=targets).reshape(1, slots)

    (sums,) = call(
        functools.partial(slot_sums_kernel, cap), [shape((slots, width), BF16)], (),
        hbm=[features, edges], flops=4 * slots * owned * width,
        scratch=[pltpu.VMEM(features.shape, F32), pltpu.VMEM(edges.shape, jnp.int32),
                 pltpu.SemaphoreType.DMA((2,))])
    arrived = lax.all_to_all(sums.reshape(ns, SLOT_PAD, width), "store",
                             split_axis=0, concat_axis=0, tiled=True).reshape(slots, width)
    if not plan.fits():
        own = self_rows.astype(BF16)
        mean = neighbor_mean(cap, arrived, recv, targets)
        preact = dot(own, w_self) + dot(mean, w_neigh)
        hidden, grad = forward(preact, cotangent)
        both = jnp.concatenate([own.T.reshape(ns, -1, targets), mean.T.reshape(ns, -1, targets)], axis=1)
        terms = dot(both.reshape(2 * width, targets), grad)
        part = lax.psum_scatter(terms, "store", scatter_dimension=0, tiled=True)
        total = lax.psum(part, "trainer")
        return hidden, total[:plan.shard], total[plan.shard:]

    n, rows, cols = len(plan.peers), plan.rows, plan.cols
    own, *own_rows = call(
        functools.partial(own_kernel, plan),
        [shape((targets, width), BF16)] + [shape((rows, targets), BF16)] * n, [self_rows], unread=[sums],
        scratch=[pltpu.VMEM((width, targets), BF16)])
    self_term = dot(own, w_self)

    def exchange(arrays):
        return [arrays[0]] + [
            plan.send(a, lambda z, x, y, c, dx=dx, dy=dy: (z, x ^ dx, y ^ dy, c))
            for (dx, dy), a in zip(plan.peers[1:], arrays[1:])]

    own_all = exchange(own_rows)
    mean, *mean_rows = call(
        functools.partial(mean_kernel, plan, cap),
        [shape((targets, width), BF16)] + [shape((rows, targets), BF16)] * n, [arrived, recv],
        scratch=[pltpu.VMEM((width, targets), BF16)], flops=2 * targets * width * slots)
    mean_all = exchange(mean_rows)
    hidden, *grads = call(
        functools.partial(layer_kernel, plan, n - 1),
        [shape((targets, out_width), BF16)] + [shape((cols // 128 * targets, 128), BF16)] * n,
        [mean, self_term, cotangent, w_neigh], unread=own_all[1:],
        scratch=[pltpu.VMEM((out_width // 128, targets, 128), BF16)],
        flops=2 * targets * width * out_width)
    keep, give = call(
        functools.partial(terms_kernel, plan),
        [shape((rows, cols), F32), shape((rows, cols), BF16)],
        own_all + mean_all + exchange(grads), scratch=[pltpu.VMEM((2 * rows, cols), F32)],
        flops=4 * rows * cols * targets * n)
    got = plan.send(give, lambda z, x, y, c: (z, x, y, 1 - c))
    block = (plan.shard, cols)
    mine, *others = call(
        functools.partial(core_sum_kernel, plan),
        [shape(block, F32)] + [shape(block, BF16)] * (plan.nz - 1), [keep, got],
        scratch=[pltpu.VMEM((rows, cols), F32)])
    got = [plan.send(others[k - 1], lambda z, x, y, c, k=k: (z ^ k, x, y, c))
           for k in sorted(range(1, plan.nz), key=lambda k: (k < 2, k))]
    (quarter,) = call(store_sum_kernel, [shape(block, BF16)], [mine] + got)
    column = [quarter] + [plan.send(quarter, lambda z, x, y, c, i=i: (z, x, y ^ i, c))
                          for i in range(1, plan.gy)]
    quarters = [q for part in column
                for q in (part, plan.send(part, lambda z, x, y, c: (z, x, y, 1 - c)))]
    grads = call(functools.partial(assemble_kernel, plan),
                 [shape((plan.shard, out_width), F32)] * 2, quarters,
                 scratch=[pltpu.VMEM((2, plan.shard, out_width), F32)])
    return hidden, grads[0], grads[1]


def solution(mesh):
    in_specs = (
        P("store", None),
        P(("store", "trainer"), None),
        P("trainer", "store", None, None, None),
        P("trainer", "store", None, None),
        P(("store", "trainer"), None),
        P(),
        P(),
    )
    out_specs = (P(("store", "trainer"), None), P("store", None), P("store", None))

    def run(features, self_rows, edge_row, recv_target, cotangent, w_self, w_neigh):
        plan = Plan(mesh, features.shape[1], w_self.shape[1])
        return jax.shard_map(
            functools.partial(per_device, plan), mesh=mesh, in_specs=in_specs,
            out_specs=out_specs, check_vma=False,
        )(features, self_rows, edge_row, recv_target, cotangent, w_self, w_neigh)

    return run
```

```python
import functools

import jax
import jax.numpy as jnp
from jax import lax
from jax.experimental import pallas as pl
from jax.experimental.pallas import tpu as pltpu
from jax.sharding import PartitionSpec as P

BF16, F32 = jnp.bfloat16, jnp.float32
SLOT_PAD = 16
VMEM = pl.BlockSpec(memory_space=pltpu.VMEM)
ANY = pl.BlockSpec(memory_space=pl.ANY)


def dot(a, b):
    return jnp.dot(a, b, preferred_element_type=F32)


def call(body, outs, args, unread=(), scratch=(), flops=0):
    moved = sum(a.size * a.dtype.itemsize for a in (*args, *outs))
    return pl.pallas_call(
        body,
        out_shape=list(outs),
        in_specs=[VMEM] * len(args) + [ANY] * len(unread),
        out_specs=[VMEM] * len(outs),
        scratch_shapes=list(scratch),
        compiler_params=pltpu.CompilerParams(vmem_limit_bytes=16 * 1024 * 1024),
        cost_estimate=pl.CostEstimate(flops=flops, bytes_accessed=moved, transcendentals=0),
    )(*args, *unread)


def shape(dims, kind):
    return jax.ShapeDtypeStruct(dims, kind)


def slot_sums_kernel(order, feat_ref, edge_ref, _, out_ref):
    owned = feat_ref.shape[0]
    _, mult, cap = edge_ref.shape
    slots = len(order) * SLOT_PAD
    fill = jnp.full((mult, SLOT_PAD - cap), owned, jnp.int32)
    ids = jnp.concatenate([p for d in order for p in (edge_ref[d], fill)], axis=1)
    row = lax.broadcasted_iota(jnp.int32, (owned, slots), 0)
    weight = jnp.zeros((owned, slots), F32)
    count = jnp.zeros((1, slots), F32)
    for m in range(ids.shape[0]):
        weight += (row == ids[m:m + 1, :]).astype(F32)
        count += (ids[m:m + 1, :] < owned).astype(F32)
    pick = weight.T.astype(BF16)
    r = lax.broadcasted_iota(jnp.int32, (slots, slots), 0)
    c = lax.broadcasted_iota(jnp.int32, (slots, slots), 1)
    here = ((r & (SLOT_PAD - 1)) == cap) & ((c - (c & (SLOT_PAD - 1))) == (r - (r & (SLOT_PAD - 1))))
    spread = jnp.where(here, jnp.broadcast_to(count, (slots, slots)), 0.0).astype(BF16)
    c2 = lax.broadcasted_iota(jnp.int32, (slots, 128), 0)
    l2 = lax.broadcasted_iota(jnp.int32, (slots, 128), 1)
    fold = ((c2 & (SLOT_PAD - 1)) == l2).astype(BF16)
    counts = dot(spread, fold)
    feat = feat_ref[...]
    high = feat.astype(BF16)
    low = (feat - high.astype(F32)).astype(BF16)
    sums = dot(pick, high) + dot(pick, low)
    out_ref[:, :128] = (sums[:, :128] + counts).astype(BF16)
    out_ref[:, 128:] = sums[:, 128:].astype(BF16)


def neighbor_mean(cap, rows, recv, targets):
    slots = rows.shape[0]
    target = lax.broadcasted_iota(jnp.int32, (targets, slots), 0)
    onehot = (target == recv).astype(BF16)
    r = lax.broadcasted_iota(jnp.int32, (slots, slots), 0)
    c = lax.broadcasted_iota(jnp.int32, (slots, slots), 1)
    from_count = (c == (r - (r & (SLOT_PAD - 1)) + cap)).astype(BF16)
    copied = dot(from_count, rows[:, :128])
    r2 = lax.broadcasted_iota(jnp.int32, (slots, 128), 0)
    l2 = lax.broadcasted_iota(jnp.int32, (slots, 128), 1)
    counts = jnp.where((r2 & (SLOT_PAD - 1)) == l2, copied, 0.0).astype(BF16)
    number = jnp.sum(dot(onehot, counts), axis=1, keepdims=True)
    return (dot(onehot, rows) / jnp.maximum(number, 1.0)).astype(BF16)


def forward(preact, cot):
    sig = jax.nn.sigmoid(preact)
    hidden = (preact * sig).astype(BF16)
    grad = (cot.astype(F32) * (sig * (1.0 + preact * (1.0 - sig)))).astype(BF16)
    return hidden, grad


class Plan:
    def __init__(self, mesh, width, out_width):
        self.ns, self.nt = mesh.shape["store"], mesh.shape["trainer"]
        self.gx = 2 if self.ns % 2 == 0 else 1
        self.nz = self.ns // self.gx
        self.gc = 2
        self.gy = max(self.nt // self.gc, 1)
        self.shard = width // self.ns
        self.rows = self.nz * self.shard
        self.cols = out_width // self.gy
        self.peers = [(dx, dy) for dx in range(self.gx) for dy in range(self.gy)]

    def fits(self):
        pow2 = all((n & (n - 1)) == 0 for n in (self.ns, self.nt))
        return (pow2 and self.ns <= 8 and self.gx == 2 and self.gy == 2 and self.gy * self.gc == self.nt and self.cols % 128 == 0
                and self.shard % 16 == 0 and len(self.peers) <= 4 and self.nz <= 4)

    def place(self):
        s, t = lax.axis_index("store"), lax.axis_index("trainer")
        return s // self.gx, s % self.gx, t // self.gc, t % self.gc

    def send(self, array, to):
        pairs = []
        for s in range(self.ns):
            for t in range(self.nt):
                z, x, y, c = to(s // self.gx, s % self.gx, t // self.gc, t % self.gc)
                pairs.append((s * self.nt + t, (z * self.gx + x) * self.nt + y * self.gc + c))
        return lax.ppermute(array, ("store", "trainer"), pairs)

    def store_order(self):
        up = [(z, x) for z in reversed(range(self.nz)) for x in reversed(range(self.gx))]
        down = [(z, x) for z in range(self.nz) for x in range(self.gx)]
        turns = [at for pair in zip(up, down) for at in pair]
        return [z * self.gx + x for z, x in turns[:self.ns]]


def write_rows(plan, trans_ref, outs):
    x = plan.place()[1]
    for (dx, dy), out in zip(plan.peers, outs):
        for z in range(plan.nz):
            start = pl.multiple_of((z * plan.gx + (x ^ dx)) * plan.shard, 16)
            out[z * plan.shard:(z + 1) * plan.shard, :] = trans_ref[pl.ds(start, plan.shard), :]


def own_kernel(plan, self_ref, own_ref, here_ref, there_ref, token_ref, trans_ref):
    own_ref[...] = self_ref[...].astype(BF16)
    trans_ref[...] = self_ref[...].T.astype(BF16)
    x = plan.place()[1]
    for dx, out in enumerate((here_ref, there_ref)):
        for z in range(plan.nz):
            start = pl.multiple_of((z * plan.gx + (x ^ dx)) * plan.shard, 16)
            out[z * plan.shard:(z + 1) * plan.shard, :] = trans_ref[pl.ds(start, plan.shard), :]
    token_ref[...] = jnp.zeros_like(token_ref)


def layer_kernel(plan, cap, order, ordered, rows_ref, recv_ref, self_ref, cot_ref, w_ref, *rest):
    hidden_ref, *outs = rest[ordered:-2]
    trans_ref, grad_ref = rest[-2:]
    targets = self_ref.shape[0]
    y = plan.place()[2]
    rows = jnp.concatenate(
        [rows_ref[p * SLOT_PAD:(p + 1) * SLOT_PAD, :] for p in (order.index(s) for s in range(plan.ns))], axis=0)
    mean = neighbor_mean(cap, rows, recv_ref[...], targets)
    preact = self_ref[...] + dot(mean, w_ref[...])
    hidden, grad = forward(preact, cot_ref[...])
    hidden_ref[...] = hidden
    trans_ref[...] = mean.astype(F32).T.astype(BF16)
    write_rows(plan, trans_ref, outs)
    for b in range(grad_ref.shape[0]):
        grad_ref[b] = grad[:, b * 128:(b + 1) * 128]
    each = plan.cols // 128
    for (dx, dy), out in zip(plan.peers, outs):
        for b in range(each):
            at = plan.rows + b * targets
            out[at:at + targets, :] = grad_ref[(y ^ dy) * each + b]


def terms_kernel(plan, *refs):
    n = len(plan.peers)
    own, late, (keep_ref, send_ref, total_ref) = refs[:n], refs[n:2 * n], refs[2 * n:]
    rows, each, targets = plan.rows, plan.cols // 128, own[0].shape[1]
    left = jnp.concatenate(
        [jnp.concatenate([o[...], l[:rows, :]], axis=0) for o, l in zip(own, late)], axis=1)
    right = jnp.concatenate(
        [jnp.concatenate([l[rows + b * targets:rows + (b + 1) * targets, :] for b in range(each)], axis=1)
         for l in late], axis=0)
    total_ref[...] = dot(left, right)
    c = plan.place()[3]
    keep_ref[...] = total_ref[pl.ds(pl.multiple_of(c * rows, 16), rows), :]
    send_ref[...] = total_ref[pl.ds(pl.multiple_of((1 - c) * rows, 16), rows), :].astype(BF16)


def core_sum_kernel(plan, keep_ref, got_ref, *rest):
    outs, total_ref = rest[:-1], rest[-1]
    total_ref[...] = keep_ref[...] + got_ref[...].astype(F32)
    z = plan.place()[0]
    for k, out in enumerate(outs):
        start = pl.multiple_of((z ^ k) * plan.shard, 16)
        out[...] = total_ref[pl.ds(start, plan.shard), :].astype(out.dtype)


def store_sum_kernel(*refs):
    total = refs[0][...]
    for r in refs[1:-1]:
        total += r[...].astype(F32)
    refs[-1][...] = total.astype(BF16)


def assemble_kernel(plan, *refs):
    parts, (self_ref, neigh_ref, both_ref) = refs[:-3], refs[-3:]
    _, _, y, c = plan.place()
    for i, part in enumerate(parts):
        cols = pl.ds(pl.multiple_of((y ^ (i // plan.gc)) * plan.cols, 128), plan.cols)
        both_ref[c ^ (i % plan.gc), :, cols] = part[...].astype(F32)
    self_ref[...] = both_ref[0]
    neigh_ref[...] = both_ref[1]


def per_device(plan, features, self_rows, edge_row, recv_target, cotangent, w_self, w_neigh):
    owned, width = features.shape
    out_width = w_self.shape[1]
    targets = self_rows.shape[0]
    ns, cap, mult = edge_row.shape[2:]
    slots = ns * SLOT_PAD
    edges = edge_row[0, 0].transpose(0, 2, 1)
    pad = ((0, 0), (0, SLOT_PAD - cap))
    recv = jnp.pad(recv_target[0, 0], pad, constant_values=targets).reshape(1, slots)

    fits = plan.fits()
    order = plan.store_order() if fits else list(range(ns))
    rows, cols, n = plan.rows, plan.cols, len(plan.peers)
    token = jnp.zeros((8, 128), F32)
    if fits:
        own, own_here, own_there, token = call(
            functools.partial(own_kernel, plan),
            [shape((targets, width), BF16)] + [shape((rows, targets), BF16)] * 2 + [shape((8, 128), F32)],
            [self_rows], scratch=[pltpu.VMEM((width, targets), BF16)])
        own_x = plan.send(own_there, lambda z, x, y, c: (z, 1 - x, y, c))
        own_y = plan.send(own_here, lambda z, x, y, c: (z, x, 1 - y, c))
    (sums,) = call(
        functools.partial(slot_sums_kernel, order), [shape((slots, width), BF16)],
        [features, edges], unread=[token], flops=4 * slots * owned * width)
    arrived = lax.all_to_all(sums.reshape(ns, SLOT_PAD, width), "store", split_axis=0, concat_axis=0,
                             tiled=True, axis_index_groups=[order]).reshape(slots, width)
    if not fits:
        own = self_rows.astype(BF16)
        mean = neighbor_mean(cap, arrived, recv, targets)
        preact = dot(own, w_self) + dot(mean, w_neigh)
        hidden, grad = forward(preact, cotangent)
        both = jnp.concatenate([own.T.reshape(ns, -1, targets), mean.T.reshape(ns, -1, targets)], axis=1)
        terms = dot(both.reshape(2 * width, targets), grad)
        part = lax.psum_scatter(terms, "store", scatter_dimension=0, tiled=True)
        total = lax.psum(part, "trainer")
        return hidden, total[:plan.shard], total[plan.shard:]

    own_xy = plan.send(own_x, lambda z, x, y, c: (z, x, 1 - y, c))
    own_all = [own_here, own_y, own_x, own_xy]
    self_term = dot(own, w_self)

    def exchange(arrays):
        out = {}
        for i in reversed(range(1, n)):
            dx, dy = plan.peers[i]
            out[i] = plan.send(arrays[i], lambda z, x, y, c, dx=dx, dy=dy: (z, x ^ dx, y ^ dy, c))
        return [arrays[0]] + [out[i] for i in range(1, n)]

    late_rows = rows + cols // 128 * targets
    hidden, *late = call(
        functools.partial(layer_kernel, plan, cap, order, n - 1),
        [shape((targets, out_width), BF16)] + [shape((late_rows, targets), BF16)] * n,
        [arrived, recv, self_term, cotangent, w_neigh], unread=own_all[1:],
        scratch=[pltpu.VMEM((width, targets), BF16), pltpu.VMEM((out_width // 128, targets, 128), BF16)],
        flops=2 * targets * width * (out_width + slots))
    keep, give = call(
        functools.partial(terms_kernel, plan),
        [shape((rows, cols), F32), shape((rows, cols), BF16)],
        own_all + exchange(late), scratch=[pltpu.VMEM((2 * rows, cols), F32)],
        flops=4 * rows * cols * targets * n)
    got = plan.send(give, lambda z, x, y, c: (z, x, y, 1 - c))
    block = (plan.shard, cols)
    mine, *others = call(
        functools.partial(core_sum_kernel, plan),
        [shape(block, F32)] + [shape(block, BF16)] * (plan.nz - 1), [keep, got],
        scratch=[pltpu.VMEM((rows, cols), F32)])
    far_first = sorted(range(1, plan.nz), key=lambda k: (k < 2, k))
    got = [plan.send(others[k - 1], lambda z, x, y, c, k=k: (z ^ k, x, y, c)) for k in far_first]
    (quarter,) = call(store_sum_kernel, [shape(block, BF16)], [mine] + got)
    column = [quarter] + [plan.send(quarter, lambda z, x, y, c, i=i: (z, x, y ^ i, c))
                          for i in range(1, plan.gy)]
    quarters = [q for part in column
                for q in (part, plan.send(part, lambda z, x, y, c: (z, x, y, 1 - c)))]
    grads = call(functools.partial(assemble_kernel, plan),
                 [shape((plan.shard, out_width), F32)] * 2, quarters,
                 scratch=[pltpu.VMEM((2, plan.shard, out_width), F32)])
    return hidden, grads[0], grads[1]


def solution(mesh):
    in_specs = (
        P("store", None),
        P(("store", "trainer"), None),
        P("trainer", "store", None, None, None),
        P("trainer", "store", None, None),
        P(("store", "trainer"), None),
        P(),
        P(),
    )
    out_specs = (P(("store", "trainer"), None), P("store", None), P("store", None))

    def run(features, self_rows, edge_row, recv_target, cotangent, w_self, w_neigh):
        plan = Plan(mesh, features.shape[1], w_self.shape[1])
        return jax.shard_map(
            functools.partial(per_device, plan), mesh=mesh, in_specs=in_specs,
            out_specs=out_specs, check_vma=False,
        )(features, self_rows, edge_row, recv_target, cotangent, w_self, w_neigh)

    return run
```

```python
import functools

import jax
import jax.numpy as jnp
from jax import lax
from jax.experimental import pallas as pl
from jax.experimental.pallas import tpu as pltpu
from jax.sharding import PartitionSpec as P

BF16, F32 = jnp.bfloat16, jnp.float32
SLOT_PAD = 16
VMEM = pl.BlockSpec(memory_space=pltpu.VMEM)
ANY = pl.BlockSpec(memory_space=pl.ANY)
HBM = pl.BlockSpec(memory_space=pltpu.HBM)


def dot(a, b):
    return jnp.dot(a, b, preferred_element_type=F32)


def call(body, outs, args, unread=(), hbm=(), scratch=(), flops=0, vmem=16):
    moved = sum(a.size * a.dtype.itemsize for a in (*args, *outs))
    return pl.pallas_call(
        body,
        out_shape=list(outs),
        in_specs=[VMEM] * len(args) + [ANY] * len(unread) + [HBM] * len(hbm),
        out_specs=[VMEM] * len(outs),
        scratch_shapes=list(scratch),
        compiler_params=pltpu.CompilerParams(vmem_limit_bytes=vmem * 1024 * 1024),
        cost_estimate=pl.CostEstimate(flops=flops, bytes_accessed=moved, transcendentals=0),
    )(*args, *unread, *hbm)


def shape(dims, kind):
    return jax.ShapeDtypeStruct(dims, kind)


def slot_sums_kernel(plan, order, feat_hbm, edge_hbm, *rest):
    with_own = len(rest) > 4
    if with_own:
        self_hbm, out_ref, *own_refs, feat_ref, edge_ref, sems, self_ref, trans_ref = rest
    else:
        out_ref, feat_ref, edge_ref, sems = rest
    copies = [pltpu.make_async_copy(edge_hbm, edge_ref, sems.at[0]),
              pltpu.make_async_copy(feat_hbm, feat_ref, sems.at[1])]
    if with_own:
        copies.append(pltpu.make_async_copy(self_hbm, self_ref, sems.at[2]))
    for copy in copies:
        copy.start()
    owned = feat_ref.shape[0]
    _, mult, cap = edge_ref.shape
    slots = len(order) * SLOT_PAD
    copies[0].wait()
    fill = jnp.full((mult, SLOT_PAD - cap), owned, jnp.int32)
    ids = jnp.concatenate([p for d in order for p in (edge_ref[d], fill)], axis=1)
    row = lax.broadcasted_iota(jnp.int32, (owned, slots), 0)
    weight = jnp.zeros((owned, slots), F32)
    count = jnp.zeros((1, slots), F32)
    for m in range(ids.shape[0]):
        weight += (row == ids[m:m + 1, :]).astype(F32)
        count += (ids[m:m + 1, :] < owned).astype(F32)
    pick = weight.T.astype(BF16)
    r = lax.broadcasted_iota(jnp.int32, (slots, slots), 0)
    c = lax.broadcasted_iota(jnp.int32, (slots, slots), 1)
    here = ((r & (SLOT_PAD - 1)) == cap) & ((c - (c & (SLOT_PAD - 1))) == (r - (r & (SLOT_PAD - 1))))
    spread = jnp.where(here, jnp.broadcast_to(count, (slots, slots)), 0.0).astype(BF16)
    c2 = lax.broadcasted_iota(jnp.int32, (slots, 128), 0)
    l2 = lax.broadcasted_iota(jnp.int32, (slots, 128), 1)
    fold = ((c2 & (SLOT_PAD - 1)) == l2).astype(BF16)
    counts = dot(spread, fold)
    copies[1].wait()
    feat = feat_ref[...]
    high = feat.astype(BF16)
    low = (feat - high.astype(F32)).astype(BF16)
    sums = dot(pick, high) + dot(pick, low)
    out_ref[:, :128] = (sums[:, :128] + counts).astype(BF16)
    out_ref[:, 128:] = sums[:, 128:].astype(BF16)
    if with_own:
        copies[2].wait()
        write_own(plan, self_ref, *own_refs, trans_ref)


def neighbor_mean(cap, rows, recv, targets):
    slots = rows.shape[0]
    target = lax.broadcasted_iota(jnp.int32, (targets, slots), 0)
    onehot = (target == recv).astype(BF16)
    r = lax.broadcasted_iota(jnp.int32, (slots, slots), 0)
    c = lax.broadcasted_iota(jnp.int32, (slots, slots), 1)
    from_count = (c == (r - (r & (SLOT_PAD - 1)) + cap)).astype(BF16)
    copied = dot(from_count, rows[:, :128])
    r2 = lax.broadcasted_iota(jnp.int32, (slots, 128), 0)
    l2 = lax.broadcasted_iota(jnp.int32, (slots, 128), 1)
    counts = jnp.where((r2 & (SLOT_PAD - 1)) == l2, copied, 0.0).astype(BF16)
    number = jnp.sum(dot(onehot, counts), axis=1, keepdims=True)
    return (dot(onehot, rows) / jnp.maximum(number, 1.0)).astype(BF16)


def forward(preact, cot):
    sig = jax.nn.sigmoid(preact)
    hidden = (preact * sig).astype(BF16)
    grad = (cot.astype(F32) * (sig * (1.0 + preact * (1.0 - sig)))).astype(BF16)
    return hidden, grad


class Plan:
    def __init__(self, mesh, width, out_width):
        self.ns, self.nt = mesh.shape["store"], mesh.shape["trainer"]
        self.gx = 2 if self.ns % 2 == 0 else 1
        self.nz = self.ns // self.gx
        self.gc = 2
        self.gy = max(self.nt // self.gc, 1)
        self.shard = width // self.ns
        self.rows = self.nz * self.shard
        self.cols = out_width // self.gy
        self.peers = [(dx, dy) for dx in range(self.gx) for dy in range(self.gy)]

    def fits(self):
        pow2 = all((n & (n - 1)) == 0 for n in (self.ns, self.nt))
        return (pow2 and self.ns <= 8 and self.gx == 2 and self.gy == 2 and self.gy * self.gc == self.nt and self.cols % 128 == 0
                and self.shard % 16 == 0 and len(self.peers) <= 4 and self.nz <= 4)

    def place(self):
        s, t = lax.axis_index("store"), lax.axis_index("trainer")
        return s // self.gx, s % self.gx, t // self.gc, t % self.gc

    def send(self, array, to):
        pairs = []
        for s in range(self.ns):
            for t in range(self.nt):
                z, x, y, c = to(s // self.gx, s % self.gx, t // self.gc, t % self.gc)
                pairs.append((s * self.nt + t, (z * self.gx + x) * self.nt + y * self.gc + c))
        return lax.ppermute(array, ("store", "trainer"), pairs)

    def store_order(self):
        up = [(z, x) for z in reversed(range(self.nz)) for x in reversed(range(self.gx))]
        down = [(z, x) for z in range(self.nz) for x in range(self.gx)]
        turns = [at for pair in zip(up, down) for at in pair]
        return [z * self.gx + x for z, x in turns[:self.ns]]


def write_rows(plan, trans_ref, *outs):
    x = plan.place()[1]
    for dx, out in enumerate(outs):
        for z in range(plan.nz):
            start = pl.multiple_of((z * plan.gx + (x ^ dx)) * plan.shard, 16)
            out[z * plan.shard:(z + 1) * plan.shard, :] = trans_ref[pl.ds(start, plan.shard), :]


def write_own(plan, self_ref, own_ref, here_ref, there_ref, trans_ref):
    own_ref[...] = self_ref[...].astype(BF16)
    trans_ref[...] = self_ref[...].T.astype(BF16)
    write_rows(plan, trans_ref, here_ref, there_ref)


def layer_kernel(plan, cap, order, ordered, arrived_ref, recv_ref, self_ref, cot_ref, w_ref, *rest):
    hidden_ref, mean_here, mean_there, grad_here, grad_there, trans_ref, grad_ref = rest[ordered:]
    targets = self_ref.shape[0]
    rows = jnp.concatenate(
        [arrived_ref[p * SLOT_PAD:(p + 1) * SLOT_PAD, :] for p in (order.index(s) for s in range(plan.ns))], axis=0)
    mean = neighbor_mean(cap, rows, recv_ref[...], targets)
    trans_ref[...] = mean.astype(F32).T.astype(BF16)
    write_rows(plan, trans_ref, mean_here, mean_there)
    preact = self_ref[...] + dot(mean, w_ref[...])
    hidden, grad = forward(preact, cot_ref[...])
    hidden_ref[...] = hidden
    for b in range(grad_ref.shape[0]):
        grad_ref[b] = grad[:, b * 128:(b + 1) * 128]
    y, each = plan.place()[2], plan.cols // 128
    for dy, out in enumerate((grad_here, grad_there)):
        for b in range(each):
            out[b * targets:(b + 1) * targets, :] = grad_ref[(y ^ dy) * each + b]


def terms_kernel(plan, keep, *refs):
    n = len(plan.peers)
    own, mean, grad, out_ref = refs[:n], refs[n:2 * n], refs[2 * n:3 * n], refs[3 * n]
    targets = own[0].shape[1]
    use_own = plan.place()[3] == (0 if keep else 1)
    left = jnp.concatenate([jnp.where(use_own, o[...], m[...]) for o, m in zip(own, mean)], axis=1)
    right = jnp.concatenate(
        [jnp.concatenate([g[b * targets:(b + 1) * targets, :] for b in range(plan.cols // 128)], axis=1)
         for g in grad], axis=0)
    out_ref[...] = dot(left, right).astype(out_ref.dtype)


def core_sum_kernel(plan, keep_ref, got_ref, *rest):
    outs, total_ref = rest[:-1], rest[-1]
    total_ref[...] = keep_ref[...] + got_ref[...].astype(F32)
    z = plan.place()[0]
    for k, out in enumerate(outs):
        start = pl.multiple_of((z ^ k) * plan.shard, 16)
        out[...] = total_ref[pl.ds(start, plan.shard), :].astype(out.dtype)


def store_sum_kernel(*refs):
    total = refs[0][...]
    for r in refs[1:-1]:
        total += r[...].astype(F32)
    refs[-1][...] = total.astype(BF16)


def assemble_kernel(plan, *refs):
    parts, (self_ref, neigh_ref, both_ref) = refs[:-3], refs[-3:]
    _, _, y, c = plan.place()
    for i, part in enumerate(parts):
        cols = pl.ds(pl.multiple_of((y ^ (i // plan.gc)) * plan.cols, 128), plan.cols)
        both_ref[c ^ (i % plan.gc), :, cols] = part[...].astype(F32)
    self_ref[...] = both_ref[0]
    neigh_ref[...] = both_ref[1]


def per_device(plan, features, self_rows, edge_row, recv_target, cotangent, w_self, w_neigh):
    owned, width = features.shape
    out_width = w_self.shape[1]
    targets = self_rows.shape[0]
    ns, cap, mult = edge_row.shape[2:]
    slots = ns * SLOT_PAD
    edges = edge_row[0, 0].transpose(0, 2, 1)
    pad = ((0, 0), (0, SLOT_PAD - cap))
    recv = jnp.pad(recv_target[0, 0], pad, constant_values=targets).reshape(1, slots)

    fits = plan.fits()
    order = plan.store_order() if fits else list(range(ns))
    rows, cols, n = plan.rows, plan.cols, len(plan.peers)
    scratch = [pltpu.VMEM(features.shape, F32), pltpu.VMEM(edges.shape, jnp.int32),
               pltpu.SemaphoreType.DMA((3,))]
    outs, more = [shape((slots, width), BF16)], []
    if fits:
        outs += [shape((targets, width), BF16)] + [shape((rows, targets), BF16)] * 2
        more = [self_rows]
        scratch += [pltpu.VMEM(self_rows.shape, F32), pltpu.VMEM((width, targets), BF16)]
    sums, *owns = call(
        functools.partial(slot_sums_kernel, plan, order), outs, (), hbm=[features, edges] + more,
        flops=4 * slots * owned * width, vmem=60 if fits else 16, scratch=scratch)
    arrived = lax.all_to_all(sums.reshape(ns, SLOT_PAD, width), "store", split_axis=0, concat_axis=0,
                             tiled=True, axis_index_groups=[order]).reshape(slots, width)
    if not fits:
        own = self_rows.astype(BF16)
        mean = neighbor_mean(cap, arrived, recv, targets)
        preact = dot(own, w_self) + dot(mean, w_neigh)
        hidden, grad = forward(preact, cotangent)
        both = jnp.concatenate([own.T.reshape(ns, -1, targets), mean.T.reshape(ns, -1, targets)], axis=1)
        terms = dot(both.reshape(2 * width, targets), grad)
        part = lax.psum_scatter(terms, "store", scatter_dimension=0, tiled=True)
        total = lax.psum(part, "trainer")
        return hidden, total[:plan.shard], total[plan.shard:]

    def to_x(array):
        return plan.send(array, lambda z, x, y, c: (z, 1 - x, y, c))

    def to_y(array):
        return plan.send(array, lambda z, x, y, c: (z, x, 1 - y, c))

    own, own_here, own_there = owns
    own_x = to_x(own_there)
    own_all = [own_here, to_y(own_here), own_x, to_y(own_x)]
    self_term = dot(own, w_self)

    hidden, mean_here, mean_there, grad_here, grad_there = call(
        functools.partial(layer_kernel, plan, cap, order, n - 1),
        [shape((targets, out_width), BF16)] + [shape((rows, targets), BF16)] * 2
        + [shape((cols // 128 * targets, 128), BF16)] * 2,
        [arrived, recv, self_term, cotangent, w_neigh], unread=own_all[1:],
        scratch=[pltpu.VMEM((width, targets), BF16), pltpu.VMEM((out_width // 128, targets, 128), BF16)],
        flops=2 * targets * width * (out_width + slots))
    mean_x, grad_y = to_x(mean_there), to_y(grad_there)
    mean_all = [mean_here, to_y(mean_here), mean_x, to_y(mean_x)]
    grad_all = [grad_here, grad_y, to_x(grad_here), to_x(grad_y)]
    factors = own_all + mean_all + grad_all
    (give,) = call(functools.partial(terms_kernel, plan, False), [shape((rows, cols), BF16)], factors,
                   flops=2 * rows * cols * targets * n)
    (keep,) = call(functools.partial(terms_kernel, plan, True), [shape((rows, cols), F32)], factors,
                   flops=2 * rows * cols * targets * n)
    got = plan.send(give, lambda z, x, y, c: (z, x, y, 1 - c))
    block = (plan.shard, cols)
    mine, *others = call(
        functools.partial(core_sum_kernel, plan),
        [shape(block, F32)] + [shape(block, BF16)] * (plan.nz - 1), [keep, got],
        scratch=[pltpu.VMEM((rows, cols), F32)])
    far_first = sorted(range(1, plan.nz), key=lambda k: (k < 2, k))
    got = [plan.send(others[k - 1], lambda z, x, y, c, k=k: (z ^ k, x, y, c)) for k in far_first]
    (quarter,) = call(store_sum_kernel, [shape(block, BF16)], [mine] + got)
    column = [quarter] + [plan.send(quarter, lambda z, x, y, c, i=i: (z, x, y ^ i, c))
                          for i in range(1, plan.gy)]
    quarters = [q for part in column
                for q in (part, plan.send(part, lambda z, x, y, c: (z, x, y, 1 - c)))]
    grads = call(functools.partial(assemble_kernel, plan),
                 [shape((plan.shard, out_width), F32)] * 2, quarters,
                 scratch=[pltpu.VMEM((2, plan.shard, out_width), F32)])
    return hidden, grads[0], grads[1]


def solution(mesh):
    in_specs = (
        P("store", None),
        P(("store", "trainer"), None),
        P("trainer", "store", None, None, None),
        P("trainer", "store", None, None),
        P(("store", "trainer"), None),
        P(),
        P(),
    )
    out_specs = (P(("store", "trainer"), None), P("store", None), P("store", None))

    def run(features, self_rows, edge_row, recv_target, cotangent, w_self, w_neigh):
        plan = Plan(mesh, features.shape[1], w_self.shape[1])
        return jax.shard_map(
            functools.partial(per_device, plan), mesh=mesh, in_specs=in_specs,
            out_specs=out_specs, check_vma=False,
        )(features, self_rows, edge_row, recv_target, cotangent, w_self, w_neigh)

    return run
```

```python
import functools

import jax
import jax.numpy as jnp
from jax import lax
from jax.experimental import pallas as pl
from jax.experimental.pallas import tpu as pltpu
from jax.sharding import PartitionSpec as P

BF16, F32 = jnp.bfloat16, jnp.float32
SLOT_PAD = 16
VMEM = pl.BlockSpec(memory_space=pltpu.VMEM)
ANY = pl.BlockSpec(memory_space=pl.ANY)
HBM = pl.BlockSpec(memory_space=pltpu.HBM)


def dot(a, b):
    return jnp.dot(a, b, preferred_element_type=F32)


def call(body, outs, args, unread=(), hbm=(), scratch=(), flops=0, vmem=16):
    moved = sum(a.size * a.dtype.itemsize for a in (*args, *outs))
    return pl.pallas_call(
        body,
        out_shape=list(outs),
        in_specs=[VMEM] * len(args) + [ANY] * len(unread) + [HBM] * len(hbm),
        out_specs=[VMEM] * len(outs),
        scratch_shapes=list(scratch),
        compiler_params=pltpu.CompilerParams(vmem_limit_bytes=vmem * 1024 * 1024),
        cost_estimate=pl.CostEstimate(flops=flops, bytes_accessed=moved, transcendentals=0),
    )(*args, *unread, *hbm)


def shape(dims, kind):
    return jax.ShapeDtypeStruct(dims, kind)


def slot_sums_kernel(plan, order, feat_hbm, edge_hbm, *rest):
    with_own = len(rest) > 4
    if with_own:
        self_hbm, out_ref, *own_refs, feat_ref, edge_ref, sems, self_ref, trans_ref = rest
    else:
        out_ref, feat_ref, edge_ref, sems = rest
    copies = [pltpu.make_async_copy(edge_hbm, edge_ref, sems.at[0]),
              pltpu.make_async_copy(feat_hbm, feat_ref, sems.at[1])]
    if with_own:
        copies.append(pltpu.make_async_copy(self_hbm, self_ref, sems.at[2]))
    for copy in copies:
        copy.start()
    owned = feat_ref.shape[0]
    _, mult, cap = edge_ref.shape
    slots = len(order) * SLOT_PAD
    copies[0].wait()
    fill = jnp.full((mult, SLOT_PAD - cap), owned, jnp.int32)
    ids = jnp.concatenate([p for d in order for p in (edge_ref[d], fill)], axis=1)
    row = lax.broadcasted_iota(jnp.int32, (owned, slots), 0)
    weight = jnp.zeros((owned, slots), F32)
    count = jnp.zeros((1, slots), F32)
    for m in range(ids.shape[0]):
        weight += (row == ids[m:m + 1, :]).astype(F32)
        count += (ids[m:m + 1, :] < owned).astype(F32)
    pick = weight.T.astype(BF16)
    r = lax.broadcasted_iota(jnp.int32, (slots, slots), 0)
    c = lax.broadcasted_iota(jnp.int32, (slots, slots), 1)
    here = ((r & (SLOT_PAD - 1)) == cap) & ((c - (c & (SLOT_PAD - 1))) == (r - (r & (SLOT_PAD - 1))))
    spread = jnp.where(here, jnp.broadcast_to(count, (slots, slots)), 0.0).astype(BF16)
    c2 = lax.broadcasted_iota(jnp.int32, (slots, 128), 0)
    l2 = lax.broadcasted_iota(jnp.int32, (slots, 128), 1)
    fold = ((c2 & (SLOT_PAD - 1)) == l2).astype(BF16)
    counts = dot(spread, fold)
    copies[1].wait()
    feat = feat_ref[...]
    high = feat.astype(BF16)
    low = (feat - high.astype(F32)).astype(BF16)
    sums = dot(pick, high) + dot(pick, low)
    out_ref[:, :128] = (sums[:, :128] + counts).astype(BF16)
    out_ref[:, 128:] = sums[:, 128:].astype(BF16)
    if with_own:
        copies[2].wait()
        write_own(plan, self_ref, *own_refs, trans_ref)


def neighbor_mean(cap, rows, recv, targets):
    slots = rows.shape[0]
    target = lax.broadcasted_iota(jnp.int32, (targets, slots), 0)
    onehot = (target == recv).astype(BF16)
    r = lax.broadcasted_iota(jnp.int32, (slots, slots), 0)
    c = lax.broadcasted_iota(jnp.int32, (slots, slots), 1)
    from_count = (c == (r - (r & (SLOT_PAD - 1)) + cap)).astype(BF16)
    copied = dot(from_count, rows[:, :128])
    r2 = lax.broadcasted_iota(jnp.int32, (slots, 128), 0)
    l2 = lax.broadcasted_iota(jnp.int32, (slots, 128), 1)
    counts = jnp.where((r2 & (SLOT_PAD - 1)) == l2, copied, 0.0).astype(BF16)
    number = jnp.sum(dot(onehot, counts), axis=1, keepdims=True)
    return (dot(onehot, rows) / jnp.maximum(number, 1.0)).astype(BF16)


def forward(preact, cot):
    sig = jax.nn.sigmoid(preact)
    hidden = (preact * sig).astype(BF16)
    grad = (cot.astype(F32) * (sig * (1.0 + preact * (1.0 - sig)))).astype(BF16)
    return hidden, grad


class Plan:
    def __init__(self, mesh, width, out_width):
        self.ns, self.nt = mesh.shape["store"], mesh.shape["trainer"]
        self.gx = 2 if self.ns % 2 == 0 else 1
        self.nz = self.ns // self.gx
        self.gc = 2
        self.gy = max(self.nt // self.gc, 1)
        self.shard = width // self.ns
        self.rows = self.nz * self.shard
        self.cols = out_width // self.gy
        self.peers = [(dx, dy) for dx in range(self.gx) for dy in range(self.gy)]

    def fits(self):
        pow2 = all((n & (n - 1)) == 0 for n in (self.ns, self.nt))
        return (pow2 and self.ns <= 8 and self.gx == 2 and self.gy == 2 and self.gy * self.gc == self.nt and self.cols % 128 == 0
                and self.shard % 16 == 0 and len(self.peers) <= 4 and self.nz <= 4)

    def place(self):
        s, t = lax.axis_index("store"), lax.axis_index("trainer")
        return s // self.gx, s % self.gx, t // self.gc, t % self.gc

    def send(self, array, to):
        pairs = []
        for s in range(self.ns):
            for t in range(self.nt):
                z, x, y, c = to(s // self.gx, s % self.gx, t // self.gc, t % self.gc)
                pairs.append((s * self.nt + t, (z * self.gx + x) * self.nt + y * self.gc + c))
        return lax.ppermute(array, ("store", "trainer"), pairs)

    def store_order(self):
        up = [(z, x) for z in reversed(range(self.nz)) for x in reversed(range(self.gx))]
        down = [(z, x) for z in range(self.nz) for x in range(self.gx)]
        turns = [at for pair in zip(up, down) for at in pair]
        return [z * self.gx + x for z, x in turns[:self.ns]]


def write_rows(plan, trans_ref, *outs):
    x = plan.place()[1]
    for dx, out in enumerate(outs):
        for z in range(plan.nz):
            start = pl.multiple_of((z * plan.gx + (x ^ dx)) * plan.shard, 16)
            out[z * plan.shard:(z + 1) * plan.shard, :] = trans_ref[pl.ds(start, plan.shard), :]


def write_own(plan, self_ref, own_ref, here_ref, there_ref, trans_ref):
    own_ref[...] = self_ref[...].astype(BF16)
    trans_ref[...] = self_ref[...].T.astype(BF16)
    write_rows(plan, trans_ref, here_ref, there_ref)


def mean_kernel(plan, cap, order, rows_ref, recv_ref, _, mean_ref, here_ref, there_ref, trans_ref):
    rows = jnp.concatenate(
        [rows_ref[p * SLOT_PAD:(p + 1) * SLOT_PAD, :] for p in (order.index(s) for s in range(plan.ns))], axis=0)
    mean = neighbor_mean(cap, rows, recv_ref[...], mean_ref.shape[0])
    mean_ref[...] = mean
    trans_ref[...] = mean.astype(F32).T.astype(BF16)
    write_rows(plan, trans_ref, here_ref, there_ref)


def layer_kernel(plan, mean_ref, self_ref, cot_ref, w_ref, hidden_ref, here_ref, there_ref, grad_ref):
    targets = self_ref.shape[0]
    preact = self_ref[...] + dot(mean_ref[...], w_ref[...])
    hidden, grad = forward(preact, cot_ref[...])
    hidden_ref[...] = hidden
    for b in range(grad_ref.shape[0]):
        grad_ref[b] = grad[:, b * 128:(b + 1) * 128]
    y, each = plan.place()[2], plan.cols // 128
    for dy, out in enumerate((here_ref, there_ref)):
        for b in range(each):
            out[b * targets:(b + 1) * targets, :] = grad_ref[(y ^ dy) * each + b]


def terms_kernel(plan, keep, *refs):
    n = len(plan.peers)
    own, mean, grad, out_ref = refs[:n], refs[n:2 * n], refs[2 * n:3 * n], refs[3 * n]
    targets = own[0].shape[1]
    use_own = plan.place()[3] == (0 if keep else 1)
    left = jnp.concatenate([jnp.where(use_own, o[...], m[...]) for o, m in zip(own, mean)], axis=1)
    right = jnp.concatenate(
        [jnp.concatenate([g[b * targets:(b + 1) * targets, :] for b in range(plan.cols // 128)], axis=1)
         for g in grad], axis=0)
    out_ref[...] = dot(left, right).astype(out_ref.dtype)


def core_sum_kernel(plan, keep_ref, got_ref, *rest):
    outs, total_ref = rest[:-1], rest[-1]
    total_ref[...] = keep_ref[...] + got_ref[...].astype(F32)
    z = plan.place()[0]
    for k, out in enumerate(outs):
        start = pl.multiple_of((z ^ k) * plan.shard, 16)
        out[...] = total_ref[pl.ds(start, plan.shard), :].astype(out.dtype)


def store_sum_kernel(*refs):
    total = refs[0][...]
    for r in refs[1:-1]:
        total += r[...].astype(F32)
    refs[-1][...] = total.astype(BF16)


def assemble_kernel(plan, *refs):
    parts, (self_ref, neigh_ref, both_ref) = refs[:-3], refs[-3:]
    _, _, y, c = plan.place()
    for i, part in enumerate(parts):
        cols = pl.ds(pl.multiple_of((y ^ (i // plan.gc)) * plan.cols, 128), plan.cols)
        both_ref[c ^ (i % plan.gc), :, cols] = part[...].astype(F32)
    self_ref[...] = both_ref[0]
    neigh_ref[...] = both_ref[1]


def per_device(plan, features, self_rows, edge_row, recv_target, cotangent, w_self, w_neigh):
    owned, width = features.shape
    out_width = w_self.shape[1]
    targets = self_rows.shape[0]
    ns, cap, mult = edge_row.shape[2:]
    slots = ns * SLOT_PAD
    edges = edge_row[0, 0].transpose(0, 2, 1)
    pad = ((0, 0), (0, SLOT_PAD - cap))
    recv = jnp.pad(recv_target[0, 0], pad, constant_values=targets).reshape(1, slots)

    fits = plan.fits()
    order = plan.store_order() if fits else list(range(ns))
    rows, cols, n = plan.rows, plan.cols, len(plan.peers)
    scratch = [pltpu.VMEM(features.shape, F32), pltpu.VMEM(edges.shape, jnp.int32),
               pltpu.SemaphoreType.DMA((3,))]
    outs, more = [shape((slots, width), BF16)], []
    if fits:
        outs += [shape((targets, width), BF16)] + [shape((rows, targets), BF16)] * 2
        more = [self_rows]
        scratch += [pltpu.VMEM(self_rows.shape, F32), pltpu.VMEM((width, targets), BF16)]
    sums, *owns = call(
        functools.partial(slot_sums_kernel, plan, order), outs, (), hbm=[features, edges] + more,
        flops=4 * slots * owned * width, vmem=60 if fits else 16, scratch=scratch)
    arrived = lax.all_to_all(sums.reshape(ns, SLOT_PAD, width), "store", split_axis=0, concat_axis=0,
                             tiled=True, axis_index_groups=[order]).reshape(slots, width)
    if not fits:
        own = self_rows.astype(BF16)
        mean = neighbor_mean(cap, arrived, recv, targets)
        preact = dot(own, w_self) + dot(mean, w_neigh)
        hidden, grad = forward(preact, cotangent)
        both = jnp.concatenate([own.T.reshape(ns, -1, targets), mean.T.reshape(ns, -1, targets)], axis=1)
        terms = dot(both.reshape(2 * width, targets), grad)
        part = lax.psum_scatter(terms, "store", scatter_dimension=0, tiled=True)
        total = lax.psum(part, "trainer")
        return hidden, total[:plan.shard], total[plan.shard:]

    def to_x(array):
        return plan.send(array, lambda z, x, y, c: (z, 1 - x, y, c))

    def to_y(array):
        return plan.send(array, lambda z, x, y, c: (z, x, 1 - y, c))

    def to_diagonal(array):
        return plan.send(array, lambda z, x, y, c: (z, 1 - x, 1 - y, c))

    def held(array, *until):
        return lax.optimization_barrier((array,) + until)[0]

    own, own_here, own_there = owns
    own_all = [own_here, to_y(own_here), to_x(own_there), to_diagonal(own_there)]
    self_term = dot(own, w_self)

    mean, mean_here, mean_there = call(
        functools.partial(mean_kernel, plan, cap, order),
        [shape((targets, width), BF16)] + [shape((rows, targets), BF16)] * 2, [arrived, recv, self_term],
        scratch=[pltpu.VMEM((width, targets), BF16)], flops=2 * targets * width * slots)
    hidden, grad_here, grad_there = call(
        functools.partial(layer_kernel, plan),
        [shape((targets, out_width), BF16)] + [shape((cols // 128 * targets, 128), BF16)] * 2,
        [mean, self_term, cotangent, w_neigh],
        scratch=[pltpu.VMEM((out_width // 128, targets, 128), BF16)],
        flops=2 * targets * width * out_width)
    mean_x, grad_y = to_x(mean_there), to_y(grad_there)
    mean_all = [mean_here, to_y(mean_here), mean_x, to_y(held(mean_x, *own_all[1:]))]
    grad_all = [grad_here, grad_y, to_x(grad_here), to_x(grad_y)]
    factors = own_all + mean_all + grad_all
    (give,) = call(functools.partial(terms_kernel, plan, False), [shape((rows, cols), BF16)], factors,
                   flops=2 * rows * cols * targets * n)
    (keep,) = call(functools.partial(terms_kernel, plan, True), [shape((rows, cols), F32)], factors,
                   flops=2 * rows * cols * targets * n)
    got = plan.send(give, lambda z, x, y, c: (z, x, y, 1 - c))
    block = (plan.shard, cols)
    mine, *others = call(
        functools.partial(core_sum_kernel, plan),
        [shape(block, F32)] + [shape(block, BF16)] * (plan.nz - 1), [keep, got],
        scratch=[pltpu.VMEM((rows, cols), F32)])
    far_first = sorted(range(1, plan.nz), key=lambda k: (k < 2, k))
    got = [plan.send(others[k - 1], lambda z, x, y, c, k=k: (z ^ k, x, y, c)) for k in far_first]
    (quarter,) = call(store_sum_kernel, [shape(block, BF16)], [mine] + got)
    column = [quarter] + [plan.send(quarter, lambda z, x, y, c, i=i: (z, x, y ^ i, c))
                          for i in range(1, plan.gy)]
    quarters = [q for part in column
                for q in (part, plan.send(part, lambda z, x, y, c: (z, x, y, 1 - c)))]
    grads = call(functools.partial(assemble_kernel, plan),
                 [shape((plan.shard, out_width), F32)] * 2, quarters,
                 scratch=[pltpu.VMEM((2, plan.shard, out_width), F32)])
    return hidden, grads[0], grads[1]


def solution(mesh):
    in_specs = (
        P("store", None),
        P(("store", "trainer"), None),
        P("trainer", "store", None, None, None),
        P("trainer", "store", None, None),
        P(("store", "trainer"), None),
        P(),
        P(),
    )
    out_specs = (P(("store", "trainer"), None), P("store", None), P("store", None))

    def run(features, self_rows, edge_row, recv_target, cotangent, w_self, w_neigh):
        plan = Plan(mesh, features.shape[1], w_self.shape[1])
        return jax.shard_map(
            functools.partial(per_device, plan), mesh=mesh, in_specs=in_specs,
            out_specs=out_specs, check_vma=False,
        )(features, self_rows, edge_row, recv_target, cotangent, w_self, w_neigh)

    return run
```

```python
import functools

import jax
import jax.numpy as jnp
from jax import lax
from jax.experimental import pallas as pl
from jax.experimental.pallas import tpu as pltpu
from jax.sharding import PartitionSpec as P

BF16, F32 = jnp.bfloat16, jnp.float32
SLOT_PAD = 16
VMEM = pl.BlockSpec(memory_space=pltpu.VMEM)
ANY = pl.BlockSpec(memory_space=pl.ANY)
HBM = pl.BlockSpec(memory_space=pltpu.HBM)


def dot(a, b):
    return jnp.dot(a, b, preferred_element_type=F32)


def call(body, outs, args, unread=(), hbm=(), scratch=(), flops=0, vmem=16):
    moved = sum(a.size * a.dtype.itemsize for a in (*args, *outs))
    return pl.pallas_call(
        body,
        out_shape=list(outs),
        in_specs=[VMEM] * len(args) + [ANY] * len(unread) + [HBM] * len(hbm),
        out_specs=[VMEM] * len(outs),
        scratch_shapes=list(scratch),
        compiler_params=pltpu.CompilerParams(vmem_limit_bytes=vmem * 1024 * 1024),
        cost_estimate=pl.CostEstimate(flops=flops, bytes_accessed=moved, transcendentals=0),
    )(*args, *unread, *hbm)


def shape(dims, kind):
    return jax.ShapeDtypeStruct(dims, kind)


def slot_sums_kernel(plan, order, feat_hbm, edge_hbm, *rest):
    with_own = len(rest) > 4
    if with_own:
        self_hbm, out_ref, *own_refs, feat_ref, edge_ref, sems, self_ref, trans_ref = rest
    else:
        out_ref, feat_ref, edge_ref, sems = rest
    copies = [pltpu.make_async_copy(edge_hbm, edge_ref, sems.at[0]),
              pltpu.make_async_copy(feat_hbm, feat_ref, sems.at[1])]
    if with_own:
        copies.append(pltpu.make_async_copy(self_hbm, self_ref, sems.at[2]))
    for copy in copies:
        copy.start()
    owned = feat_ref.shape[0]
    _, mult, cap = edge_ref.shape
    slots = len(order) * SLOT_PAD
    copies[0].wait()
    fill = jnp.full((mult, SLOT_PAD - cap), owned, jnp.int32)
    ids = jnp.concatenate([p for d in order for p in (edge_ref[d], fill)], axis=1)
    row = lax.broadcasted_iota(jnp.int32, (owned, slots), 0)
    weight = jnp.zeros((owned, slots), F32)
    count = jnp.zeros((1, slots), F32)
    for m in range(ids.shape[0]):
        weight += (row == ids[m:m + 1, :]).astype(F32)
        count += (ids[m:m + 1, :] < owned).astype(F32)
    pick = weight.T.astype(BF16)
    r = lax.broadcasted_iota(jnp.int32, (slots, slots), 0)
    c = lax.broadcasted_iota(jnp.int32, (slots, slots), 1)
    here = ((r & (SLOT_PAD - 1)) == cap) & ((c - (c & (SLOT_PAD - 1))) == (r - (r & (SLOT_PAD - 1))))
    spread = jnp.where(here, jnp.broadcast_to(count, (slots, slots)), 0.0).astype(BF16)
    c2 = lax.broadcasted_iota(jnp.int32, (slots, 128), 0)
    l2 = lax.broadcasted_iota(jnp.int32, (slots, 128), 1)
    fold = ((c2 & (SLOT_PAD - 1)) == l2).astype(BF16)
    counts = dot(spread, fold)
    copies[1].wait()
    feat = feat_ref[...]
    high = feat.astype(BF16)
    low = (feat - high.astype(F32)).astype(BF16)
    sums = dot(pick, high) + dot(pick, low)
    out_ref[:, :128] = (sums[:, :128] + counts).astype(BF16)
    out_ref[:, 128:] = sums[:, 128:].astype(BF16)
    if with_own:
        copies[2].wait()
        write_own(plan, self_ref, *own_refs, trans_ref)


def neighbor_mean(cap, rows, recv, targets):
    slots = rows.shape[0]
    target = lax.broadcasted_iota(jnp.int32, (targets, slots), 0)
    onehot = (target == recv).astype(BF16)
    r = lax.broadcasted_iota(jnp.int32, (slots, slots), 0)
    c = lax.broadcasted_iota(jnp.int32, (slots, slots), 1)
    from_count = (c == (r - (r & (SLOT_PAD - 1)) + cap)).astype(BF16)
    copied = dot(from_count, rows[:, :128])
    r2 = lax.broadcasted_iota(jnp.int32, (slots, 128), 0)
    l2 = lax.broadcasted_iota(jnp.int32, (slots, 128), 1)
    counts = jnp.where((r2 & (SLOT_PAD - 1)) == l2, copied, 0.0).astype(BF16)
    number = jnp.sum(dot(onehot, counts), axis=1, keepdims=True)
    return (dot(onehot, rows) / jnp.maximum(number, 1.0)).astype(BF16)


def forward(preact, cot):
    sig = jax.nn.sigmoid(preact)
    hidden = (preact * sig).astype(BF16)
    grad = (cot.astype(F32) * (sig * (1.0 + preact * (1.0 - sig)))).astype(BF16)
    return hidden, grad


class Plan:
    def __init__(self, mesh, width, out_width):
        self.ns, self.nt = mesh.shape["store"], mesh.shape["trainer"]
        self.gx = 2 if self.ns % 2 == 0 else 1
        self.nz = self.ns // self.gx
        self.gc = 2
        self.gy = max(self.nt // self.gc, 1)
        self.shard = width // self.ns
        self.rows = self.nz * self.shard
        self.cols = out_width // self.gy
        self.peers = [(dx, dy) for dx in range(self.gx) for dy in range(self.gy)]

    def fits(self):
        pow2 = all((n & (n - 1)) == 0 for n in (self.ns, self.nt))
        return (pow2 and self.ns <= 8 and self.gx == 2 and self.gy == 2 and self.gy * self.gc == self.nt and self.cols % 128 == 0
                and self.shard % 16 == 0 and len(self.peers) <= 4 and self.nz <= 4)

    def place(self):
        s, t = lax.axis_index("store"), lax.axis_index("trainer")
        return s // self.gx, s % self.gx, t // self.gc, t % self.gc

    def send(self, array, to):
        pairs = []
        for s in range(self.ns):
            for t in range(self.nt):
                z, x, y, c = to(s // self.gx, s % self.gx, t // self.gc, t % self.gc)
                pairs.append((s * self.nt + t, (z * self.gx + x) * self.nt + y * self.gc + c))
        return lax.ppermute(array, ("store", "trainer"), pairs)

    def store_order(self):
        up = [(z, x) for z in reversed(range(self.nz)) for x in reversed(range(self.gx))]
        down = [(z, x) for z in range(self.nz) for x in range(self.gx)]
        turns = [at for pair in zip(up, down) for at in pair]
        return [z * self.gx + x for z, x in turns[:self.ns]]


def write_rows(plan, trans_ref, *outs):
    x = plan.place()[1]
    for dx, out in enumerate(outs):
        for z in range(plan.nz):
            start = pl.multiple_of((z * plan.gx + (x ^ dx)) * plan.shard, 16)
            out[z * plan.shard:(z + 1) * plan.shard, :] = trans_ref[pl.ds(start, plan.shard), :]


def write_own(plan, self_ref, own_ref, here_ref, there_ref, trans_ref):
    own_ref[...] = self_ref[...].astype(BF16)
    trans_ref[...] = self_ref[...].T.astype(BF16)
    write_rows(plan, trans_ref, here_ref, there_ref)


def mean_kernel(plan, cap, order, rows_ref, recv_ref, _, mean_ref, here_ref, there_ref, trans_ref):
    rows = jnp.concatenate(
        [rows_ref[p * SLOT_PAD:(p + 1) * SLOT_PAD, :] for p in (order.index(s) for s in range(plan.ns))], axis=0)
    mean = neighbor_mean(cap, rows, recv_ref[...], mean_ref.shape[0])
    mean_ref[...] = mean
    trans_ref[...] = mean.astype(F32).T.astype(BF16)
    write_rows(plan, trans_ref, here_ref, there_ref)


def layer_kernel(plan, mean_ref, self_ref, cot_ref, w_ref, hidden_ref, here_ref, there_ref, grad_ref):
    targets = self_ref.shape[0]
    preact = self_ref[...] + dot(mean_ref[...], w_ref[...])
    hidden, grad = forward(preact, cot_ref[...])
    hidden_ref[...] = hidden
    for b in range(grad_ref.shape[0]):
        grad_ref[b] = grad[:, b * 128:(b + 1) * 128]
    y, each = plan.place()[2], plan.cols // 128
    for dy, out in enumerate((here_ref, there_ref)):
        for b in range(each):
            out[b * targets:(b + 1) * targets, :] = grad_ref[(y ^ dy) * each + b]


def left_kernel(plan, *refs):
    n = len(plan.peers)
    own, mean, (give_ref, keep_ref) = refs[:n], refs[n:2 * n], refs[2 * n:]
    targets = own[0].shape[1]
    keep_own = plan.place()[3] == 0
    for i, (o, m) in enumerate(zip(own, mean)):
        at = slice(i * targets, (i + 1) * targets)
        keep_ref[:, at] = jnp.where(keep_own, o[...], m[...])
        give_ref[:, at] = jnp.where(keep_own, m[...], o[...])


def terms_kernel(plan, left_ref, *refs):
    grad, out_ref = refs[:-1], refs[-1]
    targets = left_ref.shape[1] // len(grad)
    right = jnp.concatenate(
        [jnp.concatenate([g[b * targets:(b + 1) * targets, :] for b in range(plan.cols // 128)], axis=1)
         for g in grad], axis=0)
    out_ref[...] = dot(left_ref[...], right).astype(out_ref.dtype)


def core_sum_kernel(plan, keep_ref, got_ref, *rest):
    outs, total_ref = rest[:-1], rest[-1]
    total_ref[...] = keep_ref[...] + got_ref[...].astype(F32)
    z = plan.place()[0]
    for k, out in enumerate(outs):
        start = pl.multiple_of((z ^ k) * plan.shard, 16)
        out[...] = total_ref[pl.ds(start, plan.shard), :].astype(out.dtype)


def store_sum_kernel(*refs):
    total = refs[0][...]
    for r in refs[1:-1]:
        total += r[...].astype(F32)
    refs[-1][...] = total.astype(BF16)


def assemble_kernel(plan, *refs):
    parts, (self_ref, neigh_ref, both_ref) = refs[:-3], refs[-3:]
    _, _, y, c = plan.place()
    for i, part in enumerate(parts):
        cols = pl.ds(pl.multiple_of((y ^ (i // plan.gc)) * plan.cols, 128), plan.cols)
        both_ref[c ^ (i % plan.gc), :, cols] = part[...].astype(F32)
    self_ref[...] = both_ref[0]
    neigh_ref[...] = both_ref[1]


def per_device(plan, features, self_rows, edge_row, recv_target, cotangent, w_self, w_neigh):
    owned, width = features.shape
    out_width = w_self.shape[1]
    targets = self_rows.shape[0]
    ns, cap, mult = edge_row.shape[2:]
    slots = ns * SLOT_PAD
    edges = edge_row[0, 0].transpose(0, 2, 1)
    pad = ((0, 0), (0, SLOT_PAD - cap))
    recv = jnp.pad(recv_target[0, 0], pad, constant_values=targets).reshape(1, slots)

    fits = plan.fits()
    order = plan.store_order() if fits else list(range(ns))
    rows, cols, n = plan.rows, plan.cols, len(plan.peers)
    scratch = [pltpu.VMEM(features.shape, F32), pltpu.VMEM(edges.shape, jnp.int32),
               pltpu.SemaphoreType.DMA((3,))]
    outs, more = [shape((slots, width), BF16)], []
    if fits:
        outs += [shape((targets, width), BF16)] + [shape((rows, targets), BF16)] * 2
        more = [self_rows]
        scratch += [pltpu.VMEM(self_rows.shape, F32), pltpu.VMEM((width, targets), BF16)]
    sums, *owns = call(
        functools.partial(slot_sums_kernel, plan, order), outs, (), hbm=[features, edges] + more,
        flops=4 * slots * owned * width, vmem=60 if fits else 16, scratch=scratch)
    arrived = lax.all_to_all(sums.reshape(ns, SLOT_PAD, width), "store", split_axis=0, concat_axis=0,
                             tiled=True, axis_index_groups=[order]).reshape(slots, width)
    if not fits:
        own = self_rows.astype(BF16)
        mean = neighbor_mean(cap, arrived, recv, targets)
        preact = dot(own, w_self) + dot(mean, w_neigh)
        hidden, grad = forward(preact, cotangent)
        both = jnp.concatenate([own.T.reshape(ns, -1, targets), mean.T.reshape(ns, -1, targets)], axis=1)
        terms = dot(both.reshape(2 * width, targets), grad)
        part = lax.psum_scatter(terms, "store", scatter_dimension=0, tiled=True)
        total = lax.psum(part, "trainer")
        return hidden, total[:plan.shard], total[plan.shard:]

    def to_x(array):
        return plan.send(array, lambda z, x, y, c: (z, 1 - x, y, c))

    def to_y(array):
        return plan.send(array, lambda z, x, y, c: (z, x, 1 - y, c))

    def to_diagonal(array):
        return plan.send(array, lambda z, x, y, c: (z, 1 - x, 1 - y, c))

    def held(array, *until):
        return lax.optimization_barrier((array,) + until)[0]

    own, own_here, own_there = owns
    own_all = [own_here, to_y(own_here), to_x(own_there), to_diagonal(own_there)]
    self_term = dot(own, w_self)

    mean, mean_here, mean_there = call(
        functools.partial(mean_kernel, plan, cap, order),
        [shape((targets, width), BF16)] + [shape((rows, targets), BF16)] * 2, [arrived, recv, self_term],
        scratch=[pltpu.VMEM((width, targets), BF16)], flops=2 * targets * width * slots)
    hidden, grad_here, grad_there = call(
        functools.partial(layer_kernel, plan),
        [shape((targets, out_width), BF16)] + [shape((cols // 128 * targets, 128), BF16)] * 2,
        [mean, self_term, cotangent, w_neigh],
        scratch=[pltpu.VMEM((out_width // 128, targets, 128), BF16)],
        flops=2 * targets * width * out_width)
    mean_x, grad_y = to_x(mean_there), to_y(grad_there)
    mean_all = [mean_here, to_y(mean_here), mean_x, to_y(held(mean_x, *own_all[1:]))]
    grad_all = [grad_here, grad_y, to_x(grad_here), to_x(grad_y)]
    give_left, keep_left = call(functools.partial(left_kernel, plan), [shape((rows, n * targets), BF16)] * 2,
                                own_all + mean_all)
    (give,) = call(functools.partial(terms_kernel, plan), [shape((rows, cols), BF16)], [give_left] + grad_all,
                   flops=2 * rows * cols * targets * n)
    (keep,) = call(functools.partial(terms_kernel, plan), [shape((rows, cols), F32)], [keep_left] + grad_all,
                   flops=2 * rows * cols * targets * n)
    got = plan.send(give, lambda z, x, y, c: (z, x, y, 1 - c))
    block = (plan.shard, cols)
    mine, *others = call(
        functools.partial(core_sum_kernel, plan),
        [shape(block, F32)] + [shape(block, BF16)] * (plan.nz - 1), [keep, got],
        scratch=[pltpu.VMEM((rows, cols), F32)])
    far_first = sorted(range(1, plan.nz), key=lambda k: (k < 2, k))
    got = [plan.send(others[k - 1], lambda z, x, y, c, k=k: (z ^ k, x, y, c)) for k in far_first]
    (quarter,) = call(store_sum_kernel, [shape(block, BF16)], [mine] + got)
    column = [quarter] + [plan.send(quarter, lambda z, x, y, c, i=i: (z, x, y ^ i, c))
                          for i in range(1, plan.gy)]
    quarters = [q for part in column
                for q in (part, plan.send(part, lambda z, x, y, c: (z, x, y, 1 - c)))]
    grads = call(functools.partial(assemble_kernel, plan),
                 [shape((plan.shard, out_width), F32)] * 2, quarters,
                 scratch=[pltpu.VMEM((2, plan.shard, out_width), F32)])
    return hidden, grads[0], grads[1]


def solution(mesh):
    in_specs = (
        P("store", None),
        P(("store", "trainer"), None),
        P("trainer", "store", None, None, None),
        P("trainer", "store", None, None),
        P(("store", "trainer"), None),
        P(),
        P(),
    )
    out_specs = (P(("store", "trainer"), None), P("store", None), P("store", None))

    def run(features, self_rows, edge_row, recv_target, cotangent, w_self, w_neigh):
        plan = Plan(mesh, features.shape[1], w_self.shape[1])
        return jax.shard_map(
            functools.partial(per_device, plan), mesh=mesh, in_specs=in_specs,
            out_specs=out_specs, check_vma=False,
        )(features, self_rows, edge_row, recv_target, cotangent, w_self, w_neigh)

    return run
```

```python
import functools

import jax
import jax.numpy as jnp
from jax import lax
from jax.experimental import pallas as pl
from jax.experimental.pallas import tpu as pltpu
from jax.sharding import PartitionSpec as P

BF16, F32 = jnp.bfloat16, jnp.float32
SLOT_PAD = 16
VMEM = pl.BlockSpec(memory_space=pltpu.VMEM)
ANY = pl.BlockSpec(memory_space=pl.ANY)
HBM = pl.BlockSpec(memory_space=pltpu.HBM)


def dot(a, b):
    return jnp.dot(a, b, preferred_element_type=F32)


def call(body, outs, args, unread=(), hbm=(), scratch=(), flops=0, vmem=16):
    moved = sum(a.size * a.dtype.itemsize for a in (*args, *outs))
    return pl.pallas_call(
        body,
        out_shape=list(outs),
        in_specs=[VMEM] * len(args) + [ANY] * len(unread) + [HBM] * len(hbm),
        out_specs=[VMEM] * len(outs),
        scratch_shapes=list(scratch),
        compiler_params=pltpu.CompilerParams(vmem_limit_bytes=vmem * 1024 * 1024),
        cost_estimate=pl.CostEstimate(flops=flops, bytes_accessed=moved, transcendentals=0),
    )(*args, *unread, *hbm)


def shape(dims, kind):
    return jax.ShapeDtypeStruct(dims, kind)


def pack_rows(cap, width):
    return cap * (width // 128) + 8


def pack(sums, counts, cap):
    blocks = sums.shape[1] // 128
    out = []
    for d in range(sums.shape[0] // SLOT_PAD):
        at = d * SLOT_PAD
        part = [sums[at:at + SLOT_PAD, j * 128:(j + 1) * 128] for j in range(blocks)]
        out += [p[:8] for p in part]
        out += [jnp.concatenate([part[j][8:cap], part[j + 1][8:cap]], axis=0) for j in range(0, blocks, 2)]
        out.append(counts[at + 8:at + SLOT_PAD])
    return jnp.concatenate(out, axis=0).astype(BF16)


def unpack(packed, order, cap, blocks):
    size = packed.shape[0] // len(order)
    rows = []
    for s in range(len(order)):
        at = order.index(s) * size
        part = packed[at:at + size, :].astype(F32)
        tail, counts = part[blocks * 8:size - 8], part[size - 8:]
        columns = []
        for j in range(blocks):
            low = tail[j // 2 * 8 + j % 2 * 4:j // 2 * 8 + j % 2 * 4 + 4]
            rest = counts[4:] if j == 0 else jnp.zeros((4, 128), F32)
            columns.append(jnp.concatenate([part[j * 8:j * 8 + 8], low, rest], axis=0))
        rows.append(jnp.concatenate(columns, axis=1))
    return jnp.concatenate(rows, axis=0).astype(BF16)


def slot_sums_kernel(plan, order, feat_hbm, edge_hbm, *rest):
    with_own = len(rest) > 4
    if with_own:
        self_hbm, out_ref, *own_refs, feat_ref, edge_ref, sems, self_ref, trans_ref = rest
    else:
        out_ref, feat_ref, edge_ref, sems = rest
    copies = [pltpu.make_async_copy(edge_hbm, edge_ref, sems.at[0]),
              pltpu.make_async_copy(feat_hbm, feat_ref, sems.at[1])]
    if with_own:
        copies.append(pltpu.make_async_copy(self_hbm, self_ref, sems.at[2]))
    for copy in copies:
        copy.start()
    owned = feat_ref.shape[0]
    _, mult, cap = edge_ref.shape
    slots = len(order) * SLOT_PAD
    copies[0].wait()
    fill = jnp.full((mult, SLOT_PAD - cap), owned, jnp.int32)
    ids = jnp.concatenate([p for d in order for p in (edge_ref[d], fill)], axis=1)
    row = lax.broadcasted_iota(jnp.int32, (owned, slots), 0)
    weight = jnp.zeros((owned, slots), F32)
    count = jnp.zeros((1, slots), F32)
    for m in range(ids.shape[0]):
        weight += (row == ids[m:m + 1, :]).astype(F32)
        count += (ids[m:m + 1, :] < owned).astype(F32)
    pick = weight.T.astype(BF16)
    r = lax.broadcasted_iota(jnp.int32, (slots, slots), 0)
    c = lax.broadcasted_iota(jnp.int32, (slots, slots), 1)
    here = ((r & (SLOT_PAD - 1)) == cap) & ((c - (c & (SLOT_PAD - 1))) == (r - (r & (SLOT_PAD - 1))))
    spread = jnp.where(here, jnp.broadcast_to(count, (slots, slots)), 0.0).astype(BF16)
    c2 = lax.broadcasted_iota(jnp.int32, (slots, 128), 0)
    l2 = lax.broadcasted_iota(jnp.int32, (slots, 128), 1)
    fold = ((c2 & (SLOT_PAD - 1)) == l2).astype(BF16)
    counts = dot(spread, fold)
    copies[1].wait()
    feat = feat_ref[...]
    high = feat.astype(BF16)
    low = (feat - high.astype(F32)).astype(BF16)
    sums = dot(pick, high) + dot(pick, low)
    out_ref[...] = pack(sums, counts, cap)
    if with_own:
        copies[2].wait()
        write_own(plan, self_ref, *own_refs, trans_ref)


def neighbor_mean(cap, rows, recv, targets):
    slots = rows.shape[0]
    target = lax.broadcasted_iota(jnp.int32, (targets, slots), 0)
    onehot = (target == recv).astype(BF16)
    r = lax.broadcasted_iota(jnp.int32, (slots, slots), 0)
    c = lax.broadcasted_iota(jnp.int32, (slots, slots), 1)
    from_count = (c == (r - (r & (SLOT_PAD - 1)) + cap)).astype(BF16)
    copied = dot(from_count, rows[:, :128])
    r2 = lax.broadcasted_iota(jnp.int32, (slots, 128), 0)
    l2 = lax.broadcasted_iota(jnp.int32, (slots, 128), 1)
    counts = jnp.where((r2 & (SLOT_PAD - 1)) == l2, copied, 0.0).astype(BF16)
    number = jnp.sum(dot(onehot, counts), axis=1, keepdims=True)
    return (dot(onehot, rows) / jnp.maximum(number, 1.0)).astype(BF16)


def forward(preact, cot):
    sig = jax.nn.sigmoid(preact)
    hidden = (preact * sig).astype(BF16)
    grad = (cot.astype(F32) * (sig * (1.0 + preact * (1.0 - sig)))).astype(BF16)
    return hidden, grad


class Plan:
    def __init__(self, mesh, width, out_width):
        self.ns, self.nt = mesh.shape["store"], mesh.shape["trainer"]
        self.gx = 2 if self.ns % 2 == 0 else 1
        self.nz = self.ns // self.gx
        self.gc = 2
        self.gy = max(self.nt // self.gc, 1)
        self.shard = width // self.ns
        self.rows = self.nz * self.shard
        self.cols = out_width // self.gy
        self.peers = [(dx, dy) for dx in range(self.gx) for dy in range(self.gy)]

    def fits(self):
        pow2 = all((n & (n - 1)) == 0 for n in (self.ns, self.nt))
        return (pow2 and self.ns <= 8 and self.gx == 2 and self.gy == 2 and self.gy * self.gc == self.nt and self.cols % 128 == 0
                and self.shard % 16 == 0 and len(self.peers) <= 4 and self.nz == 4)

    def place(self):
        s, t = lax.axis_index("store"), lax.axis_index("trainer")
        return s // self.gx, s % self.gx, t // self.gc, t % self.gc

    def far(self):
        return list(range(2, self.nz))

    def near(self):
        return list(range(min(2, self.nz)))[::-1]

    def send(self, array, to):
        pairs = []
        for s in range(self.ns):
            for t in range(self.nt):
                z, x, y, c = to(s // self.gx, s % self.gx, t // self.gc, t % self.gc)
                pairs.append((s * self.nt + t, (z * self.gx + x) * self.nt + y * self.gc + c))
        return lax.ppermute(array, ("store", "trainer"), pairs)

    def store_order(self):
        up = [(z, x) for z in reversed(range(self.nz)) for x in reversed(range(self.gx))]
        down = [(z, x) for z in range(self.nz) for x in range(self.gx)]
        turns = [at for pair in zip(up, down) for at in pair]
        return [z * self.gx + x for z, x in turns[:self.ns]]


def write_rows(plan, trans_ref, *outs):
    x = plan.place()[1]
    for dx, out in enumerate(outs):
        for z in range(plan.nz):
            start = pl.multiple_of((z * plan.gx + (x ^ dx)) * plan.shard, 16)
            out[z * plan.shard:(z + 1) * plan.shard, :] = trans_ref[pl.ds(start, plan.shard), :]


def write_own(plan, self_ref, own_ref, here_ref, there_ref, trans_ref):
    own_ref[...] = self_ref[...].astype(BF16)
    trans_ref[...] = self_ref[...].T.astype(BF16)
    write_rows(plan, trans_ref, here_ref, there_ref)


def mean_kernel(plan, cap, order, rows_ref, recv_ref, _, mean_ref, here_ref, there_ref, trans_ref):
    rows = unpack(rows_ref[...], order, cap, mean_ref.shape[1] // 128)
    targets = mean_ref.shape[0]
    fill = jnp.full((1, SLOT_PAD - cap), targets, jnp.int32)
    recv = jnp.concatenate([p for s in range(plan.ns) for p in (recv_ref[s:s + 1, :], fill)], axis=1)
    mean = neighbor_mean(cap, rows, recv, targets)
    mean_ref[...] = mean
    trans_ref[...] = mean.astype(F32).T.astype(BF16)
    write_rows(plan, trans_ref, here_ref, there_ref)


def layer_kernel(plan, mean_ref, self_ref, cot_ref, w_ref, hidden_ref, here_ref, there_ref, grad_ref):
    targets = self_ref.shape[0]
    preact = self_ref[...] + dot(mean_ref[...], w_ref[...])
    hidden, grad = forward(preact, cot_ref[...])
    hidden_ref[...] = hidden.astype(F32)
    for b in range(grad_ref.shape[0]):
        grad_ref[b] = grad[:, b * 128:(b + 1) * 128]
    y, each = plan.place()[2], plan.cols // 128
    for dy, out in enumerate((here_ref, there_ref)):
        for b in range(each):
            out[b * targets:(b + 1) * targets, :] = grad_ref[(y ^ dy) * each + b]


def left_kernel(plan, *refs):
    n = len(plan.peers)
    own, mean, outs = refs[n - 1::-1], refs[n:2 * n], refs[2 * n:]
    targets = own[0].shape[1]
    z, _, _, c = plan.place()
    keep_own = c == 0
    for i, (o, m) in enumerate(zip(own, mean)):
        at = slice(i * targets, (i + 1) * targets)
        for j, shards in enumerate((plan.far(), plan.near())):
            for r, k in enumerate(shards):
                rows = pl.ds(pl.multiple_of((z ^ k) * plan.shard, 16), plan.shard)
                to = slice(r * plan.shard, (r + 1) * plan.shard)
                outs[j][to, at] = jnp.where(keep_own, m[rows, :], o[rows, :])
                outs[2 + j][to, at] = jnp.where(keep_own, o[rows, :], m[rows, :])


def terms_kernel(left_ref, *refs):
    grad, out_ref = refs[:-1], refs[-1]
    targets = left_ref.shape[1] // len(grad)
    right = jnp.concatenate(
        [jnp.concatenate([g[b * targets:(b + 1) * targets, :] for b in range(grad[0].shape[0] // targets)], axis=1)
         for g in grad], axis=0)
    out_ref[...] = dot(left_ref[...], right).astype(out_ref.dtype)


def core_sum_kernel(plan, keep_ref, got_ref, *outs):
    for r, out in enumerate(outs):
        at = slice(r * plan.shard, (r + 1) * plan.shard)
        out[...] = (keep_ref[at, :] + got_ref[at, :].astype(F32)).astype(out.dtype)


def store_sum_kernel(*refs):
    total = refs[0][...]
    for r in refs[1:-1]:
        total += r[...].astype(F32)
    refs[-1][...] = total.astype(BF16)


def assemble_kernel(plan, *refs):
    parts, (self_ref, neigh_ref, both_ref) = refs[:-3], refs[-3:]
    _, _, y, c = plan.place()
    for i, part in enumerate(parts):
        cols = pl.ds(pl.multiple_of((y ^ (i // plan.gc)) * plan.cols, 128), plan.cols)
        both_ref[c ^ (i % plan.gc), :, cols] = part[...].astype(F32)
    self_ref[...] = both_ref[0]
    neigh_ref[...] = both_ref[1]


def per_device(plan, features, self_rows, edge_row, recv_target, cotangent, w_self, w_neigh):
    owned, width = features.shape
    out_width = w_self.shape[1]
    targets = self_rows.shape[0]
    ns, cap, mult = edge_row.shape[2:]
    slots = ns * SLOT_PAD
    edges = edge_row[0, 0].transpose(0, 2, 1)
    fits = plan.fits()
    order = plan.store_order() if fits else list(range(ns))
    rows, cols, n = plan.rows, plan.cols, len(plan.peers)
    scratch = [pltpu.VMEM(features.shape, F32), pltpu.VMEM(edges.shape, jnp.int32),
               pltpu.SemaphoreType.DMA((3,))]
    packed = pack_rows(cap, width)
    outs, more = [shape((ns * packed, 128), BF16)], []
    if fits:
        outs += [shape((targets, width), BF16)] + [shape((rows, targets), BF16)] * 2
        more = [self_rows]
        scratch += [pltpu.VMEM(self_rows.shape, F32), pltpu.VMEM((width, targets), BF16)]
    sums, *owns = call(
        functools.partial(slot_sums_kernel, plan, order), outs, (), hbm=[features, edges] + more,
        flops=4 * slots * owned * width, vmem=60 if fits else 16, scratch=scratch)
    arrived = lax.all_to_all(sums.reshape(ns, packed, 128), "store", split_axis=0, concat_axis=0,
                             tiled=True, axis_index_groups=[order]).reshape(ns * packed, 128)
    if not fits:
        own = self_rows.astype(BF16)
        recv = jnp.pad(recv_target[0, 0], ((0, 0), (0, SLOT_PAD - cap)), constant_values=targets).reshape(1, slots)
        mean = neighbor_mean(cap, unpack(arrived, order, cap, width // 128), recv, targets)
        preact = dot(own, w_self) + dot(mean, w_neigh)
        hidden, grad = forward(preact, cotangent)
        both = jnp.concatenate([own.T.reshape(ns, -1, targets), mean.T.reshape(ns, -1, targets)], axis=1)
        terms = dot(both.reshape(2 * width, targets), grad)
        part = lax.psum_scatter(terms, "store", scatter_dimension=0, tiled=True)
        total = lax.psum(part, "trainer")
        return hidden, total[:plan.shard], total[plan.shard:]

    def to_x(array):
        return plan.send(array, lambda z, x, y, c: (z, 1 - x, y, c))

    def to_y(array):
        return plan.send(array, lambda z, x, y, c: (z, x, 1 - y, c))

    def to_diagonal(array):
        return plan.send(array, lambda z, x, y, c: (z, 1 - x, 1 - y, c))

    def held(array, *until):
        return lax.optimization_barrier((array,) + until)[0]

    own, own_here, own_there = owns
    own_all = [own_here, to_y(own_here), to_x(own_there), to_diagonal(own_there)]
    self_term = dot(own, w_self)

    mean, mean_here, mean_there = call(
        functools.partial(mean_kernel, plan, cap, order),
        [shape((targets, width), BF16)] + [shape((rows, targets), BF16)] * 2, [arrived, recv_target[0, 0], self_term],
        scratch=[pltpu.VMEM((width, targets), BF16)], flops=2 * targets * width * slots)
    hidden, grad_here, grad_there = call(
        functools.partial(layer_kernel, plan),
        [shape((targets, out_width), F32)] + [shape((cols // 128 * targets, 128), BF16)] * 2,
        [mean, self_term, cotangent, w_neigh],
        scratch=[pltpu.VMEM((out_width // 128, targets, 128), BF16)],
        flops=2 * targets * width * out_width)
    mean_x, grad_y = to_x(mean_there), to_y(grad_there)
    grad_x = to_x(grad_here)
    mean_all = [mean_here, to_y(mean_here), mean_x, to_y(held(mean_x, *own_all[1:]))]
    grad_all = [grad_here, grad_y, grad_x, to_x(held(grad_y, mean_x, *own_all[1:]))]
    def to_core(array):
        return plan.send(array, lambda z, x, y, c: (z, x, y, 1 - c))

    def to_z(array, k):
        return plan.send(array, lambda z, x, y, c: (z ^ k, x, y, c))

    def terms(left, kind):
        return call(terms_kernel, [shape((left.shape[0], cols), kind)], [left] + grad_all,
                    flops=2 * left.shape[0] * cols * targets * n)[0]

    block = (plan.shard, cols)
    halves = [plan.far(), plan.near()]
    lefts = call(functools.partial(left_kernel, plan),
                 [shape((len(half) * plan.shard, n * targets), BF16) for half in halves * 2],
                 own_all[::-1] + mean_all)
    got, mine = [], None
    for half, give_left, keep_left in zip(halves, lefts[:2], lefts[2:]):
        came = to_core(terms(give_left, BF16))
        sums = call(functools.partial(core_sum_kernel, plan),
                    [shape(block, BF16 if k else F32) for k in half], [terms(keep_left, F32), came])
        for k, part in zip(half, sums):
            if k:
                got.append(to_z(part, k))
            else:
                mine = part
    (quarter,) = call(store_sum_kernel, [shape(block, BF16)], [mine] + got)
    column = [quarter] + [plan.send(quarter, lambda z, x, y, c, i=i: (z, x, y ^ i, c))
                          for i in range(1, plan.gy)]
    quarters = [q for part in column
                for q in (part, plan.send(part, lambda z, x, y, c: (z, x, y, 1 - c)))]
    grads = call(functools.partial(assemble_kernel, plan),
                 [shape((plan.shard, out_width), F32)] * 2, quarters,
                 scratch=[pltpu.VMEM((2, plan.shard, out_width), F32)])
    return hidden.astype(BF16), grads[0], grads[1]


def solution(mesh):
    in_specs = (
        P("store", None),
        P(("store", "trainer"), None),
        P("trainer", "store", None, None, None),
        P("trainer", "store", None, None),
        P(("store", "trainer"), None),
        P(),
        P(),
    )
    out_specs = (P(("store", "trainer"), None), P("store", None), P("store", None))

    def run(features, self_rows, edge_row, recv_target, cotangent, w_self, w_neigh):
        plan = Plan(mesh, features.shape[1], w_self.shape[1])
        return jax.shard_map(
            functools.partial(per_device, plan), mesh=mesh, in_specs=in_specs,
            out_specs=out_specs, check_vma=False,
        )(features, self_rows, edge_row, recv_target, cotangent, w_self, w_neigh)

    return run
```

```python
import functools

import jax
import jax.numpy as jnp
from jax import lax
from jax.experimental import pallas as pl
from jax.experimental.pallas import tpu as pltpu
from jax.sharding import PartitionSpec as P

BF16, F32 = jnp.bfloat16, jnp.float32
SLOT_PAD = 16
VMEM = pl.BlockSpec(memory_space=pltpu.VMEM)
ANY = pl.BlockSpec(memory_space=pl.ANY)
HBM = pl.BlockSpec(memory_space=pltpu.HBM)


def dot(a, b):
    return jnp.dot(a, b, preferred_element_type=F32)


def call(body, outs, args, unread=(), hbm=(), scratch=(), flops=0, vmem=16):
    moved = sum(a.size * a.dtype.itemsize for a in (*args, *outs))
    return pl.pallas_call(
        body,
        out_shape=list(outs),
        in_specs=[VMEM] * len(args) + [ANY] * len(unread) + [HBM] * len(hbm),
        out_specs=[VMEM] * len(outs),
        scratch_shapes=list(scratch),
        compiler_params=pltpu.CompilerParams(vmem_limit_bytes=vmem * 1024 * 1024),
        cost_estimate=pl.CostEstimate(flops=flops, bytes_accessed=moved, transcendentals=0),
    )(*args, *unread, *hbm)


def shape(dims, kind):
    return jax.ShapeDtypeStruct(dims, kind)


def pack_rows(cap, width):
    return cap * (width // 128) + 8


def pack(sums, counts, cap):
    blocks = sums.shape[1] // 128
    out = []
    for d in range(sums.shape[0] // SLOT_PAD):
        at = d * SLOT_PAD
        part = [sums[at:at + SLOT_PAD, j * 128:(j + 1) * 128] for j in range(blocks)]
        out += [p[:8] for p in part]
        out += [jnp.concatenate([part[j][8:cap], part[j + 1][8:cap]], axis=0) for j in range(0, blocks, 2)]
        out.append(counts[at + 8:at + SLOT_PAD])
    return jnp.concatenate(out, axis=0).astype(BF16)


def unpack(packed, order, cap, blocks):
    size = packed.shape[0] // len(order)
    rows = []
    for s in range(len(order)):
        at = order.index(s) * size
        part = packed[at:at + size, :].astype(F32)
        tail, counts = part[blocks * 8:size - 8], part[size - 8:]
        columns = []
        for j in range(blocks):
            low = tail[j // 2 * 8 + j % 2 * 4:j // 2 * 8 + j % 2 * 4 + 4]
            rest = counts[4:] if j == 0 else jnp.zeros((4, 128), F32)
            columns.append(jnp.concatenate([part[j * 8:j * 8 + 8], low, rest], axis=0))
        rows.append(jnp.concatenate(columns, axis=1))
    return jnp.concatenate(rows, axis=0).astype(BF16)


def slot_sums_kernel(plan, order, feat_hbm, edge_hbm, *rest):
    with_own = len(rest) > 4
    if with_own:
        self_hbm, out_ref, *own_refs, feat_ref, edge_ref, sems, self_ref, trans_ref = rest
    else:
        out_ref, feat_ref, edge_ref, sems = rest
    copies = [pltpu.make_async_copy(edge_hbm, edge_ref, sems.at[0]),
              pltpu.make_async_copy(feat_hbm, feat_ref, sems.at[1])]
    if with_own:
        copies.append(pltpu.make_async_copy(self_hbm, self_ref, sems.at[2]))
    for copy in copies:
        copy.start()
    owned = feat_ref.shape[0]
    _, mult, cap = edge_ref.shape
    slots = len(order) * SLOT_PAD
    copies[0].wait()
    fill = jnp.full((mult, SLOT_PAD - cap), owned, jnp.int32)
    ids = jnp.concatenate([p for d in order for p in (edge_ref[d], fill)], axis=1)
    row = lax.broadcasted_iota(jnp.int32, (owned, slots), 0)
    weight = jnp.zeros((owned, slots), F32)
    count = jnp.zeros((1, slots), F32)
    for m in range(ids.shape[0]):
        weight += (row == ids[m:m + 1, :]).astype(F32)
        count += (ids[m:m + 1, :] < owned).astype(F32)
    pick = weight.T.astype(BF16)
    r = lax.broadcasted_iota(jnp.int32, (slots, slots), 0)
    c = lax.broadcasted_iota(jnp.int32, (slots, slots), 1)
    here = ((r & (SLOT_PAD - 1)) == cap) & ((c - (c & (SLOT_PAD - 1))) == (r - (r & (SLOT_PAD - 1))))
    spread = jnp.where(here, jnp.broadcast_to(count, (slots, slots)), 0.0).astype(BF16)
    c2 = lax.broadcasted_iota(jnp.int32, (slots, 128), 0)
    l2 = lax.broadcasted_iota(jnp.int32, (slots, 128), 1)
    fold = ((c2 & (SLOT_PAD - 1)) == l2).astype(BF16)
    counts = dot(spread, fold)
    copies[1].wait()
    feat = feat_ref[...]
    high = feat.astype(BF16)
    low = (feat - high.astype(F32)).astype(BF16)
    sums = dot(pick, high) + dot(pick, low)
    out_ref[...] = pack(sums, counts, cap)
    if with_own:
        copies[2].wait()
        write_own(plan, self_ref, *own_refs, trans_ref)


def neighbor_mean(cap, rows, recv, targets):
    slots = rows.shape[0]
    target = lax.broadcasted_iota(jnp.int32, (targets, slots), 0)
    onehot = (target == recv).astype(BF16)
    r = lax.broadcasted_iota(jnp.int32, (slots, slots), 0)
    c = lax.broadcasted_iota(jnp.int32, (slots, slots), 1)
    from_count = (c == (r - (r & (SLOT_PAD - 1)) + cap)).astype(BF16)
    copied = dot(from_count, rows[:, :128])
    r2 = lax.broadcasted_iota(jnp.int32, (slots, 128), 0)
    l2 = lax.broadcasted_iota(jnp.int32, (slots, 128), 1)
    counts = jnp.where((r2 & (SLOT_PAD - 1)) == l2, copied, 0.0).astype(BF16)
    number = jnp.sum(dot(onehot, counts), axis=1, keepdims=True)
    return (dot(onehot, rows) / jnp.maximum(number, 1.0)).astype(BF16)


def forward(preact, cot):
    sig = jax.nn.sigmoid(preact)
    hidden = (preact * sig).astype(BF16)
    grad = (cot.astype(F32) * (sig * (1.0 + preact * (1.0 - sig)))).astype(BF16)
    return hidden, grad


class Plan:
    def __init__(self, mesh, width, out_width):
        self.ns, self.nt = mesh.shape["store"], mesh.shape["trainer"]
        self.gx = 2 if self.ns % 2 == 0 else 1
        self.nz = self.ns // self.gx
        self.gc = 2
        self.gy = max(self.nt // self.gc, 1)
        self.shard = width // self.ns
        self.rows = self.nz * self.shard
        self.cols = out_width // self.gy
        self.peers = [(dx, dy) for dx in range(self.gx) for dy in range(self.gy)]

    def fits(self):
        pow2 = all((n & (n - 1)) == 0 for n in (self.ns, self.nt))
        return (pow2 and self.ns <= 8 and self.gx == 2 and self.gy == 2 and self.gy * self.gc == self.nt and self.cols % 128 == 0
                and self.shard % 16 == 0 and len(self.peers) <= 4 and self.nz == 4)

    def place(self):
        s, t = lax.axis_index("store"), lax.axis_index("trainer")
        return s // self.gx, s % self.gx, t // self.gc, t % self.gc

    def far(self):
        return list(range(2, self.nz))

    def near(self):
        return list(range(min(2, self.nz)))[::-1]

    def send(self, array, to):
        pairs = []
        for s in range(self.ns):
            for t in range(self.nt):
                z, x, y, c = to(s // self.gx, s % self.gx, t // self.gc, t % self.gc)
                pairs.append((s * self.nt + t, (z * self.gx + x) * self.nt + y * self.gc + c))
        return lax.ppermute(array, ("store", "trainer"), pairs)

    def store_order(self):
        up = [(z, x) for z in reversed(range(self.nz)) for x in reversed(range(self.gx))]
        down = [(z, x) for z in range(self.nz) for x in range(self.gx)]
        turns = [at for pair in zip(up, down) for at in pair]
        return [z * self.gx + x for z, x in turns[:self.ns]]


def write_rows(plan, trans_ref, *outs):
    x = plan.place()[1]
    for dx, out in enumerate(outs):
        for z in range(plan.nz):
            start = pl.multiple_of((z * plan.gx + (x ^ dx)) * plan.shard, 16)
            out[z * plan.shard:(z + 1) * plan.shard, :] = trans_ref[pl.ds(start, plan.shard), :]


def write_own(plan, self_ref, own_ref, here_ref, there_ref, trans_ref):
    own_ref[...] = self_ref[...].astype(BF16)
    trans_ref[...] = self_ref[...].T.astype(BF16)
    write_rows(plan, trans_ref, here_ref, there_ref)


def layer_kernel(plan, cap, order, rows_ref, recv_ref, self_ref, cot_ref, w_ref, hidden_ref, mean_here, mean_there,
                 grad_here, grad_there, trans_ref, grad_ref):
    targets = self_ref.shape[0]
    rows = unpack(rows_ref[...], order, cap, hidden_ref.shape[1] // 128)
    fill = jnp.full((1, SLOT_PAD - cap), targets, jnp.int32)
    recv = jnp.concatenate([p for s in range(plan.ns) for p in (recv_ref[s:s + 1, :], fill)], axis=1)
    mean = neighbor_mean(cap, rows, recv, targets)
    preact = self_ref[...] + dot(mean, w_ref[...])
    trans_ref[...] = mean.astype(F32).T.astype(BF16)
    write_rows(plan, trans_ref, mean_here, mean_there)
    hidden, grad = forward(preact, cot_ref[...])
    hidden_ref[...] = hidden.astype(F32)
    for b in range(grad_ref.shape[0]):
        grad_ref[b] = grad[:, b * 128:(b + 1) * 128]
    y, each = plan.place()[2], plan.cols // 128
    for dy, out in enumerate((grad_here, grad_there)):
        for b in range(each):
            out[b * targets:(b + 1) * targets, :] = grad_ref[(y ^ dy) * each + b]


def left_kernel(plan, *refs):
    n = len(plan.peers)
    own, mean, outs = refs[n - 1::-1], refs[n:2 * n], refs[2 * n:]
    targets = own[0].shape[1]
    z, _, _, c = plan.place()
    keep_own = c == 0
    for i, (o, m) in enumerate(zip(own, mean)):
        at = slice(i * targets, (i + 1) * targets)
        for j, shards in enumerate((plan.far(), plan.near())):
            for r, k in enumerate(shards):
                rows = pl.ds(pl.multiple_of((z ^ k) * plan.shard, 16), plan.shard)
                to = slice(r * plan.shard, (r + 1) * plan.shard)
                outs[j][to, at] = jnp.where(keep_own, m[rows, :], o[rows, :])
                outs[2 + j][to, at] = jnp.where(keep_own, o[rows, :], m[rows, :])


def terms_kernel(left_ref, *refs):
    grad, out_ref = refs[:-1], refs[-1]
    targets = left_ref.shape[1] // len(grad)
    right = jnp.concatenate(
        [jnp.concatenate([g[b * targets:(b + 1) * targets, :] for b in range(grad[0].shape[0] // targets)], axis=1)
         for g in grad], axis=0)
    out_ref[...] = dot(left_ref[...], right).astype(out_ref.dtype)


def core_sum_kernel(plan, keep_ref, got_ref, *outs):
    for r, out in enumerate(outs):
        at = slice(r * plan.shard, (r + 1) * plan.shard)
        out[...] = (keep_ref[at, :] + got_ref[at, :].astype(F32)).astype(out.dtype)


def store_sum_kernel(*refs):
    total = refs[0][...]
    for r in refs[1:-1]:
        total += r[...].astype(F32)
    refs[-1][...] = total.astype(BF16)


def assemble_kernel(plan, *refs):
    parts, (self_ref, neigh_ref, both_ref) = refs[:-3], refs[-3:]
    _, _, y, c = plan.place()
    for i, part in enumerate(parts):
        cols = pl.ds(pl.multiple_of((y ^ (i // plan.gc)) * plan.cols, 128), plan.cols)
        both_ref[c ^ (i % plan.gc), :, cols] = part[...].astype(F32)
    self_ref[...] = both_ref[0]
    neigh_ref[...] = both_ref[1]


def per_device(plan, features, self_rows, edge_row, recv_target, cotangent, w_self, w_neigh):
    owned, width = features.shape
    out_width = w_self.shape[1]
    targets = self_rows.shape[0]
    ns, cap, mult = edge_row.shape[2:]
    slots = ns * SLOT_PAD
    edges = edge_row[0, 0].transpose(0, 2, 1)
    fits = plan.fits()
    order = plan.store_order() if fits else list(range(ns))
    rows, cols, n = plan.rows, plan.cols, len(plan.peers)
    scratch = [pltpu.VMEM(features.shape, F32), pltpu.VMEM(edges.shape, jnp.int32),
               pltpu.SemaphoreType.DMA((3,))]
    packed = pack_rows(cap, width)
    outs, more = [shape((ns * packed, 128), BF16)], []
    if fits:
        outs += [shape((targets, width), BF16)] + [shape((rows, targets), BF16)] * 2
        more = [self_rows]
        scratch += [pltpu.VMEM(self_rows.shape, F32), pltpu.VMEM((width, targets), BF16)]
    sums, *owns = call(
        functools.partial(slot_sums_kernel, plan, order), outs, (), hbm=[features, edges] + more,
        flops=4 * slots * owned * width, vmem=60 if fits else 16, scratch=scratch)
    arrived = lax.all_to_all(sums.reshape(ns, packed, 128), "store", split_axis=0, concat_axis=0,
                             tiled=True, axis_index_groups=[order]).reshape(ns * packed, 128)
    if not fits:
        own = self_rows.astype(BF16)
        recv = jnp.pad(recv_target[0, 0], ((0, 0), (0, SLOT_PAD - cap)), constant_values=targets).reshape(1, slots)
        mean = neighbor_mean(cap, unpack(arrived, order, cap, width // 128), recv, targets)
        preact = dot(own, w_self) + dot(mean, w_neigh)
        hidden, grad = forward(preact, cotangent)
        both = jnp.concatenate([own.T.reshape(ns, -1, targets), mean.T.reshape(ns, -1, targets)], axis=1)
        terms = dot(both.reshape(2 * width, targets), grad)
        part = lax.psum_scatter(terms, "store", scatter_dimension=0, tiled=True)
        total = lax.psum(part, "trainer")
        return hidden, total[:plan.shard], total[plan.shard:]

    def to_x(array):
        return plan.send(array, lambda z, x, y, c: (z, 1 - x, y, c))

    def to_y(array):
        return plan.send(array, lambda z, x, y, c: (z, x, 1 - y, c))

    def to_diagonal(array):
        return plan.send(array, lambda z, x, y, c: (z, 1 - x, 1 - y, c))

    def held(array, *until):
        return lax.optimization_barrier((array,) + until)[0]

    own, own_here, own_there = owns
    own_all = [own_here, to_y(own_here), to_x(own_there), to_diagonal(own_there)]
    self_term = dot(own, w_self)

    hidden, mean_here, mean_there, grad_here, grad_there = call(
        functools.partial(layer_kernel, plan, cap, order),
        [shape((targets, out_width), F32)] + [shape((rows, targets), BF16)] * 2
        + [shape((cols // 128 * targets, 128), BF16)] * 2,
        [arrived, recv_target[0, 0], self_term, cotangent, w_neigh],
        scratch=[pltpu.VMEM((width, targets), BF16), pltpu.VMEM((out_width // 128, targets, 128), BF16)],
        flops=2 * targets * width * (out_width + slots))
    mean_x, grad_y = to_x(mean_there), to_y(grad_there)
    grad_x = to_x(grad_here)
    mean_all = [mean_here, to_y(mean_here), mean_x, to_y(held(mean_x, *own_all[1:]))]
    grad_all = [grad_here, grad_y, grad_x, to_x(held(grad_y, mean_x, *own_all[1:]))]
    def to_core(array):
        return plan.send(array, lambda z, x, y, c: (z, x, y, 1 - c))

    def to_z(array, k):
        return plan.send(array, lambda z, x, y, c: (z ^ k, x, y, c))

    def terms(left, kind):
        return call(terms_kernel, [shape((left.shape[0], cols), kind)], [left] + grad_all,
                    flops=2 * left.shape[0] * cols * targets * n)[0]

    block = (plan.shard, cols)
    halves = [plan.far(), plan.near()]
    lefts = call(functools.partial(left_kernel, plan),
                 [shape((len(half) * plan.shard, n * targets), BF16) for half in halves * 2],
                 own_all[::-1] + mean_all)
    got, mine = [], None
    for half, give_left, keep_left in zip(halves, lefts[:2], lefts[2:]):
        came = to_core(terms(give_left, BF16))
        sums = call(functools.partial(core_sum_kernel, plan),
                    [shape(block, BF16 if k else F32) for k in half], [terms(keep_left, F32), came])
        for k, part in zip(half, sums):
            if k:
                got.append(to_z(part, k))
            else:
                mine = part
    (quarter,) = call(store_sum_kernel, [shape(block, BF16)], [mine] + got)
    column = [quarter] + [plan.send(quarter, lambda z, x, y, c, i=i: (z, x, y ^ i, c))
                          for i in range(1, plan.gy)]
    quarters = [q for part in column
                for q in (part, plan.send(part, lambda z, x, y, c: (z, x, y, 1 - c)))]
    grads = call(functools.partial(assemble_kernel, plan),
                 [shape((plan.shard, out_width), F32)] * 2, quarters,
                 scratch=[pltpu.VMEM((2, plan.shard, out_width), F32)])
    return hidden.astype(BF16), grads[0], grads[1]


def solution(mesh):
    in_specs = (
        P("store", None),
        P(("store", "trainer"), None),
        P("trainer", "store", None, None, None),
        P("trainer", "store", None, None),
        P(("store", "trainer"), None),
        P(),
        P(),
    )
    out_specs = (P(("store", "trainer"), None), P("store", None), P("store", None))

    def run(features, self_rows, edge_row, recv_target, cotangent, w_self, w_neigh):
        plan = Plan(mesh, features.shape[1], w_self.shape[1])
        return jax.shard_map(
            functools.partial(per_device, plan), mesh=mesh, in_specs=in_specs,
            out_specs=out_specs, check_vma=False,
        )(features, self_rows, edge_row, recv_target, cotangent, w_self, w_neigh)

    return run
```

```python
import functools

import jax
import jax.numpy as jnp
from jax import lax
from jax.experimental import pallas as pl
from jax.experimental.pallas import tpu as pltpu
from jax.sharding import PartitionSpec as P

BF16, F32 = jnp.bfloat16, jnp.float32
SLOT_PAD = 16
VMEM = pl.BlockSpec(memory_space=pltpu.VMEM)
ANY = pl.BlockSpec(memory_space=pl.ANY)
HBM = pl.BlockSpec(memory_space=pltpu.HBM)


def dot(a, b):
    return jnp.dot(a, b, preferred_element_type=F32)


def call(body, outs, args, unread=(), hbm=(), scratch=(), flops=0, vmem=16):
    moved = sum(a.size * a.dtype.itemsize for a in (*args, *outs))
    return pl.pallas_call(
        body,
        out_shape=list(outs),
        in_specs=[VMEM] * len(args) + [ANY] * len(unread) + [HBM] * len(hbm),
        out_specs=[VMEM] * len(outs),
        scratch_shapes=list(scratch),
        compiler_params=pltpu.CompilerParams(vmem_limit_bytes=vmem * 1024 * 1024),
        cost_estimate=pl.CostEstimate(flops=flops, bytes_accessed=moved, transcendentals=0),
    )(*args, *unread, *hbm)


def shape(dims, kind):
    return jax.ShapeDtypeStruct(dims, kind)


def pack_rows(cap, width):
    return cap * (width // 128) + 8


def pack(sums, counts, cap):
    blocks = sums.shape[1] // 128
    out = []
    for d in range(sums.shape[0] // SLOT_PAD):
        at = d * SLOT_PAD
        part = [sums[at:at + SLOT_PAD, j * 128:(j + 1) * 128] for j in range(blocks)]
        out += [p[:8] for p in part]
        out += [jnp.concatenate([part[j][8:cap], part[j + 1][8:cap]], axis=0) for j in range(0, blocks, 2)]
        out.append(counts[at + 8:at + SLOT_PAD])
    return jnp.concatenate(out, axis=0).astype(BF16)


def unpack(packed, order, cap, blocks):
    size = packed.shape[0] // len(order)
    rows = []
    for s in range(len(order)):
        at = order.index(s) * size
        part = packed[at:at + size, :].astype(F32)
        tail, counts = part[blocks * 8:size - 8], part[size - 8:]
        columns = []
        for j in range(blocks):
            low = tail[j // 2 * 8 + j % 2 * 4:j // 2 * 8 + j % 2 * 4 + 4]
            rest = counts[4:] if j == 0 else jnp.zeros((4, 128), F32)
            columns.append(jnp.concatenate([part[j * 8:j * 8 + 8], low, rest], axis=0))
        rows.append(jnp.concatenate(columns, axis=1))
    return jnp.concatenate(rows, axis=0).astype(BF16)


def slot_sums_kernel(plan, order, feat_hbm, edge_hbm, *rest):
    with_own = len(rest) > 4
    if with_own:
        self_hbm, out_ref, *own_refs, feat_ref, edge_ref, sems, self_ref, trans_ref = rest
    else:
        out_ref, feat_ref, edge_ref, sems = rest
    copies = [pltpu.make_async_copy(edge_hbm, edge_ref, sems.at[0]),
              pltpu.make_async_copy(feat_hbm, feat_ref, sems.at[1])]
    if with_own:
        copies.append(pltpu.make_async_copy(self_hbm, self_ref, sems.at[2]))
    for copy in copies:
        copy.start()
    owned = feat_ref.shape[0]
    _, mult, cap = edge_ref.shape
    slots = len(order) * SLOT_PAD
    copies[0].wait()
    fill = jnp.full((mult, SLOT_PAD - cap), owned, jnp.int32)
    ids = jnp.concatenate([p for d in order for p in (edge_ref[d], fill)], axis=1)
    row = lax.broadcasted_iota(jnp.int32, (owned, slots), 0)
    weight = jnp.zeros((owned, slots), F32)
    count = jnp.zeros((1, slots), F32)
    for m in range(ids.shape[0]):
        weight += (row == ids[m:m + 1, :]).astype(F32)
        count += (ids[m:m + 1, :] < owned).astype(F32)
    pick = weight.T.astype(BF16)
    r = lax.broadcasted_iota(jnp.int32, (slots, slots), 0)
    c = lax.broadcasted_iota(jnp.int32, (slots, slots), 1)
    here = ((r & (SLOT_PAD - 1)) == cap) & ((c - (c & (SLOT_PAD - 1))) == (r - (r & (SLOT_PAD - 1))))
    spread = jnp.where(here, jnp.broadcast_to(count, (slots, slots)), 0.0).astype(BF16)
    c2 = lax.broadcasted_iota(jnp.int32, (slots, 128), 0)
    l2 = lax.broadcasted_iota(jnp.int32, (slots, 128), 1)
    fold = ((c2 & (SLOT_PAD - 1)) == l2).astype(BF16)
    counts = dot(spread, fold)
    copies[1].wait()
    feat = feat_ref[...]
    high = feat.astype(BF16)
    low = (feat - high.astype(F32)).astype(BF16)
    sums = dot(pick, high) + dot(pick, low)
    out_ref[...] = pack(sums, counts, cap)
    if with_own:
        copies[2].wait()
        write_own(plan, self_ref, *own_refs, trans_ref)


def neighbor_mean(cap, rows, recv, targets):
    slots = rows.shape[0]
    target = lax.broadcasted_iota(jnp.int32, (targets, slots), 0)
    onehot = (target == recv).astype(BF16)
    r = lax.broadcasted_iota(jnp.int32, (slots, slots), 0)
    c = lax.broadcasted_iota(jnp.int32, (slots, slots), 1)
    from_count = (c == (r - (r & (SLOT_PAD - 1)) + cap)).astype(BF16)
    copied = dot(from_count, rows[:, :128])
    r2 = lax.broadcasted_iota(jnp.int32, (slots, 128), 0)
    l2 = lax.broadcasted_iota(jnp.int32, (slots, 128), 1)
    counts = jnp.where((r2 & (SLOT_PAD - 1)) == l2, copied, 0.0).astype(BF16)
    number = jnp.sum(dot(onehot, counts), axis=1, keepdims=True)
    return (dot(onehot, rows) / jnp.maximum(number, 1.0)).astype(BF16)


def forward(preact, cot):
    sig = jax.nn.sigmoid(preact)
    hidden = (preact * sig).astype(BF16)
    grad = (cot.astype(F32) * (sig * (1.0 + preact * (1.0 - sig)))).astype(BF16)
    return hidden, grad


class Plan:
    def __init__(self, mesh, width, out_width):
        self.ns, self.nt = mesh.shape["store"], mesh.shape["trainer"]
        self.gx = 2 if self.ns % 2 == 0 else 1
        self.nz = self.ns // self.gx
        self.gc = 2
        self.gy = max(self.nt // self.gc, 1)
        self.shard = width // self.ns
        self.rows = self.nz * self.shard
        self.cols = out_width // self.gy
        self.peers = [(dx, dy) for dx in range(self.gx) for dy in range(self.gy)]

    def fits(self):
        pow2 = all((n & (n - 1)) == 0 for n in (self.ns, self.nt))
        return (pow2 and self.ns <= 8 and self.gx == 2 and self.gy == 2 and self.gy * self.gc == self.nt and self.cols % 128 == 0
                and self.shard % 16 == 0 and len(self.peers) <= 4 and self.nz == 4)

    def place(self):
        s, t = lax.axis_index("store"), lax.axis_index("trainer")
        return s // self.gx, s % self.gx, t // self.gc, t % self.gc

    def far(self):
        return list(range(2, self.nz))

    def near(self):
        return list(range(min(2, self.nz)))[::-1]

    def send(self, array, to):
        pairs = []
        for s in range(self.ns):
            for t in range(self.nt):
                z, x, y, c = to(s // self.gx, s % self.gx, t // self.gc, t % self.gc)
                pairs.append((s * self.nt + t, (z * self.gx + x) * self.nt + y * self.gc + c))
        return lax.ppermute(array, ("store", "trainer"), pairs)

    def store_order(self):
        up = [(z, x) for z in reversed(range(self.nz)) for x in reversed(range(self.gx))]
        down = [(z, x) for z in range(self.nz) for x in range(self.gx)]
        turns = [at for pair in zip(up, down) for at in pair]
        return [z * self.gx + x for z, x in turns[:self.ns]][::-1]


def write_rows(plan, trans_ref, *outs):
    x = plan.place()[1]
    for dx, out in enumerate(outs):
        for z in range(plan.nz):
            start = pl.multiple_of((z * plan.gx + (x ^ dx)) * plan.shard, 16)
            out[z * plan.shard:(z + 1) * plan.shard, :] = trans_ref[pl.ds(start, plan.shard), :]


def write_own(plan, self_ref, own_ref, here_ref, there_ref, trans_ref):
    own_ref[...] = self_ref[...].astype(BF16)
    trans_ref[...] = self_ref[...].T.astype(BF16)
    write_rows(plan, trans_ref, here_ref, there_ref)


def layer_kernel(plan, cap, order, rows_ref, recv_ref, self_ref, cot_ref, w_ref, hidden_ref, mean_here, mean_there,
                 grad_here, grad_there, trans_ref, grad_ref):
    targets = self_ref.shape[0]
    rows = unpack(rows_ref[...], order, cap, hidden_ref.shape[1] // 128)
    fill = jnp.full((1, SLOT_PAD - cap), targets, jnp.int32)
    recv = jnp.concatenate([p for s in range(plan.ns) for p in (recv_ref[s:s + 1, :], fill)], axis=1)
    mean = neighbor_mean(cap, rows, recv, targets)
    preact = self_ref[...] + dot(mean, w_ref[...])
    trans_ref[...] = mean.astype(F32).T.astype(BF16)
    write_rows(plan, trans_ref, mean_here, mean_there)
    hidden, grad = forward(preact, cot_ref[...])
    hidden_ref[...] = hidden.astype(F32)
    for b in range(grad_ref.shape[0]):
        grad_ref[b] = grad[:, b * 128:(b + 1) * 128]
    y, each = plan.place()[2], plan.cols // 128
    for dy, out in enumerate((grad_here, grad_there)):
        for b in range(each):
            out[b * targets:(b + 1) * targets, :] = grad_ref[(y ^ dy) * each + b]


def left_kernel(plan, *refs):
    n = len(plan.peers)
    own, mean, outs = refs[n - 1::-1], refs[n:2 * n], refs[2 * n:]
    targets = own[0].shape[1]
    z, _, _, c = plan.place()
    keep_own = c == 0
    for i, (o, m) in enumerate(zip(own, mean)):
        at = slice(i * targets, (i + 1) * targets)
        for j, shards in enumerate((plan.far(), plan.near())):
            for r, k in enumerate(shards):
                rows = pl.ds(pl.multiple_of((z ^ k) * plan.shard, 16), plan.shard)
                to = slice(r * plan.shard, (r + 1) * plan.shard)
                outs[j][to, at] = jnp.where(keep_own, m[rows, :], o[rows, :])
                outs[2 + j][to, at] = jnp.where(keep_own, o[rows, :], m[rows, :])


def terms_kernel(left_ref, *refs):
    grad, out_ref = refs[:-1], refs[-1]
    targets = left_ref.shape[1] // len(grad)
    right = jnp.concatenate(
        [jnp.concatenate([g[b * targets:(b + 1) * targets, :] for b in range(grad[0].shape[0] // targets)], axis=1)
         for g in grad], axis=0)
    out_ref[...] = dot(left_ref[...], right).astype(out_ref.dtype)


def core_sum_kernel(plan, keep_ref, got_ref, *outs):
    for r, out in enumerate(outs):
        at = slice(r * plan.shard, (r + 1) * plan.shard)
        out[...] = (keep_ref[at, :] + got_ref[at, :].astype(F32)).astype(out.dtype)


def store_sum_kernel(*refs):
    total = refs[0][...]
    for r in refs[1:-1]:
        total += r[...].astype(F32)
    refs[-1][...] = total.astype(BF16)


def assemble_kernel(plan, *refs):
    parts, (self_ref, neigh_ref, both_ref) = refs[:-3], refs[-3:]
    _, _, y, c = plan.place()
    for i, part in enumerate(parts):
        cols = pl.ds(pl.multiple_of((y ^ (i // plan.gc)) * plan.cols, 128), plan.cols)
        both_ref[c ^ (i % plan.gc), :, cols] = part[...].astype(F32)
    self_ref[...] = both_ref[0]
    neigh_ref[...] = both_ref[1]


def per_device(plan, features, self_rows, edge_row, recv_target, cotangent, w_self, w_neigh):
    owned, width = features.shape
    out_width = w_self.shape[1]
    targets = self_rows.shape[0]
    ns, cap, mult = edge_row.shape[2:]
    slots = ns * SLOT_PAD
    edges = edge_row[0, 0].transpose(0, 2, 1)
    fits = plan.fits()
    order = plan.store_order() if fits else list(range(ns))
    rows, cols, n = plan.rows, plan.cols, len(plan.peers)
    scratch = [pltpu.VMEM(features.shape, F32), pltpu.VMEM(edges.shape, jnp.int32),
               pltpu.SemaphoreType.DMA((3,))]
    packed = pack_rows(cap, width)
    outs, more = [shape((ns * packed, 128), BF16)], []
    if fits:
        outs += [shape((targets, width), BF16)] + [shape((rows, targets), BF16)] * 2
        more = [self_rows]
        scratch += [pltpu.VMEM(self_rows.shape, F32), pltpu.VMEM((width, targets), BF16)]
    sums, *owns = call(
        functools.partial(slot_sums_kernel, plan, order), outs, (), hbm=[features, edges] + more,
        flops=4 * slots * owned * width, vmem=60 if fits else 16, scratch=scratch)
    arrived = lax.all_to_all(sums.reshape(ns, packed, 128), "store", split_axis=0, concat_axis=0,
                             tiled=True, axis_index_groups=[order]).reshape(ns * packed, 128)
    if not fits:
        own = self_rows.astype(BF16)
        recv = jnp.pad(recv_target[0, 0], ((0, 0), (0, SLOT_PAD - cap)), constant_values=targets).reshape(1, slots)
        mean = neighbor_mean(cap, unpack(arrived, order, cap, width // 128), recv, targets)
        preact = dot(own, w_self) + dot(mean, w_neigh)
        hidden, grad = forward(preact, cotangent)
        both = jnp.concatenate([own.T.reshape(ns, -1, targets), mean.T.reshape(ns, -1, targets)], axis=1)
        terms = dot(both.reshape(2 * width, targets), grad)
        part = lax.psum_scatter(terms, "store", scatter_dimension=0, tiled=True)
        total = lax.psum(part, "trainer")
        return hidden, total[:plan.shard], total[plan.shard:]

    def to_x(array):
        return plan.send(array, lambda z, x, y, c: (z, 1 - x, y, c))

    def to_y(array):
        return plan.send(array, lambda z, x, y, c: (z, x, 1 - y, c))

    def to_diagonal(array):
        return plan.send(array, lambda z, x, y, c: (z, 1 - x, 1 - y, c))

    def held(array, *until):
        return lax.optimization_barrier((array,) + until)[0]

    own, own_here, own_there = owns
    own_all = [own_here, to_y(own_here), to_x(own_there), to_diagonal(own_there)]
    self_term = dot(own, w_self)

    hidden, mean_here, mean_there, grad_here, grad_there = call(
        functools.partial(layer_kernel, plan, cap, order),
        [shape((targets, out_width), F32)] + [shape((rows, targets), BF16)] * 2
        + [shape((cols // 128 * targets, 128), BF16)] * 2,
        [arrived, recv_target[0, 0], self_term, cotangent, w_neigh],
        scratch=[pltpu.VMEM((width, targets), BF16), pltpu.VMEM((out_width // 128, targets, 128), BF16)],
        flops=2 * targets * width * (out_width + slots))
    mean_x, grad_y = to_x(mean_there), to_y(grad_there)
    grad_x = to_x(grad_here)
    mean_all = [mean_here, to_y(mean_here), mean_x, to_y(held(mean_x, *own_all[1:]))]
    grad_all = [grad_here, grad_y, grad_x, to_x(held(grad_y, mean_x, *own_all[1:]))]
    def to_core(array):
        return plan.send(array, lambda z, x, y, c: (z, x, y, 1 - c))

    def to_z(array, k):
        return plan.send(array, lambda z, x, y, c: (z ^ k, x, y, c))

    def terms(left, kind):
        return call(terms_kernel, [shape((left.shape[0], cols), kind)], [left] + grad_all,
                    flops=2 * left.shape[0] * cols * targets * n)[0]

    block = (plan.shard, cols)
    halves = [plan.far(), plan.near()]
    lefts = call(functools.partial(left_kernel, plan),
                 [shape((len(half) * plan.shard, n * targets), BF16) for half in halves * 2],
                 own_all[::-1] + mean_all)
    got, mine = [], None
    for half, give_left, keep_left in zip(halves, lefts[:2], lefts[2:]):
        came = to_core(terms(give_left, BF16))
        sums = call(functools.partial(core_sum_kernel, plan),
                    [shape(block, BF16 if k else F32) for k in half], [terms(keep_left, F32), came])
        for k, part in zip(half, sums):
            if k:
                got.append(to_z(part, k))
            else:
                mine = part
    (quarter,) = call(store_sum_kernel, [shape(block, BF16)], [mine] + got)
    column = [quarter] + [plan.send(quarter, lambda z, x, y, c, i=i: (z, x, y ^ i, c))
                          for i in range(1, plan.gy)]
    quarters = [q for part in column
                for q in (part, plan.send(part, lambda z, x, y, c: (z, x, y, 1 - c)))]
    grads = call(functools.partial(assemble_kernel, plan),
                 [shape((plan.shard, out_width), F32)] * 2, quarters,
                 scratch=[pltpu.VMEM((2, plan.shard, out_width), F32)])
    return hidden.astype(BF16), grads[0], grads[1]


def solution(mesh):
    in_specs = (
        P("store", None),
        P(("store", "trainer"), None),
        P("trainer", "store", None, None, None),
        P("trainer", "store", None, None),
        P(("store", "trainer"), None),
        P(),
        P(),
    )
    out_specs = (P(("store", "trainer"), None), P("store", None), P("store", None))

    def run(features, self_rows, edge_row, recv_target, cotangent, w_self, w_neigh):
        plan = Plan(mesh, features.shape[1], w_self.shape[1])
        return jax.shard_map(
            functools.partial(per_device, plan), mesh=mesh, in_specs=in_specs,
            out_specs=out_specs, check_vma=False,
        )(features, self_rows, edge_row, recv_target, cotangent, w_self, w_neigh)

    return run
```

```python
import functools

import jax
import jax.numpy as jnp
from jax import lax
from jax.experimental import pallas as pl
from jax.experimental.pallas import tpu as pltpu
from jax.sharding import PartitionSpec as P

BF16, F32 = jnp.bfloat16, jnp.float32
SLOT_PAD = 16
VMEM = pl.BlockSpec(memory_space=pltpu.VMEM)
ANY = pl.BlockSpec(memory_space=pl.ANY)
HBM = pl.BlockSpec(memory_space=pltpu.HBM)


def dot(a, b):
    return jnp.dot(a, b, preferred_element_type=F32)


def call(body, outs, args, unread=(), hbm=(), scratch=(), flops=0, vmem=16):
    moved = sum(a.size * a.dtype.itemsize for a in (*args, *outs))
    return pl.pallas_call(
        body,
        out_shape=list(outs),
        in_specs=[VMEM] * len(args) + [ANY] * len(unread) + [HBM] * len(hbm),
        out_specs=[VMEM] * len(outs),
        scratch_shapes=list(scratch),
        compiler_params=pltpu.CompilerParams(vmem_limit_bytes=vmem * 1024 * 1024),
        cost_estimate=pl.CostEstimate(flops=flops, bytes_accessed=moved, transcendentals=0),
    )(*args, *unread, *hbm)


def shape(dims, kind):
    return jax.ShapeDtypeStruct(dims, kind)


def pack_rows(cap, width):
    return cap * (width // 128) + 8


def pack(sums, counts, cap):
    blocks = sums.shape[1] // 128
    out = []
    for d in range(sums.shape[0] // SLOT_PAD):
        at = d * SLOT_PAD
        part = [sums[at:at + SLOT_PAD, j * 128:(j + 1) * 128] for j in range(blocks)]
        out += [p[:8] for p in part]
        out += [jnp.concatenate([part[j][8:cap], part[j + 1][8:cap]], axis=0) for j in range(0, blocks, 2)]
        out.append(counts[at + 8:at + SLOT_PAD])
    return jnp.concatenate(out, axis=0).astype(BF16)


def unpack(packed, order, cap, blocks):
    size = packed.shape[0] // len(order)
    rows = []
    for s in range(len(order)):
        at = order.index(s) * size
        part = packed[at:at + size, :].astype(F32)
        tail, counts = part[blocks * 8:size - 8], part[size - 8:]
        columns = []
        for j in range(blocks):
            low = tail[j // 2 * 8 + j % 2 * 4:j // 2 * 8 + j % 2 * 4 + 4]
            rest = counts[4:] if j == 0 else jnp.zeros((4, 128), F32)
            columns.append(jnp.concatenate([part[j * 8:j * 8 + 8], low, rest], axis=0))
        rows.append(jnp.concatenate(columns, axis=1))
    return jnp.concatenate(rows, axis=0).astype(BF16)


def slot_sums_kernel(plan, order, feat_hbm, edge_hbm, *rest):
    with_own = len(rest) > 4
    if with_own:
        self_hbm, out_ref, *own_refs, feat_ref, edge_ref, sems, self_ref, trans_ref = rest
    else:
        out_ref, feat_ref, edge_ref, sems = rest
    copies = [pltpu.make_async_copy(edge_hbm, edge_ref, sems.at[0]),
              pltpu.make_async_copy(feat_hbm, feat_ref, sems.at[1])]
    if with_own:
        copies.append(pltpu.make_async_copy(self_hbm, self_ref, sems.at[2]))
    for copy in copies:
        copy.start()
    owned = feat_ref.shape[0]
    _, mult, cap = edge_ref.shape
    slots = len(order) * SLOT_PAD
    copies[0].wait()
    fill = jnp.full((mult, SLOT_PAD - cap), owned, jnp.int32)
    ids = jnp.concatenate([p for d in order for p in (edge_ref[d], fill)], axis=1)
    row = lax.broadcasted_iota(jnp.int32, (owned, slots), 0)
    weight = jnp.zeros((owned, slots), F32)
    count = jnp.zeros((1, slots), F32)
    for m in range(ids.shape[0]):
        weight += (row == ids[m:m + 1, :]).astype(F32)
        count += (ids[m:m + 1, :] < owned).astype(F32)
    pick = weight.T.astype(BF16)
    r = lax.broadcasted_iota(jnp.int32, (slots, slots), 0)
    c = lax.broadcasted_iota(jnp.int32, (slots, slots), 1)
    here = ((r & (SLOT_PAD - 1)) == cap) & ((c - (c & (SLOT_PAD - 1))) == (r - (r & (SLOT_PAD - 1))))
    spread = jnp.where(here, jnp.broadcast_to(count, (slots, slots)), 0.0).astype(BF16)
    c2 = lax.broadcasted_iota(jnp.int32, (slots, 128), 0)
    l2 = lax.broadcasted_iota(jnp.int32, (slots, 128), 1)
    fold = ((c2 & (SLOT_PAD - 1)) == l2).astype(BF16)
    counts = dot(spread, fold)
    copies[1].wait()
    feat = feat_ref[...]
    high = feat.astype(BF16)
    low = (feat - high.astype(F32)).astype(BF16)
    sums = dot(pick, high) + dot(pick, low)
    out_ref[...] = pack(sums, counts, cap)
    if with_own:
        copies[2].wait()
        write_own(plan, self_ref, *own_refs, trans_ref)


def neighbor_mean(cap, rows, recv, targets):
    slots = rows.shape[0]
    target = lax.broadcasted_iota(jnp.int32, (targets, slots), 0)
    onehot = (target == recv).astype(BF16)
    r = lax.broadcasted_iota(jnp.int32, (slots, slots), 0)
    c = lax.broadcasted_iota(jnp.int32, (slots, slots), 1)
    from_count = (c == (r - (r & (SLOT_PAD - 1)) + cap)).astype(BF16)
    copied = dot(from_count, rows[:, :128])
    r2 = lax.broadcasted_iota(jnp.int32, (slots, 128), 0)
    l2 = lax.broadcasted_iota(jnp.int32, (slots, 128), 1)
    counts = jnp.where((r2 & (SLOT_PAD - 1)) == l2, copied, 0.0).astype(BF16)
    number = jnp.sum(dot(onehot, counts), axis=1, keepdims=True)
    return (dot(onehot, rows) / jnp.maximum(number, 1.0)).astype(BF16)


def forward(preact, cot):
    sig = jax.nn.sigmoid(preact)
    hidden = (preact * sig).astype(BF16)
    grad = (cot.astype(F32) * (sig * (1.0 + preact * (1.0 - sig)))).astype(BF16)
    return hidden, grad


class Plan:
    def __init__(self, mesh, width, out_width):
        self.ns, self.nt = mesh.shape["store"], mesh.shape["trainer"]
        self.gx = 2 if self.ns % 2 == 0 else 1
        self.nz = self.ns // self.gx
        self.gc = 2
        self.gy = max(self.nt // self.gc, 1)
        self.shard = width // self.ns
        self.rows = self.nz * self.shard
        self.cols = out_width // self.gy
        self.peers = [(dx, dy) for dx in range(self.gx) for dy in range(self.gy)]

    def fits(self):
        pow2 = all((n & (n - 1)) == 0 for n in (self.ns, self.nt))
        return (pow2 and self.ns <= 8 and self.gx == 2 and self.gy == 2 and self.gy * self.gc == self.nt and self.cols % 128 == 0
                and self.shard % 16 == 0 and len(self.peers) <= 4 and self.nz == 4)

    def place(self):
        s, t = lax.axis_index("store"), lax.axis_index("trainer")
        return s // self.gx, s % self.gx, t // self.gc, t % self.gc

    def far(self):
        return list(range(2, self.nz))

    def near(self):
        return list(range(min(2, self.nz)))[::-1]

    def send(self, array, to):
        pairs = []
        for s in range(self.ns):
            for t in range(self.nt):
                z, x, y, c = to(s // self.gx, s % self.gx, t // self.gc, t % self.gc)
                pairs.append((s * self.nt + t, (z * self.gx + x) * self.nt + y * self.gc + c))
        return lax.ppermute(array, ("store", "trainer"), pairs)

    def store_order(self):
        middle = self.ns // 2
        turns = [s for pair in zip(range(middle, self.ns), range(middle - 1, -1, -1)) for s in pair]
        return turns


def write_rows(plan, trans_ref, *outs):
    x = plan.place()[1]
    for dx, out in enumerate(outs):
        for z in range(plan.nz):
            start = pl.multiple_of((z * plan.gx + (x ^ dx)) * plan.shard, 16)
            out[z * plan.shard:(z + 1) * plan.shard, :] = trans_ref[pl.ds(start, plan.shard), :]


def write_own(plan, self_ref, own_ref, here_ref, there_ref, trans_ref):
    own_ref[...] = self_ref[...].astype(BF16)
    trans_ref[...] = self_ref[...].T.astype(BF16)
    write_rows(plan, trans_ref, here_ref, there_ref)


def layer_kernel(plan, cap, order, rows_ref, recv_ref, self_ref, cot_ref, w_ref, hidden_ref, mean_here, mean_there,
                 grad_here, grad_there, trans_ref, grad_ref):
    targets = self_ref.shape[0]
    rows = unpack(rows_ref[...], order, cap, hidden_ref.shape[1] // 128)
    fill = jnp.full((1, SLOT_PAD - cap), targets, jnp.int32)
    recv = jnp.concatenate([p for s in range(plan.ns) for p in (recv_ref[s:s + 1, :], fill)], axis=1)
    mean = neighbor_mean(cap, rows, recv, targets)
    preact = self_ref[...] + dot(mean, w_ref[...])
    trans_ref[...] = mean.astype(F32).T.astype(BF16)
    write_rows(plan, trans_ref, mean_here, mean_there)
    hidden, grad = forward(preact, cot_ref[...])
    hidden_ref[...] = hidden.astype(F32)
    for b in range(grad_ref.shape[0]):
        grad_ref[b] = grad[:, b * 128:(b + 1) * 128]
    y, each = plan.place()[2], plan.cols // 128
    for dy, out in enumerate((grad_here, grad_there)):
        for b in range(each):
            out[b * targets:(b + 1) * targets, :] = grad_ref[(y ^ dy) * each + b]


def left_kernel(plan, *refs):
    n = len(plan.peers)
    own, mean, outs = refs[n - 1::-1], refs[n:2 * n], refs[2 * n:]
    targets = own[0].shape[1]
    z, _, _, c = plan.place()
    keep_own = c == 0
    for i, (o, m) in enumerate(zip(own, mean)):
        at = slice(i * targets, (i + 1) * targets)
        for j, shards in enumerate((plan.far(), plan.near())):
            for r, k in enumerate(shards):
                rows = pl.ds(pl.multiple_of((z ^ k) * plan.shard, 16), plan.shard)
                to = slice(r * plan.shard, (r + 1) * plan.shard)
                outs[j][to, at] = jnp.where(keep_own, m[rows, :], o[rows, :])
                outs[2 + j][to, at] = jnp.where(keep_own, o[rows, :], m[rows, :])


def terms_kernel(left_ref, *refs):
    grad, out_ref = refs[:-1], refs[-1]
    targets = left_ref.shape[1] // len(grad)
    right = jnp.concatenate(
        [jnp.concatenate([g[b * targets:(b + 1) * targets, :] for b in range(grad[0].shape[0] // targets)], axis=1)
         for g in grad], axis=0)
    out_ref[...] = dot(left_ref[...], right).astype(out_ref.dtype)


def core_sum_kernel(plan, keep_ref, got_ref, *outs):
    for r, out in enumerate(outs):
        at = slice(r * plan.shard, (r + 1) * plan.shard)
        out[...] = (keep_ref[at, :] + got_ref[at, :].astype(F32)).astype(out.dtype)


def store_sum_kernel(*refs):
    total = refs[0][...]
    for r in refs[1:-1]:
        total += r[...].astype(F32)
    refs[-1][...] = total.astype(BF16)


def assemble_kernel(plan, *refs):
    parts, (self_ref, neigh_ref, both_ref) = refs[:-3], refs[-3:]
    _, _, y, c = plan.place()
    for i, part in enumerate(parts):
        cols = pl.ds(pl.multiple_of((y ^ (i // plan.gc)) * plan.cols, 128), plan.cols)
        both_ref[c ^ (i % plan.gc), :, cols] = part[...].astype(F32)
    self_ref[...] = both_ref[0]
    neigh_ref[...] = both_ref[1]


def per_device(plan, features, self_rows, edge_row, recv_target, cotangent, w_self, w_neigh):
    owned, width = features.shape
    out_width = w_self.shape[1]
    targets = self_rows.shape[0]
    ns, cap, mult = edge_row.shape[2:]
    slots = ns * SLOT_PAD
    edges = edge_row[0, 0].transpose(0, 2, 1)
    fits = plan.fits()
    order = plan.store_order() if fits else list(range(ns))
    rows, cols, n = plan.rows, plan.cols, len(plan.peers)
    scratch = [pltpu.VMEM(features.shape, F32), pltpu.VMEM(edges.shape, jnp.int32),
               pltpu.SemaphoreType.DMA((3,))]
    packed = pack_rows(cap, width)
    outs, more = [shape((ns * packed, 128), BF16)], []
    if fits:
        outs += [shape((targets, width), BF16)] + [shape((rows, targets), BF16)] * 2
        more = [self_rows]
        scratch += [pltpu.VMEM(self_rows.shape, F32), pltpu.VMEM((width, targets), BF16)]
    sums, *owns = call(
        functools.partial(slot_sums_kernel, plan, order), outs, (), hbm=[features, edges] + more,
        flops=4 * slots * owned * width, vmem=60 if fits else 16, scratch=scratch)
    arrived = lax.all_to_all(sums.reshape(ns, packed, 128), "store", split_axis=0, concat_axis=0,
                             tiled=True, axis_index_groups=[order]).reshape(ns * packed, 128)
    if not fits:
        own = self_rows.astype(BF16)
        recv = jnp.pad(recv_target[0, 0], ((0, 0), (0, SLOT_PAD - cap)), constant_values=targets).reshape(1, slots)
        mean = neighbor_mean(cap, unpack(arrived, order, cap, width // 128), recv, targets)
        preact = dot(own, w_self) + dot(mean, w_neigh)
        hidden, grad = forward(preact, cotangent)
        both = jnp.concatenate([own.T.reshape(ns, -1, targets), mean.T.reshape(ns, -1, targets)], axis=1)
        terms = dot(both.reshape(2 * width, targets), grad)
        part = lax.psum_scatter(terms, "store", scatter_dimension=0, tiled=True)
        total = lax.psum(part, "trainer")
        return hidden, total[:plan.shard], total[plan.shard:]

    def to_x(array):
        return plan.send(array, lambda z, x, y, c: (z, 1 - x, y, c))

    def to_y(array):
        return plan.send(array, lambda z, x, y, c: (z, x, 1 - y, c))

    def to_diagonal(array):
        return plan.send(array, lambda z, x, y, c: (z, 1 - x, 1 - y, c))

    def held(array, *until):
        return lax.optimization_barrier((array,) + until)[0]

    own, own_here, own_there = owns
    own_all = [own_here, to_y(own_here), to_x(own_there), to_diagonal(own_there)]
    self_term = dot(own, w_self)

    hidden, mean_here, mean_there, grad_here, grad_there = call(
        functools.partial(layer_kernel, plan, cap, order),
        [shape((targets, out_width), F32)] + [shape((rows, targets), BF16)] * 2
        + [shape((cols // 128 * targets, 128), BF16)] * 2,
        [arrived, recv_target[0, 0], self_term, cotangent, w_neigh],
        scratch=[pltpu.VMEM((width, targets), BF16), pltpu.VMEM((out_width // 128, targets, 128), BF16)],
        flops=2 * targets * width * (out_width + slots))
    mean_x, grad_y = to_x(mean_there), to_y(grad_there)
    grad_x = to_x(grad_here)
    mean_all = [mean_here, to_y(mean_here), mean_x, to_y(held(mean_x, *own_all[1:]))]
    grad_all = [grad_here, grad_y, grad_x, to_x(held(grad_y, mean_x, *own_all[1:]))]
    def to_core(array):
        return plan.send(array, lambda z, x, y, c: (z, x, y, 1 - c))

    def to_z(array, k):
        return plan.send(array, lambda z, x, y, c: (z ^ k, x, y, c))

    def terms(left, kind):
        return call(terms_kernel, [shape((left.shape[0], cols), kind)], [left] + grad_all,
                    flops=2 * left.shape[0] * cols * targets * n)[0]

    block = (plan.shard, cols)
    halves = [plan.far(), plan.near()]
    lefts = call(functools.partial(left_kernel, plan),
                 [shape((len(half) * plan.shard, n * targets), BF16) for half in halves * 2],
                 own_all[::-1] + mean_all)
    got, mine = [], None
    for half, give_left, keep_left in zip(halves, lefts[:2], lefts[2:]):
        came = to_core(terms(give_left, BF16))
        sums = call(functools.partial(core_sum_kernel, plan),
                    [shape(block, BF16 if k else F32) for k in half], [terms(keep_left, F32), came])
        for k, part in zip(half, sums):
            if k:
                got.append(to_z(part, k))
            else:
                mine = part
    (quarter,) = call(store_sum_kernel, [shape(block, BF16)], [mine] + got)
    column = [quarter] + [plan.send(quarter, lambda z, x, y, c, i=i: (z, x, y ^ i, c))
                          for i in range(1, plan.gy)]
    quarters = [q for part in column
                for q in (part, plan.send(part, lambda z, x, y, c: (z, x, y, 1 - c)))]
    grads = call(functools.partial(assemble_kernel, plan),
                 [shape((plan.shard, out_width), F32)] * 2, quarters,
                 scratch=[pltpu.VMEM((2, plan.shard, out_width), F32)])
    return hidden.astype(BF16), grads[0], grads[1]


def solution(mesh):
    in_specs = (
        P("store", None),
        P(("store", "trainer"), None),
        P("trainer", "store", None, None, None),
        P("trainer", "store", None, None),
        P(("store", "trainer"), None),
        P(),
        P(),
    )
    out_specs = (P(("store", "trainer"), None), P("store", None), P("store", None))

    def run(features, self_rows, edge_row, recv_target, cotangent, w_self, w_neigh):
        plan = Plan(mesh, features.shape[1], w_self.shape[1])
        return jax.shard_map(
            functools.partial(per_device, plan), mesh=mesh, in_specs=in_specs,
            out_specs=out_specs, check_vma=False,
        )(features, self_rows, edge_row, recv_target, cotangent, w_self, w_neigh)

    return run
```

```python
import functools

import jax
import jax.numpy as jnp
from jax import lax
from jax.experimental import pallas as pl
from jax.experimental.pallas import tpu as pltpu
from jax.sharding import PartitionSpec as P

BF16, F32 = jnp.bfloat16, jnp.float32
SLOT_PAD = 16
VMEM = pl.BlockSpec(memory_space=pltpu.VMEM)
ANY = pl.BlockSpec(memory_space=pl.ANY)
HBM = pl.BlockSpec(memory_space=pltpu.HBM)


def dot(a, b):
    return jnp.dot(a, b, preferred_element_type=F32)


def call(body, outs, args, unread=(), hbm=(), scratch=(), flops=0, vmem=16):
    moved = sum(a.size * a.dtype.itemsize for a in (*args, *outs))
    return pl.pallas_call(
        body,
        out_shape=list(outs),
        in_specs=[VMEM] * len(args) + [ANY] * len(unread) + [HBM] * len(hbm),
        out_specs=[VMEM] * len(outs),
        scratch_shapes=list(scratch),
        compiler_params=pltpu.CompilerParams(vmem_limit_bytes=vmem * 1024 * 1024),
        cost_estimate=pl.CostEstimate(flops=flops, bytes_accessed=moved, transcendentals=0),
    )(*args, *unread, *hbm)


def shape(dims, kind):
    return jax.ShapeDtypeStruct(dims, kind)


def pack_rows(cap, width):
    return cap * (width // 128) + 8


def pack(sums, counts, cap):
    blocks = sums.shape[1] // 128
    out = []
    for d in range(sums.shape[0] // SLOT_PAD):
        at = d * SLOT_PAD
        part = [sums[at:at + SLOT_PAD, j * 128:(j + 1) * 128] for j in range(blocks)]
        out += [p[:8] for p in part]
        out += [jnp.concatenate([part[j][8:cap], part[j + 1][8:cap]], axis=0) for j in range(0, blocks, 2)]
        out.append(counts[at + 8:at + SLOT_PAD])
    return jnp.concatenate(out, axis=0).astype(BF16)


def unpack(packed, order, cap, blocks):
    size = packed.shape[0] // len(order)
    rows = []
    for s in range(len(order)):
        at = order.index(s) * size
        part = packed[at:at + size, :].astype(F32)
        tail, counts = part[blocks * 8:size - 8], part[size - 8:]
        columns = []
        for j in range(blocks):
            low = tail[j // 2 * 8 + j % 2 * 4:j // 2 * 8 + j % 2 * 4 + 4]
            rest = counts[4:] if j == 0 else jnp.zeros((4, 128), F32)
            columns.append(jnp.concatenate([part[j * 8:j * 8 + 8], low, rest], axis=0))
        rows.append(jnp.concatenate(columns, axis=1))
    return jnp.concatenate(rows, axis=0).astype(BF16)


def slot_sums_kernel(plan, order, feat_hbm, edge_hbm, *rest):
    with_own = len(rest) > 4
    if with_own:
        self_hbm, out_ref, *own_refs, feat_ref, edge_ref, sems, self_ref, trans_ref = rest
    else:
        out_ref, feat_ref, edge_ref, sems = rest
    copies = [pltpu.make_async_copy(edge_hbm, edge_ref, sems.at[0]),
              pltpu.make_async_copy(feat_hbm, feat_ref, sems.at[1])]
    if with_own:
        copies.append(pltpu.make_async_copy(self_hbm, self_ref, sems.at[2]))
    for copy in copies:
        copy.start()
    owned = feat_ref.shape[0]
    _, mult, cap = edge_ref.shape
    slots = len(order) * SLOT_PAD
    copies[0].wait()
    fill = jnp.full((mult, SLOT_PAD - cap), owned, jnp.int32)
    ids = jnp.concatenate([p for d in order for p in (edge_ref[d], fill)], axis=1)
    row = lax.broadcasted_iota(jnp.int32, (owned, slots), 0)
    weight = jnp.zeros((owned, slots), F32)
    count = jnp.zeros((1, slots), F32)
    for m in range(ids.shape[0]):
        weight += (row == ids[m:m + 1, :]).astype(F32)
        count += (ids[m:m + 1, :] < owned).astype(F32)
    pick = weight.T.astype(BF16)
    r = lax.broadcasted_iota(jnp.int32, (slots, slots), 0)
    c = lax.broadcasted_iota(jnp.int32, (slots, slots), 1)
    here = ((r & (SLOT_PAD - 1)) == cap) & ((c - (c & (SLOT_PAD - 1))) == (r - (r & (SLOT_PAD - 1))))
    spread = jnp.where(here, jnp.broadcast_to(count, (slots, slots)), 0.0).astype(BF16)
    c2 = lax.broadcasted_iota(jnp.int32, (slots, 128), 0)
    l2 = lax.broadcasted_iota(jnp.int32, (slots, 128), 1)
    fold = ((c2 & (SLOT_PAD - 1)) == l2).astype(BF16)
    counts = dot(spread, fold)
    copies[1].wait()
    feat = feat_ref[...]
    high = feat.astype(BF16)
    low = (feat - high.astype(F32)).astype(BF16)
    sums = dot(pick, high) + dot(pick, low)
    out_ref[...] = pack(sums, counts, cap)
    if with_own:
        copies[2].wait()
        write_own(plan, self_ref, *own_refs, trans_ref)


def neighbor_mean(cap, rows, recv, targets):
    slots = rows.shape[0]
    target = lax.broadcasted_iota(jnp.int32, (targets, slots), 0)
    onehot = (target == recv).astype(BF16)
    r = lax.broadcasted_iota(jnp.int32, (slots, slots), 0)
    c = lax.broadcasted_iota(jnp.int32, (slots, slots), 1)
    from_count = (c == (r - (r & (SLOT_PAD - 1)) + cap)).astype(BF16)
    copied = dot(from_count, rows[:, :128])
    r2 = lax.broadcasted_iota(jnp.int32, (slots, 128), 0)
    l2 = lax.broadcasted_iota(jnp.int32, (slots, 128), 1)
    counts = jnp.where((r2 & (SLOT_PAD - 1)) == l2, copied, 0.0).astype(BF16)
    number = jnp.sum(dot(onehot, counts), axis=1, keepdims=True)
    return (dot(onehot, rows) / jnp.maximum(number, 1.0)).astype(BF16)


def forward(preact, cot):
    sig = jax.nn.sigmoid(preact)
    hidden = (preact * sig).astype(BF16)
    grad = (cot.astype(F32) * (sig * (1.0 + preact * (1.0 - sig)))).astype(BF16)
    return hidden, grad


class Plan:
    def __init__(self, mesh, width, out_width):
        self.ns, self.nt = mesh.shape["store"], mesh.shape["trainer"]
        self.gx = 2 if self.ns % 2 == 0 else 1
        self.nz = self.ns // self.gx
        self.gc = 2
        self.gy = max(self.nt // self.gc, 1)
        self.shard = width // self.ns
        self.rows = self.nz * self.shard
        self.cols = out_width // self.gy
        self.peers = [(dx, dy) for dx in range(self.gx) for dy in range(self.gy)]

    def fits(self):
        pow2 = all((n & (n - 1)) == 0 for n in (self.ns, self.nt))
        return (pow2 and self.ns <= 8 and self.gx == 2 and self.gy == 2 and self.gy * self.gc == self.nt and self.cols % 128 == 0
                and self.shard % 16 == 0 and len(self.peers) <= 4 and self.nz == 4)

    def place(self):
        s, t = lax.axis_index("store"), lax.axis_index("trainer")
        return s // self.gx, s % self.gx, t // self.gc, t % self.gc

    def far(self):
        return list(range(2, self.nz))

    def near(self):
        return list(range(min(2, self.nz)))[::-1]

    def send(self, array, to):
        pairs = []
        for s in range(self.ns):
            for t in range(self.nt):
                z, x, y, c = to(s // self.gx, s % self.gx, t // self.gc, t % self.gc)
                pairs.append((s * self.nt + t, (z * self.gx + x) * self.nt + y * self.gc + c))
        return lax.ppermute(array, ("store", "trainer"), pairs)

    def store_order(self):
        middle = self.ns // 2
        turns = [s for pair in zip(range(middle, self.ns), range(middle - 1, -1, -1)) for s in pair]
        return turns


def write_rows(plan, trans_ref, *outs):
    x = plan.place()[1]
    for dx, out in enumerate(outs):
        for z in range(plan.nz):
            start = pl.multiple_of((z * plan.gx + (x ^ dx)) * plan.shard, 16)
            out[z * plan.shard:(z + 1) * plan.shard, :] = trans_ref[pl.ds(start, plan.shard), :]


def write_own(plan, self_ref, own_ref, here_ref, there_ref, trans_ref):
    own_ref[...] = self_ref[...].astype(BF16)
    trans_ref[...] = self_ref[...].T.astype(BF16)
    write_rows(plan, trans_ref, here_ref, there_ref)


def layer_kernel(plan, cap, order, rows_ref, recv_ref, self_ref, cot_ref, w_ref, _, hidden_ref, mean_here, mean_there,
                 grad_here, grad_there, trans_ref, grad_ref):
    targets = self_ref.shape[0]
    rows = unpack(rows_ref[...], order, cap, hidden_ref.shape[1] // 128)
    fill = jnp.full((1, SLOT_PAD - cap), targets, jnp.int32)
    recv = jnp.concatenate([p for s in range(plan.ns) for p in (recv_ref[s:s + 1, :], fill)], axis=1)
    mean = neighbor_mean(cap, rows, recv, targets)
    preact = self_ref[...] + dot(mean, w_ref[...])
    trans_ref[...] = mean.astype(F32).T.astype(BF16)
    write_rows(plan, trans_ref, mean_here, mean_there)
    hidden, grad = forward(preact, cot_ref[...])
    hidden_ref[...] = hidden.astype(F32)
    for b in range(grad_ref.shape[0]):
        grad_ref[b] = grad[:, b * 128:(b + 1) * 128]
    y, each = plan.place()[2], plan.cols // 128
    for dy, out in enumerate((grad_here, grad_there)):
        for b in range(each):
            out[b * targets:(b + 1) * targets, :] = grad_ref[(y ^ dy) * each + b]


def left_kernel(plan, *refs):
    n = len(plan.peers)
    own, mean, outs = refs[n - 1::-1], refs[n:2 * n], refs[2 * n:]
    targets = own[0].shape[1]
    z, _, _, c = plan.place()
    keep_own = c == 0
    for i, (o, m) in enumerate(zip(own, mean)):
        at = slice(i * targets, (i + 1) * targets)
        for j, shards in enumerate((plan.far(), plan.near())):
            for r, k in enumerate(shards):
                rows = pl.ds(pl.multiple_of((z ^ k) * plan.shard, 16), plan.shard)
                to = slice(r * plan.shard, (r + 1) * plan.shard)
                outs[j][to, at] = jnp.where(keep_own, m[rows, :], o[rows, :])
                outs[2 + j][to, at] = jnp.where(keep_own, o[rows, :], m[rows, :])


def terms_kernel(left_ref, *refs):
    grad, out_ref = refs[:-1], refs[-1]
    targets = left_ref.shape[1] // len(grad)
    right = jnp.concatenate(
        [jnp.concatenate([g[b * targets:(b + 1) * targets, :] for b in range(grad[0].shape[0] // targets)], axis=1)
         for g in grad], axis=0)
    out_ref[...] = dot(left_ref[...], right).astype(out_ref.dtype)


def core_sum_kernel(plan, keep_ref, got_ref, *outs):
    for r, out in enumerate(outs):
        at = slice(r * plan.shard, (r + 1) * plan.shard)
        out[...] = (keep_ref[at, :] + got_ref[at, :].astype(F32)).astype(out.dtype)


def store_sum_kernel(*refs):
    total = refs[0][...]
    for r in refs[1:-1]:
        total += r[...].astype(F32)
    refs[-1][...] = total.astype(BF16)


def assemble_kernel(plan, *refs):
    parts, (self_ref, neigh_ref, both_ref) = refs[:-3], refs[-3:]
    _, _, y, c = plan.place()
    for i, part in enumerate(parts):
        cols = pl.ds(pl.multiple_of((y ^ (i // plan.gc)) * plan.cols, 128), plan.cols)
        both_ref[c ^ (i % plan.gc), :, cols] = part[...].astype(F32)
    self_ref[...] = both_ref[0]
    neigh_ref[...] = both_ref[1]


def per_device(plan, features, self_rows, edge_row, recv_target, cotangent, w_self, w_neigh):
    owned, width = features.shape
    out_width = w_self.shape[1]
    targets = self_rows.shape[0]
    ns, cap, mult = edge_row.shape[2:]
    slots = ns * SLOT_PAD
    edges = edge_row[0, 0].transpose(0, 2, 1)
    fits = plan.fits()
    order = plan.store_order() if fits else list(range(ns))
    rows, cols, n = plan.rows, plan.cols, len(plan.peers)
    scratch = [pltpu.VMEM(features.shape, F32), pltpu.VMEM(edges.shape, jnp.int32),
               pltpu.SemaphoreType.DMA((3,))]
    packed = pack_rows(cap, width)
    outs, more = [shape((ns * packed, 128), BF16)], []
    if fits:
        outs += [shape((targets, width), BF16)] + [shape((rows, targets), BF16)] * 2
        more = [self_rows]
        scratch += [pltpu.VMEM(self_rows.shape, F32), pltpu.VMEM((width, targets), BF16)]
    sums, *owns = call(
        functools.partial(slot_sums_kernel, plan, order), outs, (), hbm=[features, edges] + more,
        flops=4 * slots * owned * width, vmem=60 if fits else 16, scratch=scratch)
    arrived = lax.all_to_all(sums.reshape(ns, packed, 128), "store", split_axis=0, concat_axis=0,
                             tiled=True, axis_index_groups=[order]).reshape(ns * packed, 128)
    if not fits:
        own = self_rows.astype(BF16)
        recv = jnp.pad(recv_target[0, 0], ((0, 0), (0, SLOT_PAD - cap)), constant_values=targets).reshape(1, slots)
        mean = neighbor_mean(cap, unpack(arrived, order, cap, width // 128), recv, targets)
        preact = dot(own, w_self) + dot(mean, w_neigh)
        hidden, grad = forward(preact, cotangent)
        both = jnp.concatenate([own.T.reshape(ns, -1, targets), mean.T.reshape(ns, -1, targets)], axis=1)
        terms = dot(both.reshape(2 * width, targets), grad)
        part = lax.psum_scatter(terms, "store", scatter_dimension=0, tiled=True)
        total = lax.psum(part, "trainer")
        return hidden, total[:plan.shard], total[plan.shard:]

    def to_x(array):
        return plan.send(array, lambda z, x, y, c: (z, 1 - x, y, c))

    def to_y(array):
        return plan.send(array, lambda z, x, y, c: (z, x, 1 - y, c))

    def to_diagonal(array):
        return plan.send(array, lambda z, x, y, c: (z, 1 - x, 1 - y, c))

    def held(array, *until):
        return lax.optimization_barrier((array,) + until)[0]

    own, own_here, own_there = owns
    own_x = to_x(own_there)
    own_y = to_y(held(own_here, own_x))
    own_all = [own_here, own_y, own_x, to_diagonal(held(own_there, own_x))]
    self_term = dot(own, w_self)

    hidden, mean_here, mean_there, grad_here, grad_there = call(
        functools.partial(layer_kernel, plan, cap, order),
        [shape((targets, out_width), F32)] + [shape((rows, targets), BF16)] * 2
        + [shape((cols // 128 * targets, 128), BF16)] * 2,
        [arrived, recv_target[0, 0], self_term, cotangent, w_neigh], unread=[own_y],
        scratch=[pltpu.VMEM((width, targets), BF16), pltpu.VMEM((out_width // 128, targets, 128), BF16)],
        flops=2 * targets * width * (out_width + slots))
    mean_x, grad_y = to_x(mean_there), to_y(grad_there)
    grad_x = to_x(grad_here)
    mean_all = [mean_here, to_y(mean_here), mean_x, to_y(held(mean_x, *own_all[1:]))]
    grad_all = [grad_here, grad_y, grad_x, to_x(held(grad_y, mean_x, *own_all[1:]))]
    def to_core(array):
        return plan.send(array, lambda z, x, y, c: (z, x, y, 1 - c))

    def to_z(array, k):
        return plan.send(array, lambda z, x, y, c: (z ^ k, x, y, c))

    def terms(left, kind):
        return call(terms_kernel, [shape((left.shape[0], cols), kind)], [left] + grad_all,
                    flops=2 * left.shape[0] * cols * targets * n)[0]

    block = (plan.shard, cols)
    halves = [plan.far(), plan.near()]
    lefts = call(functools.partial(left_kernel, plan),
                 [shape((len(half) * plan.shard, n * targets), BF16) for half in halves * 2],
                 own_all[::-1] + mean_all)
    got, mine = [], None
    for half, give_left, keep_left in zip(halves, lefts[:2], lefts[2:]):
        came = to_core(terms(give_left, BF16))
        sums = call(functools.partial(core_sum_kernel, plan),
                    [shape(block, BF16 if k else F32) for k in half], [terms(keep_left, F32), came])
        for k, part in zip(half, sums):
            if k:
                got.append(to_z(part, k))
            else:
                mine = part
    (quarter,) = call(store_sum_kernel, [shape(block, BF16)], [mine] + got)
    column = [quarter] + [plan.send(quarter, lambda z, x, y, c, i=i: (z, x, y ^ i, c))
                          for i in range(1, plan.gy)]
    quarters = [q for part in column
                for q in (part, plan.send(part, lambda z, x, y, c: (z, x, y, 1 - c)))]
    grads = call(functools.partial(assemble_kernel, plan),
                 [shape((plan.shard, out_width), F32)] * 2, quarters,
                 scratch=[pltpu.VMEM((2, plan.shard, out_width), F32)])
    return hidden.astype(BF16), grads[0], grads[1]


def solution(mesh):
    in_specs = (
        P("store", None),
        P(("store", "trainer"), None),
        P("trainer", "store", None, None, None),
        P("trainer", "store", None, None),
        P(("store", "trainer"), None),
        P(),
        P(),
    )
    out_specs = (P(("store", "trainer"), None), P("store", None), P("store", None))

    def run(features, self_rows, edge_row, recv_target, cotangent, w_self, w_neigh):
        plan = Plan(mesh, features.shape[1], w_self.shape[1])
        return jax.shard_map(
            functools.partial(per_device, plan), mesh=mesh, in_specs=in_specs,
            out_specs=out_specs, check_vma=False,
        )(features, self_rows, edge_row, recv_target, cotangent, w_self, w_neigh)

    return run
```

```python
import functools

import jax
import jax.numpy as jnp
from jax import lax
from jax.experimental import pallas as pl
from jax.experimental.pallas import tpu as pltpu
from jax.sharding import PartitionSpec as P

BF16, F32 = jnp.bfloat16, jnp.float32
SLOT_PAD = 16
VMEM = pl.BlockSpec(memory_space=pltpu.VMEM)
ANY = pl.BlockSpec(memory_space=pl.ANY)
HBM = pl.BlockSpec(memory_space=pltpu.HBM)


def dot(a, b):
    return jnp.dot(a, b, preferred_element_type=F32)


def call(body, outs, args, unread=(), hbm=(), scratch=(), flops=0, vmem=16):
    moved = sum(a.size * a.dtype.itemsize for a in (*args, *outs))
    return pl.pallas_call(
        body,
        out_shape=list(outs),
        in_specs=[VMEM] * len(args) + [ANY] * len(unread) + [HBM] * len(hbm),
        out_specs=[VMEM] * len(outs),
        scratch_shapes=list(scratch),
        compiler_params=pltpu.CompilerParams(vmem_limit_bytes=vmem * 1024 * 1024),
        cost_estimate=pl.CostEstimate(flops=flops, bytes_accessed=moved, transcendentals=0),
    )(*args, *unread, *hbm)


def shape(dims, kind):
    return jax.ShapeDtypeStruct(dims, kind)


def pack_rows(cap, width):
    return cap * (width // 128) + 8


def pack(sums, counts, cap):
    blocks = sums.shape[1] // 128
    out = []
    for d in range(sums.shape[0] // SLOT_PAD):
        at = d * SLOT_PAD
        part = [sums[at:at + SLOT_PAD, j * 128:(j + 1) * 128] for j in range(blocks)]
        out += [p[:8] for p in part]
        out += [jnp.concatenate([part[j][8:cap], part[j + 1][8:cap]], axis=0) for j in range(0, blocks, 2)]
        out.append(counts[at + 8:at + SLOT_PAD])
    return jnp.concatenate(out, axis=0).astype(BF16)


def unpack(packed, order, cap, blocks):
    size = packed.shape[0] // len(order)
    rows = []
    for s in range(len(order)):
        at = order.index(s) * size
        part = packed[at:at + size, :].astype(F32)
        tail, counts = part[blocks * 8:size - 8], part[size - 8:]
        columns = []
        for j in range(blocks):
            low = tail[j // 2 * 8 + j % 2 * 4:j // 2 * 8 + j % 2 * 4 + 4]
            rest = counts[4:] if j == 0 else jnp.zeros((4, 128), F32)
            columns.append(jnp.concatenate([part[j * 8:j * 8 + 8], low, rest], axis=0))
        rows.append(jnp.concatenate(columns, axis=1))
    return jnp.concatenate(rows, axis=0).astype(BF16)


def slot_sums_kernel(plan, order, feat_hbm, edge_hbm, *rest):
    with_own = len(rest) > 4
    if with_own:
        self_hbm, out_ref, *own_refs, feat_ref, edge_ref, sems, self_ref, trans_ref = rest
    else:
        out_ref, feat_ref, edge_ref, sems = rest
    copies = [pltpu.make_async_copy(edge_hbm, edge_ref, sems.at[0]),
              pltpu.make_async_copy(feat_hbm, feat_ref, sems.at[1])]
    if with_own:
        copies.append(pltpu.make_async_copy(self_hbm, self_ref, sems.at[2]))
    for copy in copies:
        copy.start()
    owned = feat_ref.shape[0]
    _, mult, cap = edge_ref.shape
    slots = len(order) * SLOT_PAD
    copies[0].wait()
    fill = jnp.full((mult, SLOT_PAD - cap), owned, jnp.int32)
    ids = jnp.concatenate([p for d in order for p in (edge_ref[d], fill)], axis=1)
    row = lax.broadcasted_iota(jnp.int32, (owned, slots), 0)
    weight = jnp.zeros((owned, slots), F32)
    count = jnp.zeros((1, slots), F32)
    for m in range(ids.shape[0]):
        weight += (row == ids[m:m + 1, :]).astype(F32)
        count += (ids[m:m + 1, :] < owned).astype(F32)
    pick = weight.T.astype(BF16)
    r = lax.broadcasted_iota(jnp.int32, (slots, slots), 0)
    c = lax.broadcasted_iota(jnp.int32, (slots, slots), 1)
    here = ((r & (SLOT_PAD - 1)) == cap) & ((c - (c & (SLOT_PAD - 1))) == (r - (r & (SLOT_PAD - 1))))
    spread = jnp.where(here, jnp.broadcast_to(count, (slots, slots)), 0.0).astype(BF16)
    c2 = lax.broadcasted_iota(jnp.int32, (slots, 128), 0)
    l2 = lax.broadcasted_iota(jnp.int32, (slots, 128), 1)
    fold = ((c2 & (SLOT_PAD - 1)) == l2).astype(BF16)
    counts = dot(spread, fold)
    copies[1].wait()
    feat = feat_ref[...]
    high = feat.astype(BF16)
    low = (feat - high.astype(F32)).astype(BF16)
    sums = dot(pick, high) + dot(pick, low)
    out_ref[...] = pack(sums, counts, cap)
    if with_own:
        copies[2].wait()
        write_own(plan, self_ref, *own_refs, trans_ref)


def neighbor_mean(cap, rows, recv, targets):
    slots = rows.shape[0]
    target = lax.broadcasted_iota(jnp.int32, (targets, slots), 0)
    onehot = (target == recv).astype(BF16)
    r = lax.broadcasted_iota(jnp.int32, (slots, slots), 0)
    c = lax.broadcasted_iota(jnp.int32, (slots, slots), 1)
    from_count = (c == (r - (r & (SLOT_PAD - 1)) + cap)).astype(BF16)
    copied = dot(from_count, rows[:, :128])
    r2 = lax.broadcasted_iota(jnp.int32, (slots, 128), 0)
    l2 = lax.broadcasted_iota(jnp.int32, (slots, 128), 1)
    counts = jnp.where((r2 & (SLOT_PAD - 1)) == l2, copied, 0.0).astype(BF16)
    number = jnp.sum(dot(onehot, counts), axis=1, keepdims=True)
    return (dot(onehot, rows) / jnp.maximum(number, 1.0)).astype(BF16)


def forward(preact, cot):
    sig = jax.nn.sigmoid(preact)
    hidden = (preact * sig).astype(BF16)
    grad = (cot.astype(F32) * (sig * (1.0 + preact * (1.0 - sig)))).astype(BF16)
    return hidden, grad


class Plan:
    def __init__(self, mesh, width, out_width):
        self.ns, self.nt = mesh.shape["store"], mesh.shape["trainer"]
        self.gx = 2 if self.ns % 2 == 0 else 1
        self.nz = self.ns // self.gx
        self.gc = 2
        self.gy = max(self.nt // self.gc, 1)
        self.shard = width // self.ns
        self.rows = self.nz * self.shard
        self.cols = out_width // self.gy
        self.peers = [(dx, dy) for dx in range(self.gx) for dy in range(self.gy)]

    def fits(self):
        pow2 = all((n & (n - 1)) == 0 for n in (self.ns, self.nt))
        return (pow2 and self.ns <= 8 and self.gx == 2 and self.gy == 2 and self.gy * self.gc == self.nt and self.cols % 128 == 0
                and self.shard % 16 == 0 and len(self.peers) <= 4 and self.nz == 4)

    def place(self):
        s, t = lax.axis_index("store"), lax.axis_index("trainer")
        return s // self.gx, s % self.gx, t // self.gc, t % self.gc

    def far(self):
        return list(range(2, self.nz))

    def near(self):
        return list(range(min(2, self.nz)))[::-1]

    def send(self, array, to):
        pairs = []
        for s in range(self.ns):
            for t in range(self.nt):
                z, x, y, c = to(s // self.gx, s % self.gx, t // self.gc, t % self.gc)
                pairs.append((s * self.nt + t, (z * self.gx + x) * self.nt + y * self.gc + c))
        return lax.ppermute(array, ("store", "trainer"), pairs)

    def store_order(self):
        middle = self.ns // 2
        turns = [s for pair in zip(range(middle, self.ns), range(middle - 1, -1, -1)) for s in pair]
        return turns


def write_rows(plan, trans_ref, *outs):
    x = plan.place()[1]
    for dx, out in enumerate(outs):
        for z in range(plan.nz):
            start = pl.multiple_of((z * plan.gx + (x ^ dx)) * plan.shard, 16)
            out[z * plan.shard:(z + 1) * plan.shard, :] = trans_ref[pl.ds(start, plan.shard), :]


def write_own(plan, self_ref, own_ref, here_ref, there_ref, trans_ref):
    own_ref[...] = self_ref[...].astype(BF16)
    trans_ref[...] = self_ref[...].T.astype(BF16)
    write_rows(plan, trans_ref, here_ref, there_ref)


def mean_kernel(plan, cap, order, rows_ref, recv_ref, _, mean_ref, here_ref, there_ref, trans_ref):
    rows = unpack(rows_ref[...], order, cap, mean_ref.shape[1] // 128)
    targets = mean_ref.shape[0]
    fill = jnp.full((1, SLOT_PAD - cap), targets, jnp.int32)
    recv = jnp.concatenate([p for s in range(plan.ns) for p in (recv_ref[s:s + 1, :], fill)], axis=1)
    mean = neighbor_mean(cap, rows, recv, targets)
    mean_ref[...] = mean
    trans_ref[...] = mean.astype(F32).T.astype(BF16)
    write_rows(plan, trans_ref, here_ref, there_ref)


def layer_kernel(plan, mean_ref, self_ref, cot_ref, w_ref, hidden_ref, here_ref, there_ref, grad_ref):
    targets = self_ref.shape[0]
    preact = self_ref[...] + dot(mean_ref[...], w_ref[...])
    hidden, grad = forward(preact, cot_ref[...])
    hidden_ref[...] = hidden.astype(F32)
    for b in range(grad_ref.shape[0]):
        grad_ref[b] = grad[:, b * 128:(b + 1) * 128]
    y, each = plan.place()[2], plan.cols // 128
    for dy, out in enumerate((here_ref, there_ref)):
        for b in range(each):
            out[b * targets:(b + 1) * targets, :] = grad_ref[(y ^ dy) * each + b]


def left_kernel(plan, *refs):
    n = len(plan.peers)
    own, mean, outs = refs[n - 1::-1], refs[n:2 * n], refs[2 * n:]
    targets = own[0].shape[1]
    z, _, _, c = plan.place()
    keep_own = c == 0
    for i, (o, m) in enumerate(zip(own, mean)):
        at = slice(i * targets, (i + 1) * targets)
        for j, shards in enumerate((plan.far(), plan.near())):
            for r, k in enumerate(shards):
                rows = pl.ds(pl.multiple_of((z ^ k) * plan.shard, 16), plan.shard)
                to = slice(r * plan.shard, (r + 1) * plan.shard)
                outs[j][to, at] = jnp.where(keep_own, m[rows, :], o[rows, :])
                outs[2 + j][to, at] = jnp.where(keep_own, o[rows, :], m[rows, :])


def terms_kernel(left_ref, *refs):
    grad, out_ref = refs[:-1], refs[-1]
    targets = left_ref.shape[1] // len(grad)
    right = jnp.concatenate(
        [jnp.concatenate([g[b * targets:(b + 1) * targets, :] for b in range(grad[0].shape[0] // targets)], axis=1)
         for g in grad], axis=0)
    out_ref[...] = dot(left_ref[...], right).astype(out_ref.dtype)


def core_sum_kernel(plan, keep_ref, got_ref, *outs):
    for r, out in enumerate(outs):
        at = slice(r * plan.shard, (r + 1) * plan.shard)
        out[...] = (keep_ref[at, :] + got_ref[at, :].astype(F32)).astype(out.dtype)


def store_sum_kernel(*refs):
    total = refs[0][...]
    for r in refs[1:-1]:
        total += r[...].astype(F32)
    refs[-1][...] = total.astype(BF16)


def assemble_kernel(plan, *refs):
    parts, (self_ref, neigh_ref, both_ref) = refs[:-3], refs[-3:]
    _, _, y, c = plan.place()
    for i, part in enumerate(parts):
        cols = pl.ds(pl.multiple_of((y ^ (i // plan.gc)) * plan.cols, 128), plan.cols)
        both_ref[c ^ (i % plan.gc), :, cols] = part[...].astype(F32)
    self_ref[...] = both_ref[0]
    neigh_ref[...] = both_ref[1]


def per_device(plan, features, self_rows, edge_row, recv_target, cotangent, w_self, w_neigh):
    owned, width = features.shape
    out_width = w_self.shape[1]
    targets = self_rows.shape[0]
    ns, cap, mult = edge_row.shape[2:]
    slots = ns * SLOT_PAD
    edges = edge_row[0, 0].transpose(0, 2, 1)
    fits = plan.fits()
    order = plan.store_order() if fits else list(range(ns))
    rows, cols, n = plan.rows, plan.cols, len(plan.peers)
    scratch = [pltpu.VMEM(features.shape, F32), pltpu.VMEM(edges.shape, jnp.int32),
               pltpu.SemaphoreType.DMA((3,))]
    packed = pack_rows(cap, width)
    outs, more = [shape((ns * packed, 128), BF16)], []
    if fits:
        outs += [shape((targets, width), BF16)] + [shape((rows, targets), BF16)] * 2
        more = [self_rows]
        scratch += [pltpu.VMEM(self_rows.shape, F32), pltpu.VMEM((width, targets), BF16)]
    sums, *owns = call(
        functools.partial(slot_sums_kernel, plan, order), outs, (), hbm=[features, edges] + more,
        flops=4 * slots * owned * width, vmem=60 if fits else 16, scratch=scratch)
    arrived = lax.all_to_all(sums.reshape(ns, packed, 128), "store", split_axis=0, concat_axis=0,
                             tiled=True, axis_index_groups=[order]).reshape(ns * packed, 128)
    if not fits:
        own = self_rows.astype(BF16)
        recv = jnp.pad(recv_target[0, 0], ((0, 0), (0, SLOT_PAD - cap)), constant_values=targets).reshape(1, slots)
        mean = neighbor_mean(cap, unpack(arrived, order, cap, width // 128), recv, targets)
        preact = dot(own, w_self) + dot(mean, w_neigh)
        hidden, grad = forward(preact, cotangent)
        both = jnp.concatenate([own.T.reshape(ns, -1, targets), mean.T.reshape(ns, -1, targets)], axis=1)
        terms = dot(both.reshape(2 * width, targets), grad)
        part = lax.psum_scatter(terms, "store", scatter_dimension=0, tiled=True)
        total = lax.psum(part, "trainer")
        return hidden, total[:plan.shard], total[plan.shard:]

    def to_x(array):
        return plan.send(array, lambda z, x, y, c: (z, 1 - x, y, c))

    def to_y(array):
        return plan.send(array, lambda z, x, y, c: (z, x, 1 - y, c))

    def to_diagonal(array):
        return plan.send(array, lambda z, x, y, c: (z, 1 - x, 1 - y, c))

    def held(array, *until):
        return lax.optimization_barrier((array,) + until)[0]

    own, own_here, own_there = owns
    own_all = [own_here, to_y(own_here), to_x(own_there), to_diagonal(own_there)]
    self_term = dot(own, w_self)

    mean, mean_here, mean_there = call(
        functools.partial(mean_kernel, plan, cap, order),
        [shape((targets, width), BF16)] + [shape((rows, targets), BF16)] * 2, [arrived, recv_target[0, 0], self_term],
        scratch=[pltpu.VMEM((width, targets), BF16)], flops=2 * targets * width * slots)
    hidden, grad_here, grad_there = call(
        functools.partial(layer_kernel, plan),
        [shape((targets, out_width), F32)] + [shape((cols // 128 * targets, 128), BF16)] * 2,
        [mean, self_term, cotangent, w_neigh],
        scratch=[pltpu.VMEM((out_width // 128, targets, 128), BF16)],
        flops=2 * targets * width * out_width)
    mean_x, grad_y = to_x(mean_there), to_y(grad_there)
    grad_x = to_x(grad_here)
    mean_all = [mean_here, to_y(mean_here), mean_x, to_y(held(mean_x, *own_all[1:]))]
    grad_all = [grad_here, grad_y, grad_x, to_x(held(grad_y, mean_x, *own_all[1:]))]
    def to_core(array):
        return plan.send(array, lambda z, x, y, c: (z, x, y, 1 - c))

    def to_z(array, k):
        return plan.send(array, lambda z, x, y, c: (z ^ k, x, y, c))

    def terms(left, kind):
        return call(terms_kernel, [shape((left.shape[0], cols), kind)], [left] + grad_all,
                    flops=2 * left.shape[0] * cols * targets * n)[0]

    block = (plan.shard, cols)
    halves = [plan.far(), plan.near()]
    lefts = call(functools.partial(left_kernel, plan),
                 [shape((len(half) * plan.shard, n * targets), BF16) for half in halves * 2],
                 own_all[::-1] + mean_all)
    got, mine = [], None
    for half, give_left, keep_left in zip(halves, lefts[:2], lefts[2:]):
        came = to_core(terms(give_left, BF16))
        sums = call(functools.partial(core_sum_kernel, plan),
                    [shape(block, BF16 if k else F32) for k in half], [terms(keep_left, F32), came])
        for k, part in zip(half, sums):
            if k:
                got.append(to_z(part, k))
            else:
                mine = part
    (quarter,) = call(store_sum_kernel, [shape(block, BF16)], [mine] + got)
    column = [quarter] + [plan.send(quarter, lambda z, x, y, c, i=i: (z, x, y ^ i, c))
                          for i in range(1, plan.gy)]
    quarters = [q for part in column
                for q in (part, plan.send(part, lambda z, x, y, c: (z, x, y, 1 - c)))]
    grads = call(functools.partial(assemble_kernel, plan),
                 [shape((plan.shard, out_width), F32)] * 2, quarters,
                 scratch=[pltpu.VMEM((2, plan.shard, out_width), F32)])
    return hidden.astype(BF16), grads[0], grads[1]


def solution(mesh):
    in_specs = (
        P("store", None),
        P(("store", "trainer"), None),
        P("trainer", "store", None, None, None),
        P("trainer", "store", None, None),
        P(("store", "trainer"), None),
        P(),
        P(),
    )
    out_specs = (P(("store", "trainer"), None), P("store", None), P("store", None))

    def run(features, self_rows, edge_row, recv_target, cotangent, w_self, w_neigh):
        plan = Plan(mesh, features.shape[1], w_self.shape[1])
        return jax.shard_map(
            functools.partial(per_device, plan), mesh=mesh, in_specs=in_specs,
            out_specs=out_specs, check_vma=False,
        )(features, self_rows, edge_row, recv_target, cotangent, w_self, w_neigh)

    return run
```

```python
import functools

import jax
import jax.numpy as jnp
from jax import lax
from jax.experimental import pallas as pl
from jax.experimental.pallas import tpu as pltpu
from jax.sharding import PartitionSpec as P

BF16, F32 = jnp.bfloat16, jnp.float32
SLOT_PAD = 16
VMEM = pl.BlockSpec(memory_space=pltpu.VMEM)
ANY = pl.BlockSpec(memory_space=pl.ANY)
HBM = pl.BlockSpec(memory_space=pltpu.HBM)


def dot(a, b):
    return jnp.dot(a, b, preferred_element_type=F32)


def call(body, outs, args, unread=(), hbm=(), scratch=(), flops=0, vmem=16):
    moved = sum(a.size * a.dtype.itemsize for a in (*args, *outs))
    return pl.pallas_call(
        body,
        out_shape=list(outs),
        in_specs=[VMEM] * len(args) + [ANY] * len(unread) + [HBM] * len(hbm),
        out_specs=[VMEM] * len(outs),
        scratch_shapes=list(scratch),
        compiler_params=pltpu.CompilerParams(vmem_limit_bytes=vmem * 1024 * 1024),
        cost_estimate=pl.CostEstimate(flops=flops, bytes_accessed=moved, transcendentals=0),
    )(*args, *unread, *hbm)


def shape(dims, kind):
    return jax.ShapeDtypeStruct(dims, kind)


def pack_rows(cap, width):
    return cap * (width // 128) + 8


def pack(sums, counts, cap):
    blocks = sums.shape[1] // 128
    out = []
    for d in range(sums.shape[0] // SLOT_PAD):
        at = d * SLOT_PAD
        part = [sums[at:at + SLOT_PAD, j * 128:(j + 1) * 128] for j in range(blocks)]
        out += [p[:8] for p in part]
        out += [jnp.concatenate([part[j][8:cap], part[j + 1][8:cap]], axis=0) for j in range(0, blocks, 2)]
        out.append(counts[at + 8:at + SLOT_PAD])
    return jnp.concatenate(out, axis=0).astype(BF16)


def unpack(packed, order, cap, blocks):
    size = packed.shape[0] // len(order)
    rows = []
    for s in range(len(order)):
        at = order.index(s) * size
        part = packed[at:at + size, :].astype(F32)
        tail, counts = part[blocks * 8:size - 8], part[size - 8:]
        columns = []
        for j in range(blocks):
            low = tail[j // 2 * 8 + j % 2 * 4:j // 2 * 8 + j % 2 * 4 + 4]
            rest = counts[4:] if j == 0 else jnp.zeros((4, 128), F32)
            columns.append(jnp.concatenate([part[j * 8:j * 8 + 8], low, rest], axis=0))
        rows.append(jnp.concatenate(columns, axis=1))
    return jnp.concatenate(rows, axis=0).astype(BF16)


def slot_sums_kernel(plan, order, feat_hbm, edge_hbm, *rest):
    with_own = len(rest) > 4
    if with_own:
        self_hbm, out_ref, *own_refs, feat_ref, edge_ref, sems, self_ref, trans_ref = rest
    else:
        out_ref, feat_ref, edge_ref, sems = rest
    copies = [pltpu.make_async_copy(edge_hbm, edge_ref, sems.at[0]),
              pltpu.make_async_copy(feat_hbm, feat_ref, sems.at[1])]
    if with_own:
        copies.append(pltpu.make_async_copy(self_hbm, self_ref, sems.at[2]))
    for copy in copies:
        copy.start()
    owned = feat_ref.shape[0]
    _, mult, cap = edge_ref.shape
    slots = len(order) * SLOT_PAD
    copies[0].wait()
    fill = jnp.full((mult, SLOT_PAD - cap), owned, jnp.int32)
    ids = jnp.concatenate([p for d in order for p in (edge_ref[d], fill)], axis=1)
    row = lax.broadcasted_iota(jnp.int32, (owned, slots), 0)
    weight = jnp.zeros((owned, slots), F32)
    count = jnp.zeros((1, slots), F32)
    for m in range(ids.shape[0]):
        weight += (row == ids[m:m + 1, :]).astype(F32)
        count += (ids[m:m + 1, :] < owned).astype(F32)
    pick = weight.T.astype(BF16)
    r = lax.broadcasted_iota(jnp.int32, (slots, slots), 0)
    c = lax.broadcasted_iota(jnp.int32, (slots, slots), 1)
    here = ((r & (SLOT_PAD - 1)) == cap) & ((c - (c & (SLOT_PAD - 1))) == (r - (r & (SLOT_PAD - 1))))
    spread = jnp.where(here, jnp.broadcast_to(count, (slots, slots)), 0.0).astype(BF16)
    c2 = lax.broadcasted_iota(jnp.int32, (slots, 128), 0)
    l2 = lax.broadcasted_iota(jnp.int32, (slots, 128), 1)
    fold = ((c2 & (SLOT_PAD - 1)) == l2).astype(BF16)
    counts = dot(spread, fold)
    copies[1].wait()
    feat = feat_ref[...]
    high = feat.astype(BF16)
    low = (feat - high.astype(F32)).astype(BF16)
    sums = dot(pick, high) + dot(pick, low)
    out_ref[...] = pack(sums, counts, cap)
    if with_own:
        copies[2].wait()
        write_own(plan, self_ref, *own_refs, trans_ref)


def neighbor_mean(cap, rows, recv, targets):
    slots = rows.shape[0]
    target = lax.broadcasted_iota(jnp.int32, (targets, slots), 0)
    onehot = (target == recv).astype(BF16)
    r = lax.broadcasted_iota(jnp.int32, (slots, slots), 0)
    c = lax.broadcasted_iota(jnp.int32, (slots, slots), 1)
    from_count = (c == (r - (r & (SLOT_PAD - 1)) + cap)).astype(BF16)
    copied = dot(from_count, rows[:, :128])
    r2 = lax.broadcasted_iota(jnp.int32, (slots, 128), 0)
    l2 = lax.broadcasted_iota(jnp.int32, (slots, 128), 1)
    counts = jnp.where((r2 & (SLOT_PAD - 1)) == l2, copied, 0.0).astype(BF16)
    number = jnp.sum(dot(onehot, counts), axis=1, keepdims=True)
    return (dot(onehot, rows) / jnp.maximum(number, 1.0)).astype(BF16)


def forward(preact, cot):
    sig = jax.nn.sigmoid(preact)
    hidden = (preact * sig).astype(BF16)
    grad = (cot.astype(F32) * (sig * (1.0 + preact * (1.0 - sig)))).astype(BF16)
    return hidden, grad


class Plan:
    def __init__(self, mesh, width, out_width):
        self.ns, self.nt = mesh.shape["store"], mesh.shape["trainer"]
        self.gx = 2 if self.ns % 2 == 0 else 1
        self.nz = self.ns // self.gx
        self.gc = 2
        self.gy = max(self.nt // self.gc, 1)
        self.shard = width // self.ns
        self.rows = self.nz * self.shard
        self.cols = out_width // self.gy
        self.peers = [(dx, dy) for dx in range(self.gx) for dy in range(self.gy)]

    def fits(self):
        pow2 = all((n & (n - 1)) == 0 for n in (self.ns, self.nt))
        return (pow2 and self.ns <= 8 and self.gx == 2 and self.gy == 2 and self.gy * self.gc == self.nt and self.cols % 128 == 0
                and self.shard % 16 == 0 and len(self.peers) <= 4 and self.nz == 4)

    def place(self):
        s, t = lax.axis_index("store"), lax.axis_index("trainer")
        return s // self.gx, s % self.gx, t // self.gc, t % self.gc

    def far(self):
        return list(range(2, self.nz))

    def near(self):
        return list(range(min(2, self.nz)))[::-1]

    def send(self, array, to):
        pairs = []
        for s in range(self.ns):
            for t in range(self.nt):
                z, x, y, c = to(s // self.gx, s % self.gx, t // self.gc, t % self.gc)
                pairs.append((s * self.nt + t, (z * self.gx + x) * self.nt + y * self.gc + c))
        return lax.ppermute(array, ("store", "trainer"), pairs)

    def store_order(self):
        middle = self.ns // 2
        pairs = list(zip(range(middle, self.ns), range(middle - 1, -1, -1)))
        return [s for pair in pairs[:-2] + pairs[:-3:-1] for s in pair]


def write_rows(plan, trans_ref, *outs):
    x = plan.place()[1]
    for dx, out in enumerate(outs):
        for z in range(plan.nz):
            start = pl.multiple_of((z * plan.gx + (x ^ dx)) * plan.shard, 16)
            out[z * plan.shard:(z + 1) * plan.shard, :] = trans_ref[pl.ds(start, plan.shard), :]


def write_own(plan, self_ref, own_ref, here_ref, there_ref, trans_ref):
    own_ref[...] = self_ref[...].astype(BF16)
    trans_ref[...] = self_ref[...].T.astype(BF16)
    write_rows(plan, trans_ref, here_ref, there_ref)


def mean_kernel(plan, cap, order, rows_ref, recv_ref, _, mean_ref, here_ref, there_ref, trans_ref):
    rows = unpack(rows_ref[...], order, cap, mean_ref.shape[1] // 128)
    targets = mean_ref.shape[0]
    fill = jnp.full((1, SLOT_PAD - cap), targets, jnp.int32)
    recv = jnp.concatenate([p for s in range(plan.ns) for p in (recv_ref[s:s + 1, :], fill)], axis=1)
    mean = neighbor_mean(cap, rows, recv, targets)
    mean_ref[...] = mean
    trans_ref[...] = mean.astype(F32).T.astype(BF16)
    write_rows(plan, trans_ref, here_ref, there_ref)


def layer_kernel(plan, mean_ref, self_ref, cot_ref, w_ref, hidden_ref, here_ref, there_ref, grad_ref):
    targets = self_ref.shape[0]
    preact = self_ref[...] + dot(mean_ref[...], w_ref[...])
    hidden, grad = forward(preact, cot_ref[...])
    hidden_ref[...] = hidden.astype(F32)
    for b in range(grad_ref.shape[0]):
        grad_ref[b] = grad[:, b * 128:(b + 1) * 128]
    y, each = plan.place()[2], plan.cols // 128
    for dy, out in enumerate((here_ref, there_ref)):
        for b in range(each):
            out[b * targets:(b + 1) * targets, :] = grad_ref[(y ^ dy) * each + b]


def left_kernel(plan, *refs):
    n = len(plan.peers)
    own, mean, outs = refs[n - 1::-1], refs[n:2 * n], refs[2 * n:]
    targets = own[0].shape[1]
    z, _, _, c = plan.place()
    keep_own = c == 0
    for i, (o, m) in enumerate(zip(own, mean)):
        at = slice(i * targets, (i + 1) * targets)
        for j, shards in enumerate((plan.far(), plan.near())):
            for r, k in enumerate(shards):
                rows = pl.ds(pl.multiple_of((z ^ k) * plan.shard, 16), plan.shard)
                to = slice(r * plan.shard, (r + 1) * plan.shard)
                outs[j][to, at] = jnp.where(keep_own, m[rows, :], o[rows, :])
                outs[2 + j][to, at] = jnp.where(keep_own, o[rows, :], m[rows, :])


def terms_kernel(left_ref, *refs):
    grad, out_ref = refs[:-1], refs[-1]
    targets = left_ref.shape[1] // len(grad)
    right = jnp.concatenate(
        [jnp.concatenate([g[b * targets:(b + 1) * targets, :] for b in range(grad[0].shape[0] // targets)], axis=1)
         for g in grad], axis=0)
    out_ref[...] = dot(left_ref[...], right).astype(out_ref.dtype)


def core_sum_kernel(plan, keep_ref, got_ref, *outs):
    for r, out in enumerate(outs):
        at = slice(r * plan.shard, (r + 1) * plan.shard)
        out[...] = (keep_ref[at, :] + got_ref[at, :].astype(F32)).astype(out.dtype)


def store_sum_kernel(*refs):
    total = refs[0][...]
    for r in refs[1:-1]:
        total += r[...].astype(F32)
    refs[-1][...] = total.astype(BF16)


def assemble_kernel(plan, *refs):
    parts, (self_ref, neigh_ref, both_ref) = refs[:-3], refs[-3:]
    _, _, y, c = plan.place()
    for i, part in enumerate(parts):
        cols = pl.ds(pl.multiple_of((y ^ (i // plan.gc)) * plan.cols, 128), plan.cols)
        both_ref[c ^ (i % plan.gc), :, cols] = part[...].astype(F32)
    self_ref[...] = both_ref[0]
    neigh_ref[...] = both_ref[1]


def per_device(plan, features, self_rows, edge_row, recv_target, cotangent, w_self, w_neigh):
    owned, width = features.shape
    out_width = w_self.shape[1]
    targets = self_rows.shape[0]
    ns, cap, mult = edge_row.shape[2:]
    slots = ns * SLOT_PAD
    edges = edge_row[0, 0].transpose(0, 2, 1)
    fits = plan.fits()
    order = plan.store_order() if fits else list(range(ns))
    rows, cols, n = plan.rows, plan.cols, len(plan.peers)
    scratch = [pltpu.VMEM(features.shape, F32), pltpu.VMEM(edges.shape, jnp.int32),
               pltpu.SemaphoreType.DMA((3,))]
    packed = pack_rows(cap, width)
    outs, more = [shape((ns * packed, 128), BF16)], []
    if fits:
        outs += [shape((targets, width), BF16)] + [shape((rows, targets), BF16)] * 2
        more = [self_rows]
        scratch += [pltpu.VMEM(self_rows.shape, F32), pltpu.VMEM((width, targets), BF16)]
    sums, *owns = call(
        functools.partial(slot_sums_kernel, plan, order), outs, (), hbm=[features, edges] + more,
        flops=4 * slots * owned * width, vmem=60 if fits else 16, scratch=scratch)
    arrived = lax.all_to_all(sums.reshape(ns, packed, 128), "store", split_axis=0, concat_axis=0,
                             tiled=True, axis_index_groups=[order]).reshape(ns * packed, 128)
    if not fits:
        own = self_rows.astype(BF16)
        recv = jnp.pad(recv_target[0, 0], ((0, 0), (0, SLOT_PAD - cap)), constant_values=targets).reshape(1, slots)
        mean = neighbor_mean(cap, unpack(arrived, order, cap, width // 128), recv, targets)
        preact = dot(own, w_self) + dot(mean, w_neigh)
        hidden, grad = forward(preact, cotangent)
        both = jnp.concatenate([own.T.reshape(ns, -1, targets), mean.T.reshape(ns, -1, targets)], axis=1)
        terms = dot(both.reshape(2 * width, targets), grad)
        part = lax.psum_scatter(terms, "store", scatter_dimension=0, tiled=True)
        total = lax.psum(part, "trainer")
        return hidden, total[:plan.shard], total[plan.shard:]

    def to_x(array):
        return plan.send(array, lambda z, x, y, c: (z, 1 - x, y, c))

    def to_y(array):
        return plan.send(array, lambda z, x, y, c: (z, x, 1 - y, c))

    def to_diagonal(array):
        return plan.send(array, lambda z, x, y, c: (z, 1 - x, 1 - y, c))

    def held(array, *until):
        return lax.optimization_barrier((array,) + until)[0]

    own, own_here, own_there = owns
    own_all = [own_here, to_y(own_here), to_x(own_there), to_diagonal(own_there)]
    self_term = dot(own, w_self)

    mean, mean_here, mean_there = call(
        functools.partial(mean_kernel, plan, cap, order),
        [shape((targets, width), BF16)] + [shape((rows, targets), BF16)] * 2, [arrived, recv_target[0, 0], self_term],
        scratch=[pltpu.VMEM((width, targets), BF16)], flops=2 * targets * width * slots)
    hidden, grad_here, grad_there = call(
        functools.partial(layer_kernel, plan),
        [shape((targets, out_width), F32)] + [shape((cols // 128 * targets, 128), BF16)] * 2,
        [mean, self_term, cotangent, w_neigh],
        scratch=[pltpu.VMEM((out_width // 128, targets, 128), BF16)],
        flops=2 * targets * width * out_width)
    mean_x, grad_y = to_x(mean_there), to_y(grad_there)
    grad_x = to_x(grad_here)
    mean_all = [mean_here, to_y(mean_here), mean_x, to_y(held(mean_x, *own_all[1:]))]
    grad_all = [grad_here, grad_y, grad_x, to_x(held(grad_y, mean_x, *own_all[1:]))]
    def to_core(array):
        return plan.send(array, lambda z, x, y, c: (z, x, y, 1 - c))

    def to_z(array, k):
        return plan.send(array, lambda z, x, y, c: (z ^ k, x, y, c))

    def terms(left, kind):
        return call(terms_kernel, [shape((left.shape[0], cols), kind)], [left] + grad_all,
                    flops=2 * left.shape[0] * cols * targets * n)[0]

    block = (plan.shard, cols)
    halves = [plan.far(), plan.near()]
    lefts = call(functools.partial(left_kernel, plan),
                 [shape((len(half) * plan.shard, n * targets), BF16) for half in halves * 2],
                 own_all[::-1] + mean_all)
    got, mine = [], None
    for half, give_left, keep_left in zip(halves, lefts[:2], lefts[2:]):
        came = to_core(terms(give_left, BF16))
        sums = call(functools.partial(core_sum_kernel, plan),
                    [shape(block, BF16 if k else F32) for k in half], [terms(keep_left, F32), came])
        for k, part in zip(half, sums):
            if k:
                got.append(to_z(part, k))
            else:
                mine = part
    (quarter,) = call(store_sum_kernel, [shape(block, BF16)], [mine] + got)
    column = [quarter] + [plan.send(quarter, lambda z, x, y, c, i=i: (z, x, y ^ i, c))
                          for i in range(1, plan.gy)]
    quarters = [q for part in column
                for q in (part, plan.send(part, lambda z, x, y, c: (z, x, y, 1 - c)))]
    grads = call(functools.partial(assemble_kernel, plan),
                 [shape((plan.shard, out_width), F32)] * 2, quarters,
                 scratch=[pltpu.VMEM((2, plan.shard, out_width), F32)])
    return hidden.astype(BF16), grads[0], grads[1]


def solution(mesh):
    in_specs = (
        P("store", None),
        P(("store", "trainer"), None),
        P("trainer", "store", None, None, None),
        P("trainer", "store", None, None),
        P(("store", "trainer"), None),
        P(),
        P(),
    )
    out_specs = (P(("store", "trainer"), None), P("store", None), P("store", None))

    def run(features, self_rows, edge_row, recv_target, cotangent, w_self, w_neigh):
        plan = Plan(mesh, features.shape[1], w_self.shape[1])
        return jax.shard_map(
            functools.partial(per_device, plan), mesh=mesh, in_specs=in_specs,
            out_specs=out_specs, check_vma=False,
        )(features, self_rows, edge_row, recv_target, cotangent, w_self, w_neigh)

    return run
```

```python
import functools

import jax
import jax.numpy as jnp
from jax import lax
from jax.experimental import pallas as pl
from jax.experimental.pallas import tpu as pltpu
from jax.sharding import PartitionSpec as P

BF16, F32 = jnp.bfloat16, jnp.float32
SLOT_PAD = 16
VMEM = pl.BlockSpec(memory_space=pltpu.VMEM)
ANY = pl.BlockSpec(memory_space=pl.ANY)
HBM = pl.BlockSpec(memory_space=pltpu.HBM)


def dot(a, b):
    return jnp.dot(a, b, preferred_element_type=F32)


def call(body, outs, args, unread=(), hbm=(), scratch=(), flops=0, vmem=16):
    moved = sum(a.size * a.dtype.itemsize for a in (*args, *outs))
    return pl.pallas_call(
        body,
        out_shape=list(outs),
        in_specs=[VMEM] * len(args) + [ANY] * len(unread) + [HBM] * len(hbm),
        out_specs=[VMEM] * len(outs),
        scratch_shapes=list(scratch),
        compiler_params=pltpu.CompilerParams(vmem_limit_bytes=vmem * 1024 * 1024),
        cost_estimate=pl.CostEstimate(flops=flops, bytes_accessed=moved, transcendentals=0),
    )(*args, *unread, *hbm)


def shape(dims, kind):
    return jax.ShapeDtypeStruct(dims, kind)


def pack_rows(cap, width):
    return cap * (width // 128) + 8


def pack(sums, counts, cap):
    blocks = sums.shape[1] // 128
    out = []
    for d in range(sums.shape[0] // SLOT_PAD):
        at = d * SLOT_PAD
        part = [sums[at:at + SLOT_PAD, j * 128:(j + 1) * 128] for j in range(blocks)]
        out += [p[:8] for p in part]
        out += [jnp.concatenate([part[j][8:cap], part[j + 1][8:cap]], axis=0) for j in range(0, blocks, 2)]
        out.append(counts[at + 8:at + SLOT_PAD])
    return jnp.concatenate(out, axis=0).astype(BF16)


def unpack(packed, order, cap, blocks):
    size = packed.shape[0] // len(order)
    rows = []
    for s in range(len(order)):
        at = order.index(s) * size
        part = packed[at:at + size, :].astype(F32)
        tail, counts = part[blocks * 8:size - 8], part[size - 8:]
        columns = []
        for j in range(blocks):
            low = tail[j // 2 * 8 + j % 2 * 4:j // 2 * 8 + j % 2 * 4 + 4]
            rest = counts[4:] if j == 0 else jnp.zeros((4, 128), F32)
            columns.append(jnp.concatenate([part[j * 8:j * 8 + 8], low, rest], axis=0))
        rows.append(jnp.concatenate(columns, axis=1))
    return jnp.concatenate(rows, axis=0).astype(BF16)


def slot_sums_kernel(plan, order, feat_hbm, edge_hbm, *rest):
    with_own = len(rest) > 4
    if with_own:
        self_hbm, out_ref, *own_refs, feat_ref, edge_ref, sems, self_ref, trans_ref = rest
    else:
        out_ref, feat_ref, edge_ref, sems = rest
    copies = [pltpu.make_async_copy(edge_hbm, edge_ref, sems.at[0]),
              pltpu.make_async_copy(feat_hbm, feat_ref, sems.at[1])]
    if with_own:
        copies.append(pltpu.make_async_copy(self_hbm, self_ref, sems.at[2]))
    for copy in copies:
        copy.start()
    owned = feat_ref.shape[0]
    _, mult, cap = edge_ref.shape
    slots = len(order) * SLOT_PAD
    copies[0].wait()
    fill = jnp.full((mult, SLOT_PAD - cap), owned, jnp.int32)
    ids = jnp.concatenate([p for d in order for p in (edge_ref[d], fill)], axis=1)
    row = lax.broadcasted_iota(jnp.int32, (owned, slots), 0)
    weight = jnp.zeros((owned, slots), F32)
    count = jnp.zeros((1, slots), F32)
    for m in range(ids.shape[0]):
        weight += (row == ids[m:m + 1, :]).astype(F32)
        count += (ids[m:m + 1, :] < owned).astype(F32)
    pick = weight.T.astype(BF16)
    r = lax.broadcasted_iota(jnp.int32, (slots, slots), 0)
    c = lax.broadcasted_iota(jnp.int32, (slots, slots), 1)
    here = ((r & (SLOT_PAD - 1)) == cap) & ((c - (c & (SLOT_PAD - 1))) == (r - (r & (SLOT_PAD - 1))))
    spread = jnp.where(here, jnp.broadcast_to(count, (slots, slots)), 0.0).astype(BF16)
    c2 = lax.broadcasted_iota(jnp.int32, (slots, 128), 0)
    l2 = lax.broadcasted_iota(jnp.int32, (slots, 128), 1)
    fold = ((c2 & (SLOT_PAD - 1)) == l2).astype(BF16)
    counts = dot(spread, fold)
    copies[1].wait()
    feat = feat_ref[...]
    high = feat.astype(BF16)
    low = (feat - high.astype(F32)).astype(BF16)
    sums = dot(pick, high) + dot(pick, low)
    out_ref[...] = pack(sums, counts, cap)
    if with_own:
        copies[2].wait()
        write_own(plan, self_ref, *own_refs, trans_ref)


def neighbor_mean(cap, rows, recv, targets):
    slots = rows.shape[0]
    target = lax.broadcasted_iota(jnp.int32, (targets, slots), 0)
    onehot = (target == recv).astype(BF16)
    r = lax.broadcasted_iota(jnp.int32, (slots, slots), 0)
    c = lax.broadcasted_iota(jnp.int32, (slots, slots), 1)
    from_count = (c == (r - (r & (SLOT_PAD - 1)) + cap)).astype(BF16)
    copied = dot(from_count, rows[:, :128])
    r2 = lax.broadcasted_iota(jnp.int32, (slots, 128), 0)
    l2 = lax.broadcasted_iota(jnp.int32, (slots, 128), 1)
    counts = jnp.where((r2 & (SLOT_PAD - 1)) == l2, copied, 0.0).astype(BF16)
    number = jnp.sum(dot(onehot, counts), axis=1, keepdims=True)
    return (dot(onehot, rows) / jnp.maximum(number, 1.0)).astype(BF16)


def forward(preact, cot):
    sig = jax.nn.sigmoid(preact)
    hidden = (preact * sig).astype(BF16)
    grad = (cot.astype(F32) * (sig * (1.0 + preact * (1.0 - sig)))).astype(BF16)
    return hidden, grad


class Plan:
    def __init__(self, mesh, width, out_width):
        self.ns, self.nt = mesh.shape["store"], mesh.shape["trainer"]
        self.gx = 2 if self.ns % 2 == 0 else 1
        self.nz = self.ns // self.gx
        self.gc = 2
        self.gy = max(self.nt // self.gc, 1)
        self.shard = width // self.ns
        self.rows = self.nz * self.shard
        self.cols = out_width // self.gy
        self.peers = [(dx, dy) for dx in range(self.gx) for dy in range(self.gy)]

    def fits(self):
        pow2 = all((n & (n - 1)) == 0 for n in (self.ns, self.nt))
        return (pow2 and self.ns <= 8 and self.gx == 2 and self.gy == 2 and self.gy * self.gc == self.nt and self.cols % 128 == 0
                and self.shard % 16 == 0 and len(self.peers) <= 4 and self.nz == 4)

    def place(self):
        s, t = lax.axis_index("store"), lax.axis_index("trainer")
        return s // self.gx, s % self.gx, t // self.gc, t % self.gc

    def far(self):
        return list(range(2, self.nz))[::-1]

    def near(self):
        return list(range(min(2, self.nz)))[::-1]

    def send(self, array, to):
        pairs = []
        for s in range(self.ns):
            for t in range(self.nt):
                z, x, y, c = to(s // self.gx, s % self.gx, t // self.gc, t % self.gc)
                pairs.append((s * self.nt + t, (z * self.gx + x) * self.nt + y * self.gc + c))
        return lax.ppermute(array, ("store", "trainer"), pairs)

    def store_order(self):
        middle = self.ns // 2
        turns = [s for pair in zip(range(middle, self.ns), range(middle - 1, -1, -1)) for s in pair]
        return turns


def write_rows(plan, trans_ref, *outs):
    x = plan.place()[1]
    for dx, out in enumerate(outs):
        for z in range(plan.nz):
            start = pl.multiple_of((z * plan.gx + (x ^ dx)) * plan.shard, 16)
            out[z * plan.shard:(z + 1) * plan.shard, :] = trans_ref[pl.ds(start, plan.shard), :]


def write_own(plan, self_ref, own_ref, here_ref, there_ref, trans_ref):
    own_ref[...] = self_ref[...].astype(BF16)
    trans_ref[...] = self_ref[...].T.astype(BF16)
    write_rows(plan, trans_ref, here_ref, there_ref)


def mean_kernel(plan, cap, order, rows_ref, recv_ref, _, mean_ref, here_ref, there_ref, trans_ref):
    rows = unpack(rows_ref[...], order, cap, mean_ref.shape[1] // 128)
    targets = mean_ref.shape[0]
    fill = jnp.full((1, SLOT_PAD - cap), targets, jnp.int32)
    recv = jnp.concatenate([p for s in range(plan.ns) for p in (recv_ref[s:s + 1, :], fill)], axis=1)
    mean = neighbor_mean(cap, rows, recv, targets)
    mean_ref[...] = mean
    trans_ref[...] = mean.astype(F32).T.astype(BF16)
    write_rows(plan, trans_ref, here_ref, there_ref)


def layer_kernel(plan, mean_ref, self_ref, cot_ref, w_ref, hidden_ref, here_ref, there_ref, grad_ref):
    targets = self_ref.shape[0]
    preact = self_ref[...] + dot(mean_ref[...], w_ref[...])
    hidden, grad = forward(preact, cot_ref[...])
    hidden_ref[...] = hidden.astype(F32)
    for b in range(grad_ref.shape[0]):
        grad_ref[b] = grad[:, b * 128:(b + 1) * 128]
    y, each = plan.place()[2], plan.cols // 128
    for dy, out in enumerate((here_ref, there_ref)):
        for b in range(each):
            out[b * targets:(b + 1) * targets, :] = grad_ref[(y ^ dy) * each + b]


def left_kernel(plan, *refs):
    n = len(plan.peers)
    own, mean, outs = refs[n - 1::-1], refs[n:2 * n], refs[2 * n:]
    targets = own[0].shape[1]
    z, _, _, c = plan.place()
    keep_own = c == 0
    for i, (o, m) in enumerate(zip(own, mean)):
        at = slice(i * targets, (i + 1) * targets)
        for j, shards in enumerate((plan.far(), plan.near())):
            for r, k in enumerate(shards):
                rows = pl.ds(pl.multiple_of((z ^ k) * plan.shard, 16), plan.shard)
                to = slice(r * plan.shard, (r + 1) * plan.shard)
                outs[j][to, at] = jnp.where(keep_own, m[rows, :], o[rows, :])
                outs[2 + j][to, at] = jnp.where(keep_own, o[rows, :], m[rows, :])


def terms_kernel(left_ref, *refs):
    grad, out_ref = refs[:-1], refs[-1]
    targets = left_ref.shape[1] // len(grad)
    right = jnp.concatenate(
        [jnp.concatenate([g[b * targets:(b + 1) * targets, :] for b in range(grad[0].shape[0] // targets)], axis=1)
         for g in grad], axis=0)
    out_ref[...] = dot(left_ref[...], right).astype(out_ref.dtype)


def core_sum_kernel(plan, keep_ref, got_ref, *outs):
    for r, out in enumerate(outs):
        at = slice(r * plan.shard, (r + 1) * plan.shard)
        out[...] = (keep_ref[at, :] + got_ref[at, :].astype(F32)).astype(out.dtype)


def store_sum_kernel(*refs):
    total = refs[0][...]
    for r in refs[1:-1]:
        total += r[...].astype(F32)
    refs[-1][...] = total.astype(BF16)


def assemble_kernel(plan, *refs):
    parts, (self_ref, neigh_ref, both_ref) = refs[:-3], refs[-3:]
    _, _, y, c = plan.place()
    for i, part in enumerate(parts):
        cols = pl.ds(pl.multiple_of((y ^ (i // plan.gc)) * plan.cols, 128), plan.cols)
        both_ref[c ^ (i % plan.gc), :, cols] = part[...].astype(F32)
    self_ref[...] = both_ref[0]
    neigh_ref[...] = both_ref[1]


def per_device(plan, features, self_rows, edge_row, recv_target, cotangent, w_self, w_neigh):
    owned, width = features.shape
    out_width = w_self.shape[1]
    targets = self_rows.shape[0]
    ns, cap, mult = edge_row.shape[2:]
    slots = ns * SLOT_PAD
    edges = edge_row[0, 0].transpose(0, 2, 1)
    fits = plan.fits()
    order = plan.store_order() if fits else list(range(ns))
    rows, cols, n = plan.rows, plan.cols, len(plan.peers)
    scratch = [pltpu.VMEM(features.shape, F32), pltpu.VMEM(edges.shape, jnp.int32),
               pltpu.SemaphoreType.DMA((3,))]
    packed = pack_rows(cap, width)
    outs, more = [shape((ns * packed, 128), BF16)], []
    if fits:
        outs += [shape((targets, width), BF16)] + [shape((rows, targets), BF16)] * 2
        more = [self_rows]
        scratch += [pltpu.VMEM(self_rows.shape, F32), pltpu.VMEM((width, targets), BF16)]
    sums, *owns = call(
        functools.partial(slot_sums_kernel, plan, order), outs, (), hbm=[features, edges] + more,
        flops=4 * slots * owned * width, vmem=60 if fits else 16, scratch=scratch)
    arrived = lax.all_to_all(sums.reshape(ns, packed, 128), "store", split_axis=0, concat_axis=0,
                             tiled=True, axis_index_groups=[order]).reshape(ns * packed, 128)
    if not fits:
        own = self_rows.astype(BF16)
        recv = jnp.pad(recv_target[0, 0], ((0, 0), (0, SLOT_PAD - cap)), constant_values=targets).reshape(1, slots)
        mean = neighbor_mean(cap, unpack(arrived, order, cap, width // 128), recv, targets)
        preact = dot(own, w_self) + dot(mean, w_neigh)
        hidden, grad = forward(preact, cotangent)
        both = jnp.concatenate([own.T.reshape(ns, -1, targets), mean.T.reshape(ns, -1, targets)], axis=1)
        terms = dot(both.reshape(2 * width, targets), grad)
        part = lax.psum_scatter(terms, "store", scatter_dimension=0, tiled=True)
        total = lax.psum(part, "trainer")
        return hidden, total[:plan.shard], total[plan.shard:]

    def to_x(array):
        return plan.send(array, lambda z, x, y, c: (z, 1 - x, y, c))

    def to_y(array):
        return plan.send(array, lambda z, x, y, c: (z, x, 1 - y, c))

    def to_diagonal(array):
        return plan.send(array, lambda z, x, y, c: (z, 1 - x, 1 - y, c))

    def held(array, *until):
        return lax.optimization_barrier((array,) + until)[0]

    own, own_here, own_there = owns
    own_all = [own_here, to_y(own_here), to_x(own_there), to_diagonal(own_there)]
    self_term = dot(own, w_self)

    mean, mean_here, mean_there = call(
        functools.partial(mean_kernel, plan, cap, order),
        [shape((targets, width), BF16)] + [shape((rows, targets), BF16)] * 2, [arrived, recv_target[0, 0], self_term],
        scratch=[pltpu.VMEM((width, targets), BF16)], flops=2 * targets * width * slots)
    hidden, grad_here, grad_there = call(
        functools.partial(layer_kernel, plan),
        [shape((targets, out_width), F32)] + [shape((cols // 128 * targets, 128), BF16)] * 2,
        [mean, self_term, cotangent, w_neigh],
        scratch=[pltpu.VMEM((out_width // 128, targets, 128), BF16)],
        flops=2 * targets * width * out_width)
    mean_x, grad_y = to_x(mean_there), to_y(grad_there)
    grad_x = to_x(grad_here)
    mean_all = [mean_here, to_y(mean_here), mean_x, to_y(held(mean_x, *own_all[1:]))]
    grad_all = [grad_here, grad_y, grad_x, to_x(held(grad_y, mean_x, *own_all[1:]))]
    def to_core(array):
        return plan.send(array, lambda z, x, y, c: (z, x, y, 1 - c))

    def to_z(array, k):
        return plan.send(array, lambda z, x, y, c: (z ^ k, x, y, c))

    def terms(left, kind):
        return call(terms_kernel, [shape((left.shape[0], cols), kind)], [left] + grad_all,
                    flops=2 * left.shape[0] * cols * targets * n)[0]

    block = (plan.shard, cols)
    halves = [plan.far(), plan.near()]
    lefts = call(functools.partial(left_kernel, plan),
                 [shape((len(half) * plan.shard, n * targets), BF16) for half in halves * 2],
                 own_all[::-1] + mean_all)
    got, mine, earlier = [], None, None
    for half, give_left, keep_left in zip(halves, lefts[:2], lefts[2:]):
        came = to_core(terms(give_left, BF16))
        if earlier is not None:
            keep_left = held(keep_left, earlier)
        earlier = came
        sums = call(functools.partial(core_sum_kernel, plan),
                    [shape(block, BF16 if k else F32) for k in half], [terms(keep_left, F32), came])
        for k, part in zip(half, sums):
            if k:
                got.append(to_z(part, k))
            else:
                mine = part
    (quarter,) = call(store_sum_kernel, [shape(block, BF16)], [mine] + got)
    column = [quarter] + [plan.send(quarter, lambda z, x, y, c, i=i: (z, x, y ^ i, c))
                          for i in range(1, plan.gy)]
    quarters = [q for part in column
                for q in (part, plan.send(part, lambda z, x, y, c: (z, x, y, 1 - c)))]
    grads = call(functools.partial(assemble_kernel, plan),
                 [shape((plan.shard, out_width), F32)] * 2, quarters,
                 scratch=[pltpu.VMEM((2, plan.shard, out_width), F32)])
    return hidden.astype(BF16), grads[0], grads[1]


def solution(mesh):
    in_specs = (
        P("store", None),
        P(("store", "trainer"), None),
        P("trainer", "store", None, None, None),
        P("trainer", "store", None, None),
        P(("store", "trainer"), None),
        P(),
        P(),
    )
    out_specs = (P(("store", "trainer"), None), P("store", None), P("store", None))

    def run(features, self_rows, edge_row, recv_target, cotangent, w_self, w_neigh):
        plan = Plan(mesh, features.shape[1], w_self.shape[1])
        return jax.shard_map(
            functools.partial(per_device, plan), mesh=mesh, in_specs=in_specs,
            out_specs=out_specs, check_vma=False,
        )(features, self_rows, edge_row, recv_target, cotangent, w_self, w_neigh)

    return run
```

```python
import functools

import jax
import jax.numpy as jnp
from jax import lax
from jax.experimental import pallas as pl
from jax.experimental.pallas import tpu as pltpu
from jax.sharding import PartitionSpec as P

BF16, F32 = jnp.bfloat16, jnp.float32
SLOT_PAD = 16
VMEM = pl.BlockSpec(memory_space=pltpu.VMEM)
ANY = pl.BlockSpec(memory_space=pl.ANY)
HBM = pl.BlockSpec(memory_space=pltpu.HBM)


def dot(a, b):
    return jnp.dot(a, b, preferred_element_type=F32)


def call(body, outs, args, unread=(), hbm=(), scratch=(), flops=0, vmem=16):
    moved = sum(a.size * a.dtype.itemsize for a in (*args, *outs))
    return pl.pallas_call(
        body,
        out_shape=list(outs),
        in_specs=[VMEM] * len(args) + [ANY] * len(unread) + [HBM] * len(hbm),
        out_specs=[VMEM] * len(outs),
        scratch_shapes=list(scratch),
        compiler_params=pltpu.CompilerParams(vmem_limit_bytes=vmem * 1024 * 1024),
        cost_estimate=pl.CostEstimate(flops=flops, bytes_accessed=moved, transcendentals=0),
    )(*args, *unread, *hbm)


def shape(dims, kind):
    return jax.ShapeDtypeStruct(dims, kind)


def pack_rows(cap, width):
    return cap * (width // 128) + 8


def pack(sums, counts, cap):
    blocks = sums.shape[1] // 128
    out = []
    for d in range(sums.shape[0] // SLOT_PAD):
        at = d * SLOT_PAD
        part = [sums[at:at + SLOT_PAD, j * 128:(j + 1) * 128] for j in range(blocks)]
        out += [p[:8] for p in part]
        out += [jnp.concatenate([part[j][8:cap], part[j + 1][8:cap]], axis=0) for j in range(0, blocks, 2)]
        out.append(counts[at + 8:at + SLOT_PAD])
    return jnp.concatenate(out, axis=0).astype(BF16)


def unpack(packed, order, cap, blocks):
    size = packed.shape[0] // len(order)
    rows = []
    for s in range(len(order)):
        at = order.index(s) * size
        part = packed[at:at + size, :].astype(F32)
        tail, counts = part[blocks * 8:size - 8], part[size - 8:]
        columns = []
        for j in range(blocks):
            low = tail[j // 2 * 8 + j % 2 * 4:j // 2 * 8 + j % 2 * 4 + 4]
            rest = counts[4:] if j == 0 else jnp.zeros((4, 128), F32)
            columns.append(jnp.concatenate([part[j * 8:j * 8 + 8], low, rest], axis=0))
        rows.append(jnp.concatenate(columns, axis=1))
    return jnp.concatenate(rows, axis=0).astype(BF16)


def slot_sums_kernel(plan, order, feat_hbm, edge_hbm, *rest):
    with_own = len(rest) > 4
    if with_own:
        self_hbm, out_ref, *own_refs, feat_ref, edge_ref, sems, self_ref, trans_ref = rest
    else:
        out_ref, feat_ref, edge_ref, sems = rest
    copies = [pltpu.make_async_copy(edge_hbm, edge_ref, sems.at[0]),
              pltpu.make_async_copy(feat_hbm, feat_ref, sems.at[1])]
    if with_own:
        copies.append(pltpu.make_async_copy(self_hbm, self_ref, sems.at[2]))
    for copy in copies:
        copy.start()
    owned = feat_ref.shape[0]
    _, mult, cap = edge_ref.shape
    slots = len(order) * SLOT_PAD
    copies[0].wait()
    fill = jnp.full((mult, SLOT_PAD - cap), owned, jnp.int32)
    ids = jnp.concatenate([p for d in order for p in (edge_ref[d], fill)], axis=1)
    row = lax.broadcasted_iota(jnp.int32, (owned, slots), 0)
    weight = jnp.zeros((owned, slots), F32)
    count = jnp.zeros((1, slots), F32)
    for m in range(ids.shape[0]):
        weight += (row == ids[m:m + 1, :]).astype(F32)
        count += (ids[m:m + 1, :] < owned).astype(F32)
    pick = weight.T.astype(BF16)
    r = lax.broadcasted_iota(jnp.int32, (slots, slots), 0)
    c = lax.broadcasted_iota(jnp.int32, (slots, slots), 1)
    here = ((r & (SLOT_PAD - 1)) == cap) & ((c - (c & (SLOT_PAD - 1))) == (r - (r & (SLOT_PAD - 1))))
    spread = jnp.where(here, jnp.broadcast_to(count, (slots, slots)), 0.0).astype(BF16)
    c2 = lax.broadcasted_iota(jnp.int32, (slots, 128), 0)
    l2 = lax.broadcasted_iota(jnp.int32, (slots, 128), 1)
    fold = ((c2 & (SLOT_PAD - 1)) == l2).astype(BF16)
    counts = dot(spread, fold)
    copies[1].wait()
    feat = feat_ref[...]
    high = feat.astype(BF16)
    low = (feat - high.astype(F32)).astype(BF16)
    sums = dot(pick, high) + dot(pick, low)
    out_ref[...] = pack(sums, counts, cap)
    if with_own:
        copies[2].wait()
        write_own(plan, self_ref, *own_refs, trans_ref)


def neighbor_mean(cap, rows, recv, targets):
    slots = rows.shape[0]
    target = lax.broadcasted_iota(jnp.int32, (targets, slots), 0)
    onehot = (target == recv).astype(BF16)
    r = lax.broadcasted_iota(jnp.int32, (slots, slots), 0)
    c = lax.broadcasted_iota(jnp.int32, (slots, slots), 1)
    from_count = (c == (r - (r & (SLOT_PAD - 1)) + cap)).astype(BF16)
    copied = dot(from_count, rows[:, :128])
    r2 = lax.broadcasted_iota(jnp.int32, (slots, 128), 0)
    l2 = lax.broadcasted_iota(jnp.int32, (slots, 128), 1)
    counts = jnp.where((r2 & (SLOT_PAD - 1)) == l2, copied, 0.0).astype(BF16)
    number = jnp.sum(dot(onehot, counts), axis=1, keepdims=True)
    return (dot(onehot, rows) / jnp.maximum(number, 1.0)).astype(BF16)


def forward(preact, cot):
    sig = jax.nn.sigmoid(preact)
    hidden = (preact * sig).astype(BF16)
    grad = (cot.astype(F32) * (sig * (1.0 + preact * (1.0 - sig)))).astype(BF16)
    return hidden, grad


class Plan:
    def __init__(self, mesh, width, out_width):
        self.ns, self.nt = mesh.shape["store"], mesh.shape["trainer"]
        self.gx = 2 if self.ns % 2 == 0 else 1
        self.nz = self.ns // self.gx
        self.gc = 2
        self.gy = max(self.nt // self.gc, 1)
        self.shard = width // self.ns
        self.rows = self.nz * self.shard
        self.cols = out_width // self.gy
        self.peers = [(dx, dy) for dx in range(self.gx) for dy in range(self.gy)]

    def fits(self):
        pow2 = all((n & (n - 1)) == 0 for n in (self.ns, self.nt))
        return (pow2 and self.ns <= 8 and self.gx == 2 and self.gy == 2 and self.gy * self.gc == self.nt and self.cols % 128 == 0
                and self.shard % 16 == 0 and len(self.peers) <= 4 and self.nz == 4)

    def place(self):
        s, t = lax.axis_index("store"), lax.axis_index("trainer")
        return s // self.gx, s % self.gx, t // self.gc, t % self.gc

    def far(self):
        return list(range(2, self.nz))[::-1]

    def near(self):
        return list(range(min(2, self.nz)))[::-1]

    def send(self, array, to):
        pairs = []
        for s in range(self.ns):
            for t in range(self.nt):
                z, x, y, c = to(s // self.gx, s % self.gx, t // self.gc, t % self.gc)
                pairs.append((s * self.nt + t, (z * self.gx + x) * self.nt + y * self.gc + c))
        return lax.ppermute(array, ("store", "trainer"), pairs)

    def store_order(self):
        middle = self.ns // 2
        turns = [s for pair in zip(range(middle, self.ns), range(middle - 1, -1, -1)) for s in pair]
        return turns


def write_rows(plan, trans_ref, *outs):
    x = plan.place()[1]
    for dx, out in enumerate(outs):
        for z in range(plan.nz):
            start = pl.multiple_of((z * plan.gx + (x ^ dx)) * plan.shard, 16)
            out[z * plan.shard:(z + 1) * plan.shard, :] = trans_ref[pl.ds(start, plan.shard), :]


def write_own(plan, self_ref, own_ref, here_ref, there_ref, trans_ref):
    own_ref[...] = self_ref[...].astype(BF16)
    trans_ref[...] = self_ref[...].T.astype(BF16)
    write_rows(plan, trans_ref, here_ref, there_ref)


def mean_kernel(plan, cap, order, rows_ref, recv_ref, _, mean_ref, here_ref, there_ref, trans_ref):
    rows = unpack(rows_ref[...], order, cap, mean_ref.shape[1] // 128)
    targets = mean_ref.shape[0]
    fill = jnp.full((1, SLOT_PAD - cap), targets, jnp.int32)
    recv = jnp.concatenate([p for s in range(plan.ns) for p in (recv_ref[s:s + 1, :], fill)], axis=1)
    mean = neighbor_mean(cap, rows, recv, targets)
    mean_ref[...] = mean
    trans_ref[...] = mean.astype(F32).T.astype(BF16)
    write_rows(plan, trans_ref, here_ref, there_ref)


def layer_kernel(plan, mean_ref, self_ref, cot_ref, w_ref, hidden_ref, here_ref, there_ref, grad_ref):
    targets = self_ref.shape[0]
    preact = self_ref[...] + dot(mean_ref[...], w_ref[...])
    hidden, grad = forward(preact, cot_ref[...])
    hidden_ref[...] = hidden.astype(F32)
    for b in range(grad_ref.shape[0]):
        grad_ref[b] = grad[:, b * 128:(b + 1) * 128]
    y, each = plan.place()[2], plan.cols // 128
    for dy, out in enumerate((here_ref, there_ref)):
        for b in range(each):
            out[b * targets:(b + 1) * targets, :] = grad_ref[(y ^ dy) * each + b]


def left_kernel(plan, *refs):
    n = len(plan.peers)
    own, mean, outs = refs[n - 1::-1], refs[n:2 * n], refs[2 * n:]
    targets = own[0].shape[1]
    z, _, _, c = plan.place()
    keep_own = c == 0
    for i, (o, m) in enumerate(zip(own, mean)):
        at = slice(i * targets, (i + 1) * targets)
        for j, shards in enumerate((plan.far(), plan.near())):
            for r, k in enumerate(shards):
                rows = pl.ds(pl.multiple_of((z ^ k) * plan.shard, 16), plan.shard)
                to = slice(r * plan.shard, (r + 1) * plan.shard)
                outs[j][to, at] = jnp.where(keep_own, m[rows, :], o[rows, :])
                outs[2 + j][to, at] = jnp.where(keep_own, o[rows, :], m[rows, :])


def right_factor(grad, targets):
    return jnp.concatenate(
        [jnp.concatenate([g[b * targets:(b + 1) * targets, :] for b in range(g.shape[0] // targets)], axis=1)
         for g in grad], axis=0)


def first_terms_kernel(targets, left_ref, *refs):
    grad, out_ref = refs[:-1], refs[-1]
    out_ref[...] = dot(left_ref[:, :len(grad) * targets], right_factor(grad, targets))


def last_terms_kernel(targets, left_ref, first_ref, grad_ref, out_ref):
    last = dot(left_ref[:, left_ref.shape[1] - targets:], right_factor([grad_ref], targets))
    out_ref[...] = (first_ref[...] + last).astype(out_ref.dtype)


def core_sum_kernel(plan, keep_ref, got_ref, *outs):
    for r, out in enumerate(outs):
        at = slice(r * plan.shard, (r + 1) * plan.shard)
        out[...] = (keep_ref[at, :] + got_ref[at, :].astype(F32)).astype(out.dtype)


def store_sum_kernel(*refs):
    total = refs[0][...]
    for r in refs[1:-1]:
        total += r[...].astype(F32)
    refs[-1][...] = total.astype(BF16)


def assemble_kernel(plan, *refs):
    parts, (self_ref, neigh_ref, both_ref) = refs[:-3], refs[-3:]
    _, _, y, c = plan.place()
    for i, part in enumerate(parts):
        cols = pl.ds(pl.multiple_of((y ^ (i // plan.gc)) * plan.cols, 128), plan.cols)
        both_ref[c ^ (i % plan.gc), :, cols] = part[...].astype(F32)
    self_ref[...] = both_ref[0]
    neigh_ref[...] = both_ref[1]


def per_device(plan, features, self_rows, edge_row, recv_target, cotangent, w_self, w_neigh):
    owned, width = features.shape
    out_width = w_self.shape[1]
    targets = self_rows.shape[0]
    ns, cap, mult = edge_row.shape[2:]
    slots = ns * SLOT_PAD
    edges = edge_row[0, 0].transpose(0, 2, 1)
    fits = plan.fits()
    order = plan.store_order() if fits else list(range(ns))
    rows, cols, n = plan.rows, plan.cols, len(plan.peers)
    scratch = [pltpu.VMEM(features.shape, F32), pltpu.VMEM(edges.shape, jnp.int32),
               pltpu.SemaphoreType.DMA((3,))]
    packed = pack_rows(cap, width)
    outs, more = [shape((ns * packed, 128), BF16)], []
    if fits:
        outs += [shape((targets, width), BF16)] + [shape((rows, targets), BF16)] * 2
        more = [self_rows]
        scratch += [pltpu.VMEM(self_rows.shape, F32), pltpu.VMEM((width, targets), BF16)]
    sums, *owns = call(
        functools.partial(slot_sums_kernel, plan, order), outs, (), hbm=[features, edges] + more,
        flops=4 * slots * owned * width, vmem=60 if fits else 16, scratch=scratch)
    arrived = lax.all_to_all(sums.reshape(ns, packed, 128), "store", split_axis=0, concat_axis=0,
                             tiled=True, axis_index_groups=[order]).reshape(ns * packed, 128)
    if not fits:
        own = self_rows.astype(BF16)
        recv = jnp.pad(recv_target[0, 0], ((0, 0), (0, SLOT_PAD - cap)), constant_values=targets).reshape(1, slots)
        mean = neighbor_mean(cap, unpack(arrived, order, cap, width // 128), recv, targets)
        preact = dot(own, w_self) + dot(mean, w_neigh)
        hidden, grad = forward(preact, cotangent)
        both = jnp.concatenate([own.T.reshape(ns, -1, targets), mean.T.reshape(ns, -1, targets)], axis=1)
        terms = dot(both.reshape(2 * width, targets), grad)
        part = lax.psum_scatter(terms, "store", scatter_dimension=0, tiled=True)
        total = lax.psum(part, "trainer")
        return hidden, total[:plan.shard], total[plan.shard:]

    def to_x(array):
        return plan.send(array, lambda z, x, y, c: (z, 1 - x, y, c))

    def to_y(array):
        return plan.send(array, lambda z, x, y, c: (z, x, 1 - y, c))

    def to_diagonal(array):
        return plan.send(array, lambda z, x, y, c: (z, 1 - x, 1 - y, c))

    def held(array, *until):
        return lax.optimization_barrier((array,) + until)[0]

    own, own_here, own_there = owns
    own_all = [own_here, to_y(own_here), to_x(own_there), to_diagonal(own_there)]
    self_term = dot(own, w_self)

    mean, mean_here, mean_there = call(
        functools.partial(mean_kernel, plan, cap, order),
        [shape((targets, width), BF16)] + [shape((rows, targets), BF16)] * 2, [arrived, recv_target[0, 0], self_term],
        scratch=[pltpu.VMEM((width, targets), BF16)], flops=2 * targets * width * slots)
    hidden, grad_here, grad_there = call(
        functools.partial(layer_kernel, plan),
        [shape((targets, out_width), F32)] + [shape((cols // 128 * targets, 128), BF16)] * 2,
        [mean, self_term, cotangent, w_neigh],
        scratch=[pltpu.VMEM((out_width // 128, targets, 128), BF16)],
        flops=2 * targets * width * out_width)
    mean_x, grad_y = to_x(mean_there), to_y(grad_there)
    grad_x = to_x(grad_here)
    mean_all = [mean_here, to_y(mean_here), mean_x, to_y(held(mean_x, *own_all[1:]))]
    grad_all = [grad_here, grad_y, grad_x, to_x(held(grad_y, mean_x, *own_all[1:]))]
    def to_core(array):
        return plan.send(array, lambda z, x, y, c: (z, x, y, 1 - c))

    def to_z(array, k):
        return plan.send(array, lambda z, x, y, c: (z ^ k, x, y, c))

    def terms(left, kind):
        first = call(functools.partial(first_terms_kernel, targets), [shape((left.shape[0], cols), F32)],
                     [left] + grad_all[:-1], flops=2 * left.shape[0] * cols * targets * (n - 1))
        return call(functools.partial(last_terms_kernel, targets), [shape((left.shape[0], cols), kind)],
                    [left] + list(first) + grad_all[-1:], flops=2 * left.shape[0] * cols * targets)[0]

    block = (plan.shard, cols)
    halves = [plan.far(), plan.near()]
    lefts = call(functools.partial(left_kernel, plan),
                 [shape((len(half) * plan.shard, n * targets), BF16) for half in halves * 2],
                 own_all[::-1] + mean_all)
    got, mine, earlier = [], None, None
    for half, give_left, keep_left in zip(halves, lefts[:2], lefts[2:]):
        came = to_core(terms(give_left, BF16))
        if earlier is not None:
            keep_left = held(keep_left, earlier)
        earlier = came
        sums = call(functools.partial(core_sum_kernel, plan),
                    [shape(block, BF16 if k else F32) for k in half], [terms(keep_left, F32), came])
        for k, part in zip(half, sums):
            if k:
                got.append(to_z(part, k))
            else:
                mine = part
    (quarter,) = call(store_sum_kernel, [shape(block, BF16)], [mine] + got)
    column = [quarter] + [plan.send(quarter, lambda z, x, y, c, i=i: (z, x, y ^ i, c))
                          for i in range(1, plan.gy)]
    quarters = [q for part in column
                for q in (part, plan.send(part, lambda z, x, y, c: (z, x, y, 1 - c)))]
    grads = call(functools.partial(assemble_kernel, plan),
                 [shape((plan.shard, out_width), F32)] * 2, quarters,
                 scratch=[pltpu.VMEM((2, plan.shard, out_width), F32)])
    return hidden.astype(BF16), grads[0], grads[1]


def solution(mesh):
    in_specs = (
        P("store", None),
        P(("store", "trainer"), None),
        P("trainer", "store", None, None, None),
        P("trainer", "store", None, None),
        P(("store", "trainer"), None),
        P(),
        P(),
    )
    out_specs = (P(("store", "trainer"), None), P("store", None), P("store", None))

    def run(features, self_rows, edge_row, recv_target, cotangent, w_self, w_neigh):
        plan = Plan(mesh, features.shape[1], w_self.shape[1])
        return jax.shard_map(
            functools.partial(per_device, plan), mesh=mesh, in_specs=in_specs,
            out_specs=out_specs, check_vma=False,
        )(features, self_rows, edge_row, recv_target, cotangent, w_self, w_neigh)

    return run
```
